32 devices in a mesh: space: 8 (over z, x), mem: 4 (over y, core).
Axes of the slice: x: 2, y: 2, z: 4, core: 2. Of those that a mesh axis runs over, the one named last changes fastest.
Arguments:
- ensemble_state: bfloat16 [256, 512, 256], P('mem', 'space'), may hold values from -6 to 6
- obs_ens: bfloat16 [256, 512, 128], P('mem', 'space'), may hold values from -6 to 6
- innovation: float32 [512, 128], P('space'), may hold values from -6 to 6
- obs_prec: float32 [512, 128], P('space'), may hold values from 0.25 to 2
- block_list: int32 [512, 8], P('space'), may hold values from 0 to 511, as said below
- block_count: int32 [512], P('space'), may hold values from 1 to 8
- loc_weight: float32 [512, 8], P('space'), may hold values from 0.1 to 1
- prior_weight: float32 [512, 256], P('space'), may hold values from 0.1 to 10, as said below
Outputs:
- analysis: bfloat16 [256, 512, 256], P('mem', 'space')
The draws below stay inside these ranges and needn't reach their ends.
Inputs may be any that keep to these rules, and one draw needn't show every extreme that they name: `block_list`: among the 128 entries of the regions r with the same r // 16, at most 24 name blocks b with the same b // 64, and exactly 24 do for one such value. `prior_weight`: Positive.
All inputs are finite; a program needn't handle non-finite values.
Results may differ from the reference program's by a relative error of at most 0.012.
Values may be sent and summed in bfloat16 or wider, within the bound.
No kernel may reach another device: no remote copies, remote signals or barrier semaphores. Data moves between devices by JAX's collectives and lax.ppermute only.
A program may use at most 128 MiB of HBM per device.

```python
import math
import jax
import jax.numpy as jnp
from jax import lax

K = 256
P_SIZE = 256
OB = 128
L = 8
REGIONS = 512
BLK_DEV = 64
NBLK = 512
GROUP_REG = 16
N_SPACE = 8


def draw_block_list(key, part):
    groups = REGIONS // GROUP_REG
    entries = GROUP_REG * L
    mean_load = entries // N_SPACE

    def one_group(group_key):
        sub_keys = jax.random.split(group_key, 3)
        hot_target = jax.random.randint(sub_keys[0], (), 0, N_SPACE)
        positions = jnp.arange(entries, dtype=jnp.int32)
        base_target = positions % N_SPACE
        cold_target = (hot_target + 1) % N_SPACE
        moved_entries = (base_target == cold_target) & (positions // N_SPACE < mean_load // 2)
        target = jnp.where(moved_entries, hot_target, base_target)
        target = jax.random.permutation(sub_keys[1], target)
        local_ids = jax.random.randint(sub_keys[2], (entries,), 0, BLK_DEV)
        return (target * BLK_DEV + local_ids).reshape(GROUP_REG, L)
    drawn = jax.vmap(one_group)(jax.random.split(key, groups))
    return drawn.reshape(REGIONS, L).astype(jnp.int32)


def draw_block_count(key, part):
    counts = jax.random.randint(key, (REGIONS,), 1, L + 1)
    return counts.at[0].set(L).at[1].set(1).astype(jnp.int32)


def draw_prior_weight(key, part):
    ramp = jnp.arange(K, dtype=jnp.float32) / (K - 1.0)
    rising = jnp.exp(jnp.log(3.0) * ramp)
    noise = jnp.exp(jax.random.uniform(key, (REGIONS, K), jnp.float32, -0.69, 0.69))
    return (rising[None, :] * noise).astype(jnp.float32)


def block_levels(rng, extent, pieces, low, high):
    loudness = 1.0
    for dim, parts in pieces:
        heights = jax.random.uniform(jax.random.fold_in(jax.random.fold_in(rng, 6), dim), (parts,), jnp.float32, low / len(pieces), high / len(pieces))
        loudness = loudness * jnp.repeat(jnp.exp(heights), extent[dim] // parts).reshape((-1,) + (1,) * (len(extent) - 1 - dim))
    return loudness


def bell_draw(own_key, dims, scale, reach, cuts=(), kind=jnp.bfloat16):
    level = block_levels(own_key, dims, cuts, -0.22, 0.18) if cuts else 1.0
    values = jax.random.normal(own_key, dims, jnp.float32) * scale * level
    return jnp.minimum(jnp.maximum(values, -reach), reach).astype(kind)


def setup_inputs(seed: int = 0) -> dict:
    streams_of = jax.random.split(jax.random.key(seed), 9)
    ensemble_state = bell_draw(streams_of[0], (K, REGIONS, P_SIZE), 1.0, 6.0, ((0, 4), (1, 8)))
    obs_ens = bell_draw(streams_of[1], (K, NBLK, OB), 1.0, 6.0, ((0, 4), (1, 8)))
    innovation = bell_draw(streams_of[2], (NBLK, OB), 1.0, 6.0, ((0, 8),), jnp.float32)
    obs_prec = jnp.clip(jnp.exp(math.log(2.0) - 2.0794415 * jax.random.uniform(streams_of[3], (NBLK, OB), jnp.float32) ** block_levels(streams_of[3], (NBLK, OB), ((0, 8),), -0.2, 0.2)), 0.25, 2.0)
    block_list = draw_block_list(jax.random.fold_in(streams_of[8], 71), 0)
    block_count = draw_block_count(jax.random.fold_in(streams_of[8], 71), 0)
    loc_weight = jnp.clip(jnp.exp(math.log(1.0) - 2.3025851 * jax.random.uniform(streams_of[6], (REGIONS, L), jnp.float32) ** block_levels(streams_of[6], (REGIONS, L), ((0, 8),), -0.2, 0.2)), 0.1, 1.0)
    prior_weight = draw_prior_weight(jax.random.fold_in(streams_of[8], 71), 0)
    return {"ensemble_state": ensemble_state, "obs_ens": obs_ens, "innovation": innovation, "obs_prec": obs_prec, "block_list": block_list, "block_count": block_count, "loc_weight": loc_weight, "prior_weight": prior_weight}


INFLATION = 1.1

def transform(gram_blocks, projection, prior_rows):
    highest = lax.Precision.HIGHEST
    members = gram_blocks.shape[-1]
    shares = prior_rows / lax.optimization_barrier(jnp.sum(prior_rows, axis=1, keepdims=True))
    root_q = jnp.sqrt(members * shares)
    left_term = jnp.einsum('rk,rkj->rj', shares, gram_blocks, precision=highest)
    centred = gram_blocks - left_term[:, None, :]
    right_term = jnp.einsum('rik,rk->ri', centred, shares, precision=highest)
    centred = centred - right_term[:, :, None]
    identity = jnp.eye(members, dtype=jnp.float32)
    system = root_q[:, :, None] * centred * root_q[:, None, :] + (members - 1) / INFLATION * identity
    vector = root_q * (projection - lax.optimization_barrier(jnp.sum(shares * projection, axis=1, keepdims=True)))
    factor = jnp.linalg.cholesky(system)
    inverse = jax.scipy.linalg.solve_triangular(factor, jnp.broadcast_to(identity, system.shape), lower=True)
    solved = jnp.einsum('rij,rj->ri', inverse, vector, precision=highest)
    weights = jnp.einsum('rji,rj->ri', inverse, solved, precision=highest)
    spread = jnp.sqrt(members - 1.0) * jnp.transpose(inverse, (0, 2, 1))
    mixing = root_q[:, :, None] * (weights[:, :, None] + spread)
    mixing = mixing - shares[:, :, None] * lax.optimization_barrier(jnp.sum(mixing, axis=1, keepdims=True)) + shares[:, :, None]
    return mixing

def reference(ensemble_state, obs_ens, innovation, obs_prec, block_list, block_count, loc_weight, prior_weight):
    highest = lax.Precision.HIGHEST
    batch_regions = 16

    def one_batch(first_row):
        block_ids = lax.dynamic_slice_in_dim(block_list, first_row, batch_regions, 0)
        counts = lax.dynamic_slice_in_dim(block_count, first_row, batch_regions, 0)
        loc_rows = lax.dynamic_slice_in_dim(loc_weight, first_row, batch_regions, 0)
        prior_rows = lax.dynamic_slice_in_dim(prior_weight, first_row, batch_regions, 0)
        active = (jnp.arange(L, dtype=jnp.int32)[None, :] < counts[:, None]).astype(jnp.float32)
        obs_weight = (active * loc_rows)[:, :, None] * obs_prec[block_ids]
        obs_scale = jnp.sqrt(obs_weight)
        picked = obs_ens[:, block_ids, :].astype(jnp.float32)
        scaled = (picked * obs_scale[None]).astype(jnp.bfloat16).astype(jnp.float32)
        gram_blocks = jnp.einsum('krlo,jrlo->rkj', scaled, scaled, precision=highest)
        projection = jnp.einsum('krlo,rlo->rk', scaled, obs_scale * innovation[block_ids], precision=highest)
        mixing = transform(gram_blocks, projection, prior_rows)
        states = lax.dynamic_slice_in_dim(ensemble_state, first_row, batch_regions, 1).astype(jnp.float32)
        return jnp.einsum('krp,rkj->jrp', states, mixing, precision=highest).astype(jnp.bfloat16)
    batch_starts = jnp.arange(REGIONS // batch_regions, dtype=jnp.int32) * batch_regions
    results = lax.map(one_batch, batch_starts)
    return jnp.transpose(results, (1, 0, 2, 3)).reshape(K, REGIONS, P_SIZE)
```

```python
import functools

import jax
import jax.numpy as jnp
from jax import lax
from jax.experimental import pallas as pl
from jax.experimental.pallas import tpu as pltpu
from jax.sharding import PartitionSpec as P

INFLATION = 1.1
PANEL = 32
LANES = 128
CHUNKS = 2
F32 = jnp.float32
BF16 = jnp.bfloat16


def split3(value):
    high = value.astype(BF16)
    rest = value - high.astype(F32)
    mid = rest.astype(BF16)
    low = (rest - mid.astype(F32)).astype(BF16)
    return high, mid, low


def pick_kernel(ids_ref, table_ref, out_ref):
    @pl.loop(0, out_ref.shape[0], unroll=8)
    def _(entry):
        out_ref[entry] = table_ref[ids_ref[entry]]


def pick(ids, table):
    return pl.pallas_call(
        pick_kernel,
        out_shape=jax.ShapeDtypeStruct((ids.shape[0],) + table.shape[1:], table.dtype),
        in_specs=[
            pl.BlockSpec(memory_space=pltpu.SMEM),
            pl.BlockSpec(memory_space=pltpu.VMEM),
        ],
        out_specs=pl.BlockSpec(memory_space=pltpu.VMEM),
        compiler_params=pltpu.CompilerParams(vmem_limit_bytes=40 << 20),
    )(ids, table)


def region_setup(
    region, ids_ref, count_ref, loc_ref, prior_ref, rows_ref, states_ref, obs_refs,
    scaled_ref, work_ref, mean_ref,
):
    members = prior_ref.shape[1]
    slots = ids_ref.shape[0] // count_ref.shape[0]
    sources = states_ref.shape[0]
    members_dev = states_ref.shape[2]
    width = obs_refs[0].shape[3]
    piece = obs_refs[0].shape[2]
    innov_parts = []
    for slot in range(slots):
        entry = region * slots + slot
        row = rows_ref[pl.ds(ids_ref[entry], 1), :]
        weight = jnp.where(slot < count_ref[region], loc_ref[entry], 0.0)
        scale = jnp.sqrt(weight * row[:, :width])
        innov_parts.append(scale * row[:, width:])
        for source in range(sources):
            for index, obs_ref in enumerate(obs_refs):
                first = source * members_dev + index * piece
                values = obs_ref[source, entry].astype(F32) * scale
                scaled_ref[first : first + piece, slot * width : (slot + 1) * width] = (
                    values.astype(BF16)
                )
    scaled = scaled_ref[...]
    contract = (((1,), (1,)), ((), ()))
    gram = lax.dot_general(scaled, scaled, contract, preferred_element_type=F32)
    innov = jnp.concatenate(innov_parts, axis=1)
    high, mid, low = (part.astype(F32) for part in split3(innov))
    which = lax.broadcasted_iota(jnp.int32, (16, slots * width), 0)
    innov_rows = jnp.where(
        which == 0, high, jnp.where(which == 1, mid, jnp.where(which == 2, low, 0.0))
    ).astype(BF16)
    projection = jnp.sum(
        lax.dot_general(scaled, innov_rows, contract, preferred_element_type=F32),
        axis=1, keepdims=True,
    )
    on_diag = lax.broadcasted_iota(jnp.int32, (members, members), 0) == (
        lax.broadcasted_iota(jnp.int32, (members, members), 1)
    )
    prior_row = prior_ref[pl.ds(region, 1), :]
    share_row = prior_row / jnp.sum(prior_row, axis=1, keepdims=True)
    share_col = jnp.sum(jnp.where(on_diag, share_row, 0.0), axis=1, keepdims=True)
    root_row = jnp.sqrt(members * share_row)
    root_col = jnp.sqrt(members * share_col)
    left_row = jnp.sum(share_col * gram, axis=0, keepdims=True)
    left_col = jnp.sum(share_row * gram, axis=1, keepdims=True)
    total = jnp.sum(left_row * share_row, axis=1, keepdims=True)
    centred = (gram - left_row) - (left_col - total)
    system = root_col * centred * root_row
    work_ref[region, :, :members] = system + jnp.where(
        on_diag, (members - 1) / INFLATION, 0.0
    )
    vector = root_col * (
        projection - jnp.sum(share_col * projection, axis=0, keepdims=True)
    )
    states = jnp.concatenate(
        [states_ref[source, region].astype(F32) for source in range(sources)], axis=0
    )
    mean = jnp.sum(share_col * states, axis=0, keepdims=True)
    mean_ref[region] = jnp.broadcast_to(mean, mean_ref.shape[1:])
    points = states.shape[1]
    work_ref[region, :, members : members + points] = root_col * (states - mean)
    work_ref[region, :, members + points :] = jnp.broadcast_to(vector, (members, LANES))


def factor_diagonals(panel, packs, work_ref):
    per_pack = LANES // PANEL
    start = panel * PANEL
    base, offset = start // LANES * LANES, start % LANES
    lane = lax.broadcasted_iota(jnp.int32, (8, LANES), 1)
    sub = lax.broadcasted_iota(jnp.int32, (8, LANES), 0)
    owner, column = lane // PANEL, lane % PANEL
    tiles = PANEL // 8
    blocks = []
    for pack in range(packs):
        pieces = []
        for tile in range(tiles):
            merged = None
            for place in range(per_pack):
                region = pack * per_pack + place
                raw = work_ref[
                    region, start + 8 * tile : start + 8 * tile + 8, base : base + LANES
                ]
                shift = (place * PANEL - offset) % LANES
                if shift:
                    raw = pltpu.roll(raw, shift, axis=1)
                merged = raw if merged is None else jnp.where(owner == place, raw, merged)
            pieces.append(merged)
        blocks.append(pieces)
    pivots = [[jnp.ones((8, LANES), F32) for _ in range(tiles)] for _ in range(packs)]
    for step in range(PANEL):
        home, inside = step // 8, step % 8
        picks = owner * PANEL + step
        at_step = column == step
        below = sub > inside
        for pack in range(packs):
            pieces = blocks[pack]
            columns = {
                tile: jnp.take_along_axis(
                    pieces[tile], picks, axis=1, mode="promise_in_bounds"
                )
                for tile in range(home, tiles)
            }
            pivot = columns[home][inside : inside + 1, :]
            inverse = 1.0 / pivot
            row = jnp.where(at_step[:1], 1.0, pieces[home][inside : inside + 1, :])
            pivots[pack][home] = jnp.where(sub == inside, pivot, pivots[pack][home])
            for tile in range(home, tiles):
                ratio = columns[tile] * inverse
                cleared = at_step
                if tile == home:
                    ratio = jnp.where(below, ratio, 0.0)
                    cleared = at_step & below
                pieces[tile] = jnp.where(cleared, 0.0, pieces[tile]) - ratio * row
    results = []
    for pack in range(packs):
        rows = []
        for tile in range(tiles):
            index = sub + 8 * tile
            lower = jnp.where(
                column < index, blocks[pack][tile], jnp.where(column == index, 1.0, 0.0)
            )
            rows.append(lower * lax.rsqrt(pivots[pack][tile]))
        results.append(jnp.concatenate(rows, axis=0))
    return results


def eliminate(panel, pack, lower_ref, work_ref, members):
    per_pack = LANES // PANEL
    start = panel * PANEL
    after = start + PANEL
    first = after // LANES * LANES
    total = work_ref.shape[2]
    lower = lower_ref[pack]
    owner = lax.broadcasted_iota(jnp.int32, (PANEL, LANES), 1) // PANEL
    spread = jnp.concatenate(
        [jnp.where(owner == place, lower, 0.0) for place in range(per_pack)], axis=0
    )
    stacked = jnp.concatenate(
        [
            work_ref[pack * per_pack + place, start:after, first:]
            for place in range(per_pack)
        ],
        axis=0,
    )
    solved = jnp.dot(
        spread, stacked, precision=lax.Precision.HIGHEST, preferred_element_type=F32
    )
    for place in range(per_pack):
        region = pack * per_pack + place
        rows = solved[place * PANEL : (place + 1) * PANEL]
        work_ref[region, start:after, members:] = rows[:, members - first :]
        if after < members:
            high, mid, low = split3(rows)
            left = jnp.concatenate([high, high, mid, mid, high, low], axis=0)
            right = jnp.concatenate([high, mid, high, mid, low, high], axis=0)
            change = lax.dot_general(
                left[:, : members - first], right, (((0,), (0,)), ((), ())),
                preferred_element_type=F32,
            )
            work_ref[region, after:members, first:total] = (
                work_ref[region, after:members, first:total] - change[after - first :]
            )


def analysis_kernel(
    ids_ref, count_ref, loc_ref, prior_ref, rows_ref, states_ref, *rest
):
    obs_refs, (out_ref, scaled_ref, work_ref, mean_ref, lower_ref) = rest[:-5], rest[-5:]
    regions, members = prior_ref.shape
    sources, members_dev = states_ref.shape[0], states_ref.shape[2]
    points = states_ref.shape[3]
    packs = regions * PANEL // LANES

    @pl.loop(0, regions)
    def _(region):
        region_setup(
            region, ids_ref, count_ref, loc_ref, prior_ref, rows_ref, states_ref,
            obs_refs, scaled_ref, work_ref, mean_ref,
        )

    for panel in range(members // PANEL):
        lowers = factor_diagonals(panel, packs, work_ref)
        for pack in range(packs):
            lower_ref[pack] = lowers[pack]

        @pl.loop(0, packs)
        def _(pack):
            eliminate(panel, pack, lower_ref, work_ref, members)

    @pl.loop(0, regions)
    def _(region):
        moved = work_ref[region, :, members : members + points]
        solved = work_ref[region, :, members + points :]
        solved = jnp.concatenate([solved] * (points // LANES), axis=1)
        shift = mean_ref[region, :1] + jnp.sum(solved * moved, axis=0, keepdims=True)
        result = (shift + jnp.sqrt(members - 1.0) * moved).astype(BF16)
        for source in range(sources):
            out_ref[source, region] = result[
                source * members_dev : (source + 1) * members_dev
            ]


def analyse(ids, counts, loc, prior_rows, rows, states, obs_parts):
    regions, members = prior_rows.shape
    points = states.shape[3]
    slots = ids.shape[0] // regions
    width = obs_parts[0].shape[3]
    smem = pl.BlockSpec(memory_space=pltpu.SMEM)
    vmem = pl.BlockSpec(memory_space=pltpu.VMEM)
    return pl.pallas_call(
        analysis_kernel,
        out_shape=jax.ShapeDtypeStruct(states.shape, states.dtype),
        in_specs=[smem] * 3 + [vmem] * (3 + len(obs_parts)),
        out_specs=vmem,
        scratch_shapes=[
            pltpu.VMEM((members, slots * width), BF16),
            pltpu.VMEM((regions, members, members + points + LANES), F32),
            pltpu.VMEM((regions, 8, points), F32),
            pltpu.VMEM((regions * PANEL // LANES, PANEL, LANES), F32),
        ],
        compiler_params=pltpu.CompilerParams(vmem_limit_bytes=56 << 20),
    )(ids, counts, loc, prior_rows, rows, states, *obs_parts)


def body(
    ensemble_state, obs_ens, innovation, obs_prec, block_list, block_count, loc_weight, prior_weight
):
    mem_count = lax.axis_size("mem")
    members_dev, regions_dev, points = ensemble_state.shape
    blocks_dev, width = obs_ens.shape[1:]
    group_size = regions_dev // mem_count
    slots = block_list.shape[1]
    piece = members_dev // CHUNKS
    first_row = lax.axis_index("mem") * group_size

    def own(array):
        return lax.dynamic_slice_in_dim(array, first_row, group_size, 0)

    by_block = jnp.transpose(
        obs_ens.reshape(CHUNKS, piece, blocks_dev, width), (0, 2, 1, 3)
    )
    all_ids = block_list.reshape(regions_dev * slots)
    obs_parts = []
    for chunk in range(CHUNKS):
        table = lax.all_gather(by_block[chunk], "space", axis=0, tiled=True)
        picked = pick(all_ids, table).reshape(mem_count, group_size * slots, piece, width)
        obs_parts.append(
            lax.all_to_all(picked, "mem", split_axis=0, concat_axis=0, tiled=True)
        )
    rows = lax.all_gather(
        jnp.concatenate([obs_prec, innovation], axis=1), "space", axis=0, tiled=True
    )
    by_region = jnp.transpose(ensemble_state, (1, 0, 2)).reshape(
        mem_count, group_size, members_dev, points
    )
    states = lax.all_to_all(by_region, "mem", split_axis=0, concat_axis=0, tiled=True)
    result = analyse(
        own(block_list).reshape(group_size * slots),
        own(block_count),
        own(loc_weight).reshape(group_size * slots),
        own(prior_weight),
        rows,
        states,
        obs_parts,
    )
    back = lax.all_to_all(result, "mem", split_axis=0, concat_axis=0, tiled=True)
    return jnp.transpose(back.reshape(regions_dev, members_dev, points), (1, 0, 2))


def solution(mesh):
    return jax.shard_map(
        body,
        mesh=mesh,
        in_specs=(
            P("mem", "space", None),
            P("mem", "space", None),
            P("space", None),
            P("space", None),
            P("space", None),
            P("space"),
            P("space", None),
            P("space", None),
        ),
        out_specs=P("mem", "space", None),
        check_vma=False,
    )
```

```python
import functools

import jax
import jax.numpy as jnp
from jax import lax
from jax.experimental import pallas as pl
from jax.experimental.pallas import tpu as pltpu
from jax.sharding import PartitionSpec as P

INFLATION = 1.1
PANEL = 32
LANES = 128
CHUNKS = 4
F32 = jnp.float32
BF16 = jnp.bfloat16


def split3(value):
    high = value.astype(BF16)
    rest = value - high.astype(F32)
    mid = rest.astype(BF16)
    low = (rest - mid.astype(F32)).astype(BF16)
    return high, mid, low


def pick_kernel(ids_ref, *rest):
    shard_refs, (out_ref, table_ref, sems) = rest[:-3], rest[-3:]
    rows = shard_refs[0].shape[0]
    copies = [
        pltpu.make_async_copy(
            shard_ref, table_ref.at[index * rows : (index + 1) * rows], sems.at[index]
        )
        for index, shard_ref in enumerate(shard_refs)
    ]
    for copy in copies:
        copy.start()
    for copy in copies:
        copy.wait()

    @pl.loop(0, out_ref.shape[0], unroll=8)
    def _(entry):
        out_ref[entry] = table_ref[ids_ref[entry]]


def pick(ids, shards):
    rows, dtype = shards[0].shape, shards[0].dtype
    table = (len(shards) * rows[0],) + rows[1:]
    return pl.pallas_call(
        pick_kernel,
        out_shape=jax.ShapeDtypeStruct((ids.shape[0],) + rows[1:], dtype),
        in_specs=[pl.BlockSpec(memory_space=pltpu.SMEM)]
        + [pl.BlockSpec(memory_space=pl.ANY)] * len(shards),
        out_specs=pl.BlockSpec(memory_space=pltpu.VMEM),
        scratch_shapes=[
            pltpu.VMEM(table, dtype),
            pltpu.SemaphoreType.DMA((len(shards),)),
        ],
        compiler_params=pltpu.CompilerParams(vmem_limit_bytes=16 << 20),
    )(ids, *shards)


def swap(value, spaces, offset):
    return lax.ppermute(value, "space", [(s, s ^ offset) for s in range(spaces)])


def share_over_space(own, spaces, inner):
    shards = [own] + [None] * (spaces - 1)
    for offset in range(inner, spaces, inner):
        shards[offset] = swap(own, spaces, offset)
    for first in range(0, spaces, inner):
        for offset in range(1, inner):
            shards[first + offset] = swap(shards[first], spaces, offset)
    return shards


def region_setup(
    region, ids_ref, count_ref, loc_ref, prior_ref, rows_ref, states_ref, obs_refs,
    scaled_ref, work_ref, mean_ref,
):
    members = prior_ref.shape[1]
    slots = ids_ref.shape[0] // count_ref.shape[0]
    sources = states_ref.shape[0]
    members_dev = states_ref.shape[2]
    width = obs_refs[0].shape[3]
    piece = obs_refs[0].shape[2]
    innov_parts = []
    for slot in range(slots):
        entry = region * slots + slot
        row = rows_ref[pl.ds(ids_ref[entry], 1), :]
        weight = jnp.where(slot < count_ref[region], loc_ref[entry], 0.0)
        scale = jnp.sqrt(weight * row[:, :width])
        innov_parts.append(scale * row[:, width:])
        for source in range(sources):
            for index, obs_ref in enumerate(obs_refs):
                first = source * members_dev + index * piece
                values = obs_ref[source, entry].astype(F32) * scale
                scaled_ref[first : first + piece, slot * width : (slot + 1) * width] = (
                    values.astype(BF16)
                )
    scaled = scaled_ref[...]
    contract = (((1,), (1,)), ((), ()))
    gram = lax.dot_general(scaled, scaled, contract, preferred_element_type=F32)
    innov = jnp.concatenate(innov_parts, axis=1)
    high, mid, low = (part.astype(F32) for part in split3(innov))
    which = lax.broadcasted_iota(jnp.int32, (16, slots * width), 0)
    innov_rows = jnp.where(
        which == 0, high, jnp.where(which == 1, mid, jnp.where(which == 2, low, 0.0))
    ).astype(BF16)
    projection = jnp.sum(
        lax.dot_general(scaled, innov_rows, contract, preferred_element_type=F32),
        axis=1, keepdims=True,
    )
    on_diag = lax.broadcasted_iota(jnp.int32, (members, members), 0) == (
        lax.broadcasted_iota(jnp.int32, (members, members), 1)
    )
    prior_row = prior_ref[pl.ds(region, 1), :]
    share_row = prior_row / jnp.sum(prior_row, axis=1, keepdims=True)
    share_col = jnp.sum(jnp.where(on_diag, share_row, 0.0), axis=1, keepdims=True)
    root_row = jnp.sqrt(members * share_row)
    root_col = jnp.sqrt(members * share_col)
    left_row = jnp.sum(share_col * gram, axis=0, keepdims=True)
    left_col = jnp.sum(share_row * gram, axis=1, keepdims=True)
    total = jnp.sum(left_row * share_row, axis=1, keepdims=True)
    centred = (gram - left_row) - (left_col - total)
    system = root_col * centred * root_row
    work_ref[region, :, :members] = system + jnp.where(
        on_diag, (members - 1) / INFLATION, 0.0
    )
    vector = root_col * (
        projection - jnp.sum(share_col * projection, axis=0, keepdims=True)
    )
    states = jnp.concatenate(
        [states_ref[source, region].astype(F32) for source in range(sources)], axis=0
    )
    mean = jnp.sum(share_col * states, axis=0, keepdims=True)
    mean_ref[region] = jnp.broadcast_to(mean, mean_ref.shape[1:])
    points = states.shape[1]
    work_ref[region, :, members : members + points] = root_col * (states - mean)
    work_ref[region, :, members + points :] = jnp.broadcast_to(vector, (members, LANES))


def factor_diagonals(panel, packs, work_ref):
    per_pack = LANES // PANEL
    start = panel * PANEL
    base, offset = start // LANES * LANES, start % LANES
    lane = lax.broadcasted_iota(jnp.int32, (8, LANES), 1)
    sub = lax.broadcasted_iota(jnp.int32, (8, LANES), 0)
    owner, column = lane // PANEL, lane % PANEL
    tiles = PANEL // 8
    blocks = []
    for pack in range(packs):
        pieces = []
        for tile in range(tiles):
            merged = None
            for place in range(per_pack):
                region = pack * per_pack + place
                raw = work_ref[
                    region, start + 8 * tile : start + 8 * tile + 8, base : base + LANES
                ]
                shift = (place * PANEL - offset) % LANES
                if shift:
                    raw = pltpu.roll(raw, shift, axis=1)
                merged = raw if merged is None else jnp.where(owner == place, raw, merged)
            pieces.append(merged)
        blocks.append(pieces)
    pivots = [[jnp.ones((8, LANES), F32) for _ in range(tiles)] for _ in range(packs)]
    for step in range(PANEL):
        home, inside = step // 8, step % 8
        picks = owner * PANEL + step
        at_step = column == step
        below = sub > inside
        for pack in range(packs):
            pieces = blocks[pack]
            columns = {
                tile: jnp.take_along_axis(
                    pieces[tile], picks, axis=1, mode="promise_in_bounds"
                )
                for tile in range(home, tiles)
            }
            pivot = columns[home][inside : inside + 1, :]
            inverse = 1.0 / pivot
            row = jnp.where(at_step[:1], 1.0, pieces[home][inside : inside + 1, :])
            pivots[pack][home] = jnp.where(sub == inside, pivot, pivots[pack][home])
            for tile in range(home, tiles):
                ratio = columns[tile] * inverse
                cleared = at_step
                if tile == home:
                    ratio = jnp.where(below, ratio, 0.0)
                    cleared = at_step & below
                pieces[tile] = jnp.where(cleared, 0.0, pieces[tile]) - ratio * row
    results = []
    for pack in range(packs):
        rows = []
        for tile in range(tiles):
            index = sub + 8 * tile
            lower = jnp.where(
                column < index, blocks[pack][tile], jnp.where(column == index, 1.0, 0.0)
            )
            rows.append(lower * lax.rsqrt(pivots[pack][tile]))
        results.append(jnp.concatenate(rows, axis=0))
    return results


def eliminate(panel, pack, lower_ref, work_ref, members):
    per_pack = LANES // PANEL
    start = panel * PANEL
    after = start + PANEL
    first = after // LANES * LANES
    total = work_ref.shape[2]
    lower = lower_ref[pack]
    owner = lax.broadcasted_iota(jnp.int32, (PANEL, LANES), 1) // PANEL
    spread = jnp.concatenate(
        [jnp.where(owner == place, lower, 0.0) for place in range(per_pack)], axis=0
    )
    stacked = jnp.concatenate(
        [
            work_ref[pack * per_pack + place, start:after, first:]
            for place in range(per_pack)
        ],
        axis=0,
    )
    solved = jnp.dot(
        spread, stacked, precision=lax.Precision.HIGHEST, preferred_element_type=F32
    )
    for place in range(per_pack):
        region = pack * per_pack + place
        rows = solved[place * PANEL : (place + 1) * PANEL]
        work_ref[region, start:after, members:] = rows[:, members - first :]
        if after < members:
            high, mid, low = split3(rows)
            left = jnp.concatenate([high, high, mid, mid, high, low], axis=0)
            right = jnp.concatenate([high, mid, high, mid, low, high], axis=0)
            change = lax.dot_general(
                left[:, : members - first], right, (((0,), (0,)), ((), ())),
                preferred_element_type=F32,
            )
            work_ref[region, after:members, first:total] = (
                work_ref[region, after:members, first:total] - change[after - first :]
            )


def analysis_kernel(
    ids_ref, count_ref, loc_ref, prior_ref, rows_ref, states_ref, *rest
):
    obs_refs, (out_ref, scaled_ref, work_ref, mean_ref, lower_ref) = rest[:-5], rest[-5:]
    regions, members = prior_ref.shape
    sources, members_dev = states_ref.shape[0], states_ref.shape[2]
    points = states_ref.shape[3]
    packs = regions * PANEL // LANES

    @pl.loop(0, regions)
    def _(region):
        region_setup(
            region, ids_ref, count_ref, loc_ref, prior_ref, rows_ref, states_ref,
            obs_refs, scaled_ref, work_ref, mean_ref,
        )

    for panel in range(members // PANEL):
        lowers = factor_diagonals(panel, packs, work_ref)
        for pack in range(packs):
            lower_ref[pack] = lowers[pack]

        @pl.loop(0, packs)
        def _(pack):
            eliminate(panel, pack, lower_ref, work_ref, members)

    @pl.loop(0, regions)
    def _(region):
        moved = work_ref[region, :, members : members + points]
        solved = work_ref[region, :, members + points :]
        solved = jnp.concatenate([solved] * (points // LANES), axis=1)
        shift = mean_ref[region, :1] + jnp.sum(solved * moved, axis=0, keepdims=True)
        result = (shift + jnp.sqrt(members - 1.0) * moved).astype(BF16)
        for source in range(sources):
            out_ref[source, region] = result[
                source * members_dev : (source + 1) * members_dev
            ]


def analyse(ids, counts, loc, prior_rows, rows, states, obs_parts):
    regions, members = prior_rows.shape
    points = states.shape[3]
    slots = ids.shape[0] // regions
    width = obs_parts[0].shape[3]
    smem = pl.BlockSpec(memory_space=pltpu.SMEM)
    vmem = pl.BlockSpec(memory_space=pltpu.VMEM)
    return pl.pallas_call(
        analysis_kernel,
        out_shape=jax.ShapeDtypeStruct(states.shape, states.dtype),
        in_specs=[smem] * 3 + [vmem] * (3 + len(obs_parts)),
        out_specs=vmem,
        scratch_shapes=[
            pltpu.VMEM((members, slots * width), BF16),
            pltpu.VMEM((regions, members, members + points + LANES), F32),
            pltpu.VMEM((regions, 8, points), F32),
            pltpu.VMEM((regions * PANEL // LANES, PANEL, LANES), F32),
        ],
        compiler_params=pltpu.CompilerParams(vmem_limit_bytes=56 << 20),
    )(ids, counts, loc, prior_rows, rows, states, *obs_parts)


def body(
    ensemble_state, obs_ens, innovation, obs_prec, block_list, block_count, loc_weight, prior_weight
):
    spaces = lax.axis_size("space")
    mem_count = lax.axis_size("mem")
    members_dev, regions_dev, points = ensemble_state.shape
    blocks_dev, width = obs_ens.shape[1:]
    group_size = regions_dev // mem_count
    slots = block_list.shape[1]
    piece = members_dev // CHUNKS
    first_row = lax.axis_index("mem") * group_size

    def own(array):
        return lax.dynamic_slice_in_dim(array, first_row, group_size, 0)

    by_block = jnp.transpose(
        obs_ens.reshape(CHUNKS, piece, blocks_dev, width), (0, 2, 1, 3)
    )
    inner = 2 ** ((spaces.bit_length() - 1) // 2)
    all_ids = block_list.reshape(regions_dev * slots)
    source = (all_ids // blocks_dev) ^ lax.axis_index("space")
    places = source * blocks_dev + all_ids % blocks_dev
    obs_parts = []
    gate = None
    for chunk in range(CHUNKS):
        own_chunk = by_block[chunk]
        if gate is not None:
            own_chunk, _ = lax.optimization_barrier((own_chunk, gate))
        shards = share_over_space(own_chunk, spaces, inner)
        gate = shards[2 * inner]
        picked = pick(places, shards).reshape(mem_count, group_size * slots, piece, width)
        obs_parts.append(
            lax.all_to_all(picked, "mem", split_axis=0, concat_axis=0, tiled=True)
        )
    rows = jnp.concatenate([obs_prec, innovation], axis=1)
    rows = lax.all_to_all(
        jnp.broadcast_to(rows, (spaces,) + rows.shape), "space",
        split_axis=0, concat_axis=0, tiled=True,
    ).reshape(spaces * blocks_dev, 2 * width)
    by_region = jnp.transpose(ensemble_state, (1, 0, 2)).reshape(
        mem_count, group_size, members_dev, points
    )
    states = lax.all_to_all(by_region, "mem", split_axis=0, concat_axis=0, tiled=True)
    result = analyse(
        own(block_list).reshape(group_size * slots),
        own(block_count),
        own(loc_weight).reshape(group_size * slots),
        own(prior_weight),
        rows,
        states,
        obs_parts,
    )
    back = lax.all_to_all(result, "mem", split_axis=0, concat_axis=0, tiled=True)
    return jnp.transpose(back.reshape(regions_dev, members_dev, points), (1, 0, 2))


def solution(mesh):
    return jax.shard_map(
        body,
        mesh=mesh,
        in_specs=(
            P("mem", "space", None),
            P("mem", "space", None),
            P("space", None),
            P("space", None),
            P("space", None),
            P("space"),
            P("space", None),
            P("space", None),
        ),
        out_specs=P("mem", "space", None),
        check_vma=False,
    )
```

```python
import functools

import jax
import jax.numpy as jnp
from jax import lax
from jax.experimental import pallas as pl
from jax.experimental.pallas import tpu as pltpu
from jax.sharding import PartitionSpec as P

INFLATION = 1.1
PANEL = 32
LANES = 128
CHUNKS = 4
F32 = jnp.float32
BF16 = jnp.bfloat16


def split3(value):
    high = value.astype(BF16)
    rest = value - high.astype(F32)
    mid = rest.astype(BF16)
    low = (rest - mid.astype(F32)).astype(BF16)
    return high, mid, low


def pick_kernel(layout, ids_ref, *rest):
    shard_refs, (out_ref, table_ref, sems) = rest[:-3], rest[-3:]
    rows = table_ref.shape[0] // len(layout)
    copies = [
        pltpu.make_async_copy(
            shard_refs[operand].at[start : start + rows],
            table_ref.at[index * rows : (index + 1) * rows],
            sems.at[index],
        )
        for index, (operand, start) in enumerate(layout)
    ]
    for copy in copies:
        copy.start()
    for copy in copies:
        copy.wait()

    @pl.loop(0, out_ref.shape[0], unroll=8)
    def _(entry):
        out_ref[entry] = table_ref[ids_ref[entry]]


def pick(ids, table_rows, sources):
    operands = []
    layout = []
    for array, start in sources:
        known = [index for index, other in enumerate(operands) if other is array]
        if not known:
            operands.append(array)
        layout.append((known[0] if known else len(operands) - 1, start))
    row, dtype = operands[0].shape[1:], operands[0].dtype
    return pl.pallas_call(
        functools.partial(pick_kernel, layout),
        out_shape=jax.ShapeDtypeStruct((ids.shape[0],) + row, dtype),
        in_specs=[pl.BlockSpec(memory_space=pltpu.SMEM)]
        + [pl.BlockSpec(memory_space=pl.ANY)] * len(operands),
        out_specs=pl.BlockSpec(memory_space=pltpu.VMEM),
        scratch_shapes=[
            pltpu.VMEM((table_rows,) + row, dtype),
            pltpu.SemaphoreType.DMA((len(layout),)),
        ],
        compiler_params=pltpu.CompilerParams(vmem_limit_bytes=16 << 20),
    )(ids, *operands)


def swap(value, spaces, offset):
    return lax.ppermute(value, "space", [(s, s ^ offset) for s in range(spaces)])


def region_setup(
    region, ids_ref, count_ref, loc_ref, prior_ref, rows_ref, states_ref, obs_refs,
    scaled_ref, work_ref, mean_ref,
):
    members = prior_ref.shape[1]
    slots = ids_ref.shape[0] // count_ref.shape[0]
    sources = states_ref.shape[0]
    members_dev = states_ref.shape[2]
    width = obs_refs[0].shape[3]
    piece = obs_refs[0].shape[2]
    innov_parts = []
    for slot in range(slots):
        entry = region * slots + slot
        row = rows_ref[pl.ds(ids_ref[entry], 1), :]
        weight = jnp.where(slot < count_ref[region], loc_ref[entry], 0.0)
        scale = jnp.sqrt(weight * row[:, :width])
        innov_parts.append(scale * row[:, width:])
        for source in range(sources):
            for index, obs_ref in enumerate(obs_refs):
                first = source * members_dev + index * piece
                values = obs_ref[source, entry].astype(F32) * scale
                scaled_ref[first : first + piece, slot * width : (slot + 1) * width] = (
                    values.astype(BF16)
                )
    scaled = scaled_ref[...]
    contract = (((1,), (1,)), ((), ()))
    gram = lax.dot_general(scaled, scaled, contract, preferred_element_type=F32)
    innov = jnp.concatenate(innov_parts, axis=1)
    high, mid, low = (part.astype(F32) for part in split3(innov))
    which = lax.broadcasted_iota(jnp.int32, (16, slots * width), 0)
    innov_rows = jnp.where(
        which == 0, high, jnp.where(which == 1, mid, jnp.where(which == 2, low, 0.0))
    ).astype(BF16)
    projection = jnp.sum(
        lax.dot_general(scaled, innov_rows, contract, preferred_element_type=F32),
        axis=1, keepdims=True,
    )
    on_diag = lax.broadcasted_iota(jnp.int32, (members, members), 0) == (
        lax.broadcasted_iota(jnp.int32, (members, members), 1)
    )
    prior_row = prior_ref[pl.ds(region, 1), :]
    share_row = prior_row / jnp.sum(prior_row, axis=1, keepdims=True)
    share_col = jnp.sum(jnp.where(on_diag, share_row, 0.0), axis=1, keepdims=True)
    root_row = jnp.sqrt(members * share_row)
    root_col = jnp.sqrt(members * share_col)
    left_row = jnp.sum(share_col * gram, axis=0, keepdims=True)
    left_col = jnp.sum(share_row * gram, axis=1, keepdims=True)
    total = jnp.sum(left_row * share_row, axis=1, keepdims=True)
    centred = (gram - left_row) - (left_col - total)
    system = root_col * centred * root_row
    work_ref[region, :, :members] = system + jnp.where(
        on_diag, (members - 1) / INFLATION, 0.0
    )
    vector = root_col * (
        projection - jnp.sum(share_col * projection, axis=0, keepdims=True)
    )
    states = jnp.concatenate(
        [states_ref[source, region].astype(F32) for source in range(sources)], axis=0
    )
    mean = jnp.sum(share_col * states, axis=0, keepdims=True)
    mean_ref[region] = jnp.broadcast_to(mean, mean_ref.shape[1:])
    points = states.shape[1]
    work_ref[region, :, members : members + points] = root_col * (states - mean)
    work_ref[region, :, members + points :] = jnp.broadcast_to(vector, (members, LANES))


def factor_diagonals(panel, packs, work_ref):
    per_pack = LANES // PANEL
    start = panel * PANEL
    base, offset = start // LANES * LANES, start % LANES
    lane = lax.broadcasted_iota(jnp.int32, (8, LANES), 1)
    sub = lax.broadcasted_iota(jnp.int32, (8, LANES), 0)
    owner, column = lane // PANEL, lane % PANEL
    tiles = PANEL // 8
    blocks = []
    for pack in range(packs):
        pieces = []
        for tile in range(tiles):
            merged = None
            for place in range(per_pack):
                region = pack * per_pack + place
                raw = work_ref[
                    region, start + 8 * tile : start + 8 * tile + 8, base : base + LANES
                ]
                shift = (place * PANEL - offset) % LANES
                if shift:
                    raw = pltpu.roll(raw, shift, axis=1)
                merged = raw if merged is None else jnp.where(owner == place, raw, merged)
            pieces.append(merged)
        blocks.append(pieces)
    pivots = [[jnp.ones((8, LANES), F32) for _ in range(tiles)] for _ in range(packs)]
    for step in range(PANEL):
        home, inside = step // 8, step % 8
        picks = owner * PANEL + step
        at_step = column == step
        below = sub > inside
        for pack in range(packs):
            pieces = blocks[pack]
            columns = {
                tile: jnp.take_along_axis(
                    pieces[tile], picks, axis=1, mode="promise_in_bounds"
                )
                for tile in range(home, tiles)
            }
            pivot = columns[home][inside : inside + 1, :]
            inverse = 1.0 / pivot
            row = jnp.where(at_step[:1], 1.0, pieces[home][inside : inside + 1, :])
            pivots[pack][home] = jnp.where(sub == inside, pivot, pivots[pack][home])
            for tile in range(home, tiles):
                ratio = columns[tile] * inverse
                cleared = at_step
                if tile == home:
                    ratio = jnp.where(below, ratio, 0.0)
                    cleared = at_step & below
                pieces[tile] = jnp.where(cleared, 0.0, pieces[tile]) - ratio * row
    results = []
    for pack in range(packs):
        rows = []
        for tile in range(tiles):
            index = sub + 8 * tile
            lower = jnp.where(
                column < index, blocks[pack][tile], jnp.where(column == index, 1.0, 0.0)
            )
            rows.append(lower * lax.rsqrt(pivots[pack][tile]))
        results.append(jnp.concatenate(rows, axis=0))
    return results


def eliminate(panel, pack, lower_ref, work_ref, members):
    per_pack = LANES // PANEL
    start = panel * PANEL
    after = start + PANEL
    first = after // LANES * LANES
    total = work_ref.shape[2]
    lower = lower_ref[pack]
    owner = lax.broadcasted_iota(jnp.int32, (PANEL, LANES), 1) // PANEL
    spread = jnp.concatenate(
        [jnp.where(owner == place, lower, 0.0) for place in range(per_pack)], axis=0
    )
    stacked = jnp.concatenate(
        [
            work_ref[pack * per_pack + place, start:after, first:]
            for place in range(per_pack)
        ],
        axis=0,
    )
    solved = jnp.dot(
        spread, stacked, precision=lax.Precision.HIGHEST, preferred_element_type=F32
    )
    for place in range(per_pack):
        region = pack * per_pack + place
        rows = solved[place * PANEL : (place + 1) * PANEL]
        work_ref[region, start:after, members:] = rows[:, members - first :]
        if after < members:
            high, mid, low = split3(rows)
            left = jnp.concatenate([high, high, mid, mid, high, low], axis=0)
            right = jnp.concatenate([high, mid, high, mid, low, high], axis=0)
            change = lax.dot_general(
                left[:, : members - first], right, (((0,), (0,)), ((), ())),
                preferred_element_type=F32,
            )
            work_ref[region, after:members, first:total] = (
                work_ref[region, after:members, first:total] - change[after - first :]
            )


def analysis_kernel(
    ids_ref, count_ref, loc_ref, prior_ref, rows_ref, states_ref, *rest
):
    obs_refs, (out_ref, scaled_ref, work_ref, mean_ref, lower_ref) = rest[:-5], rest[-5:]
    regions, members = prior_ref.shape
    sources, members_dev = states_ref.shape[0], states_ref.shape[2]
    points = states_ref.shape[3]
    packs = regions * PANEL // LANES

    @pl.loop(0, regions)
    def _(region):
        region_setup(
            region, ids_ref, count_ref, loc_ref, prior_ref, rows_ref, states_ref,
            obs_refs, scaled_ref, work_ref, mean_ref,
        )

    for panel in range(members // PANEL):
        lowers = factor_diagonals(panel, packs, work_ref)
        for pack in range(packs):
            lower_ref[pack] = lowers[pack]

        @pl.loop(0, packs)
        def _(pack):
            eliminate(panel, pack, lower_ref, work_ref, members)

    @pl.loop(0, regions)
    def _(region):
        moved = work_ref[region, :, members : members + points]
        solved = work_ref[region, :, members + points :]
        solved = jnp.concatenate([solved] * (points // LANES), axis=1)
        shift = mean_ref[region, :1] + jnp.sum(solved * moved, axis=0, keepdims=True)
        result = (shift + jnp.sqrt(members - 1.0) * moved).astype(BF16)
        for source in range(sources):
            out_ref[source, region] = result[
                source * members_dev : (source + 1) * members_dev
            ]


def analyse(ids, counts, loc, prior_rows, rows, states, obs_parts):
    regions, members = prior_rows.shape
    points = states.shape[3]
    slots = ids.shape[0] // regions
    width = obs_parts[0].shape[3]
    smem = pl.BlockSpec(memory_space=pltpu.SMEM)
    vmem = pl.BlockSpec(memory_space=pltpu.VMEM)
    return pl.pallas_call(
        analysis_kernel,
        out_shape=jax.ShapeDtypeStruct(states.shape, states.dtype),
        in_specs=[smem] * 3 + [vmem] * (3 + len(obs_parts)),
        out_specs=vmem,
        scratch_shapes=[
            pltpu.VMEM((members, slots * width), BF16),
            pltpu.VMEM((regions, members, members + points + LANES), F32),
            pltpu.VMEM((regions, 8, points), F32),
            pltpu.VMEM((regions * PANEL // LANES, PANEL, LANES), F32),
        ],
        compiler_params=pltpu.CompilerParams(vmem_limit_bytes=56 << 20),
    )(ids, counts, loc, prior_rows, rows, states, *obs_parts)


def body(
    ensemble_state, obs_ens, innovation, obs_prec, block_list, block_count, loc_weight, prior_weight
):
    spaces = lax.axis_size("space")
    mem_count = lax.axis_size("mem")
    members_dev, regions_dev, points = ensemble_state.shape
    blocks_dev, width = obs_ens.shape[1:]
    group_size = regions_dev // mem_count
    slots = block_list.shape[1]
    piece = members_dev // CHUNKS
    first_row = lax.axis_index("mem") * group_size

    def own(array):
        return lax.dynamic_slice_in_dim(array, first_row, group_size, 0)

    by_block = jnp.transpose(
        obs_ens.reshape(CHUNKS, piece, blocks_dev, width), (0, 2, 1, 3)
    )
    inner = 2 ** ((spaces.bit_length() - 1) // 2)
    all_ids = block_list.reshape(regions_dev * slots)
    source = (all_ids // blocks_dev) ^ lax.axis_index("space")
    places = source * blocks_dev + all_ids % blocks_dev
    own_chunks = [by_block[chunk] for chunk in range(CHUNKS)]
    rows = jnp.concatenate([obs_prec, innovation], axis=1)
    rows = jnp.broadcast_to(rows, (spaces,) + rows.shape)
    by_region = jnp.transpose(ensemble_state, (1, 0, 2)).reshape(
        mem_count, group_size, members_dev, points
    )
    obs_parts = []
    outer_offsets = range(inner, spaces, inner)
    inner_offsets = range(1, inner)
    sources = [[None] * spaces for _ in own_chunks]
    for stage in range(CHUNKS + 1):
        sent = {"next": own_chunks[stage + 1 :], "inner": [], "outer": []}
        payload = []
        if stage < CHUNKS:
            mine = own_chunks[stage]
            sources[stage][0] = (mine, 0)
            payload.append(mine)
            sent["outer"] = [swap(mine, spaces, offset) for offset in outer_offsets]
        if stage > 0:
            payload += [sources[stage - 1][offset][0] for offset in outer_offsets]
        payload = jnp.concatenate(payload, axis=0) if len(payload) > 1 else payload[0]
        sent["inner"] = [swap(payload, spaces, offset) for offset in inner_offsets]
        if stage == 0:
            sent["rows"], sent["states"] = rows, by_region
        sent = lax.optimization_barrier(sent)
        own_chunks[stage + 1 :] = sent["next"]
        if stage == 0:
            rows = lax.all_to_all(
                sent["rows"], "space", split_axis=0, concat_axis=0, tiled=True
            ).reshape(spaces * blocks_dev, 2 * width)
            states = lax.all_to_all(
                sent["states"], "mem", split_axis=0, concat_axis=0, tiled=True
            )
        for offset, array in zip(outer_offsets, sent["outer"]):
            sources[stage][offset] = (array, 0)
        for offset, array in zip(inner_offsets, sent["inner"]):
            start = 0
            if stage < CHUNKS:
                sources[stage][offset] = (array, 0)
                start = blocks_dev
            if stage > 0:
                for index, first in enumerate(outer_offsets):
                    sources[stage - 1][first + offset] = (
                        array, start + index * blocks_dev
                    )
        if stage > 0:
            picked = pick(places, spaces * blocks_dev, sources[stage - 1])
            picked = picked.reshape(mem_count, group_size * slots, piece, width)
            obs_parts.append(
                lax.all_to_all(picked, "mem", split_axis=0, concat_axis=0, tiled=True)
            )
    result = analyse(
        own(block_list).reshape(group_size * slots),
        own(block_count),
        own(loc_weight).reshape(group_size * slots),
        own(prior_weight),
        rows,
        states,
        obs_parts,
    )
    back = lax.all_to_all(result, "mem", split_axis=0, concat_axis=0, tiled=True)
    return jnp.transpose(back.reshape(regions_dev, members_dev, points), (1, 0, 2))


def solution(mesh):
    return jax.shard_map(
        body,
        mesh=mesh,
        in_specs=(
            P("mem", "space", None),
            P("mem", "space", None),
            P("space", None),
            P("space", None),
            P("space", None),
            P("space"),
            P("space", None),
            P("space", None),
        ),
        out_specs=P("mem", "space", None),
        check_vma=False,
    )
```

```python
import functools

import jax
import jax.numpy as jnp
from jax import lax
from jax.experimental import pallas as pl
from jax.experimental.pallas import tpu as pltpu
from jax.sharding import PartitionSpec as P

INFLATION = 1.1
PANEL = 32
LANES = 128
CHUNKS = 4
F32 = jnp.float32
BF16 = jnp.bfloat16


def split3(value):
    high = value.astype(BF16)
    rest = value - high.astype(F32)
    mid = rest.astype(BF16)
    low = (rest - mid.astype(F32)).astype(BF16)
    return high, mid, low


def weights_kernel(ids_ref, local_ref, rows_ref, out_ref):
    width = out_ref.shape[1] // 2

    @pl.loop(0, out_ref.shape[0] // 8, unroll=4)
    def _(group):
        prec, innov = [], []
        for inside in range(8):
            entry = group * 8 + inside
            row = rows_ref[pl.ds(ids_ref[entry], 1), :]
            prec.append(local_ref[entry] * row[:, :width])
            innov.append(row[:, width:])
        scale = jnp.sqrt(jnp.concatenate(prec, axis=0))
        first = pl.multiple_of(group * 8, 8)
        out_ref[pl.ds(first, 8), :width] = scale
        out_ref[pl.ds(first, 8), width:] = scale * jnp.concatenate(innov, axis=0)


def weights(ids, local, rows):
    smem = pl.BlockSpec(memory_space=pltpu.SMEM)
    vmem = pl.BlockSpec(memory_space=pltpu.VMEM)
    return pl.pallas_call(
        weights_kernel,
        out_shape=jax.ShapeDtypeStruct((ids.shape[0], rows.shape[1]), F32),
        in_specs=[smem, smem, vmem],
        out_specs=vmem,
    )(ids, local, rows)


def pick_kernel(layout, ids_ref, scale_ref, *rest):
    shard_refs, (out_ref, table_ref, sems) = rest[:-3], rest[-3:]
    rows = table_ref.shape[0] // len(layout)
    width = table_ref.shape[2]
    copies = [
        pltpu.make_async_copy(
            shard_refs[operand].at[start : start + rows],
            table_ref.at[index * rows : (index + 1) * rows],
            sems.at[index],
        )
        for index, (operand, start) in enumerate(layout)
    ]
    for copy in copies:
        copy.start()
    for copy in copies:
        copy.wait()

    @pl.loop(0, out_ref.shape[0] // 8)
    def _(group):
        first = pl.multiple_of(group * 8, 8)
        scales = scale_ref[pl.ds(first, 8), :width]
        for inside in range(8):
            entry = group * 8 + inside
            values = table_ref[ids_ref[entry]].astype(F32)
            out_ref[entry] = (values * scales[inside : inside + 1]).astype(BF16)


def pick(ids, scales, table_rows, sources):
    operands = []
    layout = []
    for array, start in sources:
        known = [index for index, other in enumerate(operands) if other is array]
        if not known:
            operands.append(array)
        layout.append((known[0] if known else len(operands) - 1, start))
    row, dtype = operands[0].shape[1:], operands[0].dtype
    size = row[0] * row[1]
    return pl.pallas_call(
        functools.partial(pick_kernel, layout),
        out_shape=jax.ShapeDtypeStruct((ids.shape[0],) + row, dtype),
        in_specs=[
            pl.BlockSpec(memory_space=pltpu.SMEM),
            pl.BlockSpec(memory_space=pltpu.VMEM),
        ]
        + [pl.BlockSpec(memory_space=pl.ANY)] * len(operands),
        out_specs=pl.BlockSpec(memory_space=pltpu.VMEM),
        scratch_shapes=[
            pltpu.VMEM((table_rows,) + row, dtype),
            pltpu.SemaphoreType.DMA((len(layout),)),
        ],
        cost_estimate=pl.CostEstimate(
            flops=ids.shape[0] * size,
            bytes_accessed=4 * (ids.shape[0] + table_rows) * size,
            transcendentals=0,
        ),
        compiler_params=pltpu.CompilerParams(vmem_limit_bytes=16 << 20),
    )(ids, scales, *operands)


def swap(value, spaces, offset):
    return lax.ppermute(value, "space", [(s, s ^ offset) for s in range(spaces)])


def region_setup(
    region, first, prior_ref, weight_ref, states_ref, obs_refs, scaled_ref, work_ref, mean_ref
):
    members = prior_ref.shape[1]
    slots = weight_ref.shape[0] // (states_ref.shape[0] * prior_ref.shape[0])
    sources = states_ref.shape[0]
    members_dev = states_ref.shape[2]
    piece, width = obs_refs[0].shape[2:]
    for slot in range(slots):
        for source in range(sources):
            for index, obs_ref in enumerate(obs_refs):
                start = source * members_dev + index * piece
                scaled_ref[start : start + piece, slot * width : (slot + 1) * width] = (
                    obs_ref[source, region * slots + slot]
                )
    own = weight_ref[pl.ds(pl.multiple_of(first + region * slots, slots), slots), width:]
    innov_parts = [own[slot : slot + 1] for slot in range(slots)]
    scaled = scaled_ref[...]
    contract = (((1,), (1,)), ((), ()))
    gram = lax.dot_general(scaled, scaled, contract, preferred_element_type=F32)
    innov = jnp.concatenate(innov_parts, axis=1)
    high, mid, low = (part.astype(F32) for part in split3(innov))
    which = lax.broadcasted_iota(jnp.int32, (16, slots * width), 0)
    innov_rows = jnp.where(
        which == 0, high, jnp.where(which == 1, mid, jnp.where(which == 2, low, 0.0))
    ).astype(BF16)
    projection = jnp.sum(
        lax.dot_general(scaled, innov_rows, contract, preferred_element_type=F32),
        axis=1, keepdims=True,
    )
    on_diag = lax.broadcasted_iota(jnp.int32, (members, members), 0) == (
        lax.broadcasted_iota(jnp.int32, (members, members), 1)
    )
    prior_row = prior_ref[pl.ds(region, 1), :]
    share_row = prior_row / jnp.sum(prior_row, axis=1, keepdims=True)
    share_col = jnp.sum(jnp.where(on_diag, share_row, 0.0), axis=1, keepdims=True)
    root_row = jnp.sqrt(members * share_row)
    root_col = jnp.sqrt(members * share_col)
    left_row = jnp.sum(share_col * gram, axis=0, keepdims=True)
    left_col = jnp.sum(share_row * gram, axis=1, keepdims=True)
    total = jnp.sum(left_row * share_row, axis=1, keepdims=True)
    centred = (gram - left_row) - (left_col - total)
    system = root_col * centred * root_row
    work_ref[region, :, :members] = system + jnp.where(
        on_diag, (members - 1) / INFLATION, 0.0
    )
    vector = root_col * (
        projection - jnp.sum(share_col * projection, axis=0, keepdims=True)
    )
    states = jnp.concatenate(
        [states_ref[source, region].astype(F32) for source in range(sources)], axis=0
    )
    mean = jnp.sum(share_col * states, axis=0, keepdims=True)
    mean_ref[region] = jnp.broadcast_to(mean, mean_ref.shape[1:])
    points = states.shape[1]
    work_ref[region, :, members : members + points] = root_col * (states - mean)
    work_ref[region, :, members + points :] = jnp.broadcast_to(vector, (members, LANES))


def factor_diagonals(panel, packs, work_ref):
    per_pack = LANES // PANEL
    start = panel * PANEL
    base, offset = start // LANES * LANES, start % LANES
    lane = lax.broadcasted_iota(jnp.int32, (8, LANES), 1)
    sub = lax.broadcasted_iota(jnp.int32, (8, LANES), 0)
    owner, column = lane // PANEL, lane % PANEL
    tiles = PANEL // 8
    blocks = []
    for pack in range(packs):
        pieces = []
        for tile in range(tiles):
            merged = None
            for place in range(per_pack):
                region = pack * per_pack + place
                raw = work_ref[
                    region, start + 8 * tile : start + 8 * tile + 8, base : base + LANES
                ]
                shift = (place * PANEL - offset) % LANES
                if shift:
                    raw = pltpu.roll(raw, shift, axis=1)
                merged = raw if merged is None else jnp.where(owner == place, raw, merged)
            pieces.append(merged)
        blocks.append(pieces)
    pivots = [[jnp.ones((8, LANES), F32) for _ in range(tiles)] for _ in range(packs)]
    for home in range(tiles):
        columns = [
            [
                {
                    tile: jnp.take_along_axis(
                        blocks[pack][tile], owner * PANEL + 8 * home + inside,
                        axis=1, mode="promise_in_bounds",
                    )
                    for tile in range(home, tiles)
                }
                for inside in range(8)
            ]
            for pack in range(packs)
        ]
        for inside in range(8):
            at_step = column == 8 * home + inside
            below = sub > inside
            for pack in range(packs):
                pieces = blocks[pack]
                pivot = columns[pack][inside][home][inside : inside + 1, :]
                inverse = 1.0 / pivot
                row = jnp.where(at_step[:1], 1.0, pieces[home][inside : inside + 1, :])
                pivots[pack][home] = jnp.where(sub == inside, pivot, pivots[pack][home])
                later = [
                    columns[pack][other][home][inside : inside + 1, :]
                    for other in range(inside + 1, 8)
                ]
                for tile in range(home, tiles):
                    ratio = columns[pack][inside][tile] * inverse
                    cleared = at_step
                    if tile == home:
                        ratio = jnp.where(below, ratio, 0.0)
                        cleared = at_step & below
                    pieces[tile] = jnp.where(cleared, 0.0, pieces[tile]) - ratio * row
                    for other in range(inside + 1, 8):
                        columns[pack][other][tile] = (
                            columns[pack][other][tile] - ratio * later[other - inside - 1]
                        )
    results = []
    for pack in range(packs):
        rows = []
        for tile in range(tiles):
            index = sub + 8 * tile
            lower = jnp.where(
                column < index, blocks[pack][tile], jnp.where(column == index, 1.0, 0.0)
            )
            rows.append(lower * lax.rsqrt(pivots[pack][tile]))
        results.append(jnp.concatenate(rows, axis=0))
    return results


def eliminate(panel, pack, lower_ref, work_ref, members):
    per_pack = LANES // PANEL
    start = panel * PANEL
    after = start + PANEL
    first = after // LANES * LANES
    total = work_ref.shape[2]
    lower = lower_ref[pack]
    owner = lax.broadcasted_iota(jnp.int32, (PANEL, LANES), 1) // PANEL
    spread = jnp.concatenate(
        [jnp.where(owner == place, lower, 0.0) for place in range(per_pack)], axis=0
    )
    stacked = jnp.concatenate(
        [
            work_ref[pack * per_pack + place, start:after, first:]
            for place in range(per_pack)
        ],
        axis=0,
    )
    solved = jnp.dot(
        spread, stacked, precision=lax.Precision.HIGHEST, preferred_element_type=F32
    )
    for place in range(per_pack):
        region = pack * per_pack + place
        rows = solved[place * PANEL : (place + 1) * PANEL]
        work_ref[region, start:after, members:] = rows[:, members - first :]
        if after < members:
            high, mid, low = split3(rows)
            left = jnp.concatenate([high, high, mid, mid, high, low], axis=0)
            right = jnp.concatenate([high, mid, high, mid, low, high], axis=0)
            change = lax.dot_general(
                left[:, : members - first], right, (((0,), (0,)), ((), ())),
                preferred_element_type=F32,
            )
            work_ref[region, after:members, first:total] = (
                work_ref[region, after:members, first:total] - change[after - first :]
            )


def analysis_kernel(first_ref, prior_ref, weight_ref, states_ref, *rest):
    obs_refs, (out_ref, scaled_ref, work_ref, mean_ref, lower_ref) = rest[:-5], rest[-5:]
    regions, members = prior_ref.shape
    sources, members_dev = states_ref.shape[0], states_ref.shape[2]
    points = states_ref.shape[3]
    packs = regions * PANEL // LANES
    ways = scaled_ref.shape[0]

    @pl.loop(0, regions // ways)
    def _(step):
        for way in range(ways):
            region_setup(
                step * ways + way, first_ref[0], prior_ref, weight_ref, states_ref,
                obs_refs, scaled_ref.at[way], work_ref, mean_ref,
            )

    for panel in range(members // PANEL):
        lowers = factor_diagonals(panel, packs, work_ref)
        for pack in range(packs):
            lower_ref[pack] = lowers[pack]

        @pl.loop(0, packs)
        def _(pack):
            eliminate(panel, pack, lower_ref, work_ref, members)

    @pl.loop(0, regions)
    def _(region):
        moved = work_ref[region, :, members : members + points]
        solved = work_ref[region, :, members + points :]
        solved = jnp.concatenate([solved] * (points // LANES), axis=1)
        shift = mean_ref[region, :1] + jnp.sum(solved * moved, axis=0, keepdims=True)
        result = (shift + jnp.sqrt(members - 1.0) * moved).astype(BF16)
        for source in range(sources):
            out_ref[source, region] = result[
                source * members_dev : (source + 1) * members_dev
            ]


def analyse(first, prior_rows, weight_rows, states, obs_parts):
    regions, members = prior_rows.shape
    points = states.shape[3]
    slots = weight_rows.shape[0] // (states.shape[0] * regions)
    width = obs_parts[0].shape[3]
    vmem = pl.BlockSpec(memory_space=pltpu.VMEM)
    return pl.pallas_call(
        analysis_kernel,
        out_shape=jax.ShapeDtypeStruct(states.shape, states.dtype),
        in_specs=[pl.BlockSpec(memory_space=pltpu.SMEM)] + [vmem] * (3 + len(obs_parts)),
        out_specs=vmem,
        scratch_shapes=[
            pltpu.VMEM((2, members, slots * width), BF16),
            pltpu.VMEM((regions, members, members + points + LANES), F32),
            pltpu.VMEM((regions, 8, points), F32),
            pltpu.VMEM((regions * PANEL // LANES, PANEL, LANES), F32),
        ],
        compiler_params=pltpu.CompilerParams(vmem_limit_bytes=56 << 20),
    )(first, prior_rows, weight_rows, states, *obs_parts)


def body(
    ensemble_state, obs_ens, innovation, obs_prec, block_list, block_count, loc_weight, prior_weight
):
    spaces = lax.axis_size("space")
    mem_count = lax.axis_size("mem")
    members_dev, regions_dev, points = ensemble_state.shape
    blocks_dev, width = obs_ens.shape[1:]
    group_size = regions_dev // mem_count
    slots = block_list.shape[1]
    piece = members_dev // CHUNKS
    first_row = lax.axis_index("mem") * group_size
    by_block = jnp.transpose(
        obs_ens.reshape(CHUNKS, piece, blocks_dev, width), (0, 2, 1, 3)
    )
    inner = 2 ** ((spaces.bit_length() - 1) // 2)
    all_ids = block_list.reshape(regions_dev * slots)
    source = (all_ids // blocks_dev) ^ lax.axis_index("space")
    places = source * blocks_dev + all_ids % blocks_dev
    own_chunks = [by_block[chunk] for chunk in range(CHUNKS)]
    active = jnp.arange(slots, dtype=jnp.int32)[None, :] < block_count[:, None]
    local = jnp.where(active, loc_weight, 0.0).reshape(regions_dev * slots)
    rows = lax.all_gather(
        jnp.concatenate([obs_prec, innovation], axis=1), "space", axis=0, tiled=True
    )
    by_region = jnp.transpose(ensemble_state, (1, 0, 2)).reshape(
        mem_count, group_size, members_dev, points
    )
    states = lax.all_to_all(by_region, "mem", split_axis=0, concat_axis=0, tiled=True)
    obs_parts = []
    outer_offsets = range(inner, spaces, inner)
    inner_offsets = range(1, inner)
    sources = [[None] * spaces for _ in own_chunks]
    for stage in range(CHUNKS + 1):
        sent = {"next": own_chunks[stage + 1 :], "inner": [], "outer": []}
        payload = []
        if stage < CHUNKS:
            mine = own_chunks[stage]
            sources[stage][0] = (mine, 0)
            payload.append(mine)
            sent["outer"] = [swap(mine, spaces, offset) for offset in outer_offsets]
        if stage > 0:
            payload += [sources[stage - 1][offset][0] for offset in outer_offsets]
        payload = jnp.concatenate(payload, axis=0) if len(payload) > 1 else payload[0]
        sent["inner"] = [swap(payload, spaces, offset) for offset in inner_offsets]
        if stage == 1:
            sent["rows"], sent["states"] = rows, states
        sent = lax.optimization_barrier(sent)
        own_chunks[stage + 1 :] = sent["next"]
        if stage == 1:
            states = sent["states"]
            weight_rows = weights(all_ids, local, sent["rows"])
        for offset, array in zip(outer_offsets, sent["outer"]):
            sources[stage][offset] = (array, 0)
        for offset, array in zip(inner_offsets, sent["inner"]):
            start = 0
            if stage < CHUNKS:
                sources[stage][offset] = (array, 0)
                start = blocks_dev
            if stage > 0:
                for index, first in enumerate(outer_offsets):
                    sources[stage - 1][first + offset] = (
                        array, start + index * blocks_dev
                    )
        if stage > 0:
            picked = pick(
                places, weight_rows, spaces * blocks_dev, sources[stage - 1]
            )
            picked = picked.reshape(mem_count, group_size * slots, piece, width)
            obs_parts.append(
                lax.all_to_all(picked, "mem", split_axis=0, concat_axis=0, tiled=True)
            )
    result = analyse(
        (first_row * slots).reshape(1),
        lax.dynamic_slice_in_dim(prior_weight, first_row, group_size, 0),
        weight_rows,
        states,
        obs_parts,
    )
    back = lax.all_to_all(result, "mem", split_axis=0, concat_axis=0, tiled=True)
    return jnp.transpose(back.reshape(regions_dev, members_dev, points), (1, 0, 2))


def solution(mesh):
    return jax.shard_map(
        body,
        mesh=mesh,
        in_specs=(
            P("mem", "space", None),
            P("mem", "space", None),
            P("space", None),
            P("space", None),
            P("space", None),
            P("space"),
            P("space", None),
            P("space", None),
        ),
        out_specs=P("mem", "space", None),
        check_vma=False,
    )
```

```python
import functools

import jax
import jax.numpy as jnp
from jax import lax
from jax.experimental import pallas as pl
from jax.experimental.pallas import tpu as pltpu
from jax.sharding import PartitionSpec as P

INFLATION = 1.1
PANEL = 32
LANES = 128
CHUNKS = 4
F32 = jnp.float32
BF16 = jnp.bfloat16


def split3(value):
    high = value.astype(BF16)
    rest = value - high.astype(F32)
    mid = rest.astype(BF16)
    low = (rest - mid.astype(F32)).astype(BF16)
    return high, mid, low


def weights_kernel(ids_ref, local_ref, rows_ref, out_ref):
    width = out_ref.shape[1] // 2

    @pl.loop(0, out_ref.shape[0] // 8, unroll=4)
    def _(group):
        prec, innov = [], []
        for inside in range(8):
            entry = group * 8 + inside
            row = rows_ref[pl.ds(ids_ref[entry], 1), :]
            prec.append(local_ref[entry] * row[:, :width])
            innov.append(row[:, width:])
        scale = jnp.sqrt(jnp.concatenate(prec, axis=0))
        first = pl.multiple_of(group * 8, 8)
        out_ref[pl.ds(first, 8), :width] = scale
        out_ref[pl.ds(first, 8), width:] = scale * jnp.concatenate(innov, axis=0)


def weights(ids, local, rows):
    smem = pl.BlockSpec(memory_space=pltpu.SMEM)
    vmem = pl.BlockSpec(memory_space=pltpu.VMEM)
    return pl.pallas_call(
        weights_kernel,
        out_shape=jax.ShapeDtypeStruct((ids.shape[0], rows.shape[1]), F32),
        in_specs=[smem, smem, vmem],
        out_specs=vmem,
    )(ids, local, rows)


def pick_kernel(layout, ids_ref, scale_ref, *rest):
    shard_refs, (out_ref, table_ref, sems) = rest[:-3], rest[-3:]
    rows = table_ref.shape[0] // len(layout)
    width = table_ref.shape[2]
    copies = [
        pltpu.make_async_copy(
            shard_refs[operand].at[start : start + rows],
            table_ref.at[index * rows : (index + 1) * rows],
            sems.at[index],
        )
        for index, (operand, start) in enumerate(layout)
    ]
    for copy in copies:
        copy.start()
    for copy in copies:
        copy.wait()

    @pl.loop(0, out_ref.shape[0] // 8)
    def _(group):
        first = pl.multiple_of(group * 8, 8)
        scales = scale_ref[pl.ds(first, 8), :width]
        for inside in range(8):
            entry = group * 8 + inside
            values = table_ref[ids_ref[entry]].astype(F32)
            out_ref[entry] = (values * scales[inside : inside + 1]).astype(BF16)


def pick(ids, scales, table_rows, sources):
    operands = []
    layout = []
    for array, start in sources:
        known = [index for index, other in enumerate(operands) if other is array]
        if not known:
            operands.append(array)
        layout.append((known[0] if known else len(operands) - 1, start))
    row, dtype = operands[0].shape[1:], operands[0].dtype
    size = row[0] * row[1]
    return pl.pallas_call(
        functools.partial(pick_kernel, layout),
        out_shape=jax.ShapeDtypeStruct((ids.shape[0],) + row, dtype),
        in_specs=[
            pl.BlockSpec(memory_space=pltpu.SMEM),
            pl.BlockSpec(memory_space=pltpu.VMEM),
        ]
        + [pl.BlockSpec(memory_space=pl.ANY)] * len(operands),
        out_specs=pl.BlockSpec(memory_space=pltpu.VMEM),
        scratch_shapes=[
            pltpu.VMEM((table_rows,) + row, dtype),
            pltpu.SemaphoreType.DMA((len(layout),)),
        ],
        cost_estimate=pl.CostEstimate(
            flops=ids.shape[0] * size,
            bytes_accessed=4 * (ids.shape[0] + table_rows) * size,
            transcendentals=0,
        ),
        compiler_params=pltpu.CompilerParams(vmem_limit_bytes=16 << 20),
    )(ids, scales, *operands)


def swap(value, spaces, offset):
    return lax.ppermute(value, "space", [(s, s ^ offset) for s in range(spaces)])


def region_setup(
    region, first, prior_ref, weight_ref, states_ref, obs_refs, scaled_ref, work_ref, mean_ref
):
    members = prior_ref.shape[1]
    slots = weight_ref.shape[0] // (states_ref.shape[0] * prior_ref.shape[0])
    sources = states_ref.shape[0]
    members_dev = states_ref.shape[2]
    piece, width = obs_refs[0].shape[2:]
    for slot in range(slots):
        for source in range(sources):
            for index, obs_ref in enumerate(obs_refs):
                start = source * members_dev + index * piece
                scaled_ref[start : start + piece, slot * width : (slot + 1) * width] = (
                    obs_ref[source, region * slots + slot]
                )
    own = weight_ref[pl.ds(pl.multiple_of(first + region * slots, slots), slots), width:]
    innov_parts = [own[slot : slot + 1] for slot in range(slots)]
    scaled = scaled_ref[...]
    contract = (((1,), (1,)), ((), ()))
    gram = lax.dot_general(scaled, scaled, contract, preferred_element_type=F32)
    innov = jnp.concatenate(innov_parts, axis=1)
    high, mid, low = (part.astype(F32) for part in split3(innov))
    which = lax.broadcasted_iota(jnp.int32, (16, slots * width), 0)
    innov_rows = jnp.where(
        which == 0, high, jnp.where(which == 1, mid, jnp.where(which == 2, low, 0.0))
    ).astype(BF16)
    projection = jnp.sum(
        lax.dot_general(scaled, innov_rows, contract, preferred_element_type=F32),
        axis=1, keepdims=True,
    )
    on_diag = lax.broadcasted_iota(jnp.int32, (members, members), 0) == (
        lax.broadcasted_iota(jnp.int32, (members, members), 1)
    )
    prior_row = prior_ref[pl.ds(region, 1), :]
    share_row = prior_row / jnp.sum(prior_row, axis=1, keepdims=True)
    share_col = jnp.sum(jnp.where(on_diag, share_row, 0.0), axis=1, keepdims=True)
    root_row = jnp.sqrt(members * share_row)
    root_col = jnp.sqrt(members * share_col)
    left_row = jnp.sum(share_col * gram, axis=0, keepdims=True)
    left_col = jnp.sum(share_row * gram, axis=1, keepdims=True)
    total = jnp.sum(left_row * share_row, axis=1, keepdims=True)
    centred = (gram - left_row) - (left_col - total)
    system = root_col * centred * root_row
    work_ref[region, :, :members] = system + jnp.where(
        on_diag, (members - 1) / INFLATION, 0.0
    )
    vector = root_col * (
        projection - jnp.sum(share_col * projection, axis=0, keepdims=True)
    )
    states = jnp.concatenate(
        [states_ref[source, region].astype(F32) for source in range(sources)], axis=0
    )
    mean = jnp.sum(share_col * states, axis=0, keepdims=True)
    mean_ref[region] = jnp.broadcast_to(mean, mean_ref.shape[1:])
    points = states.shape[1]
    work_ref[region, :, members : members + points] = root_col * (states - mean)
    work_ref[region, :, members + points :] = jnp.broadcast_to(vector, (members, LANES))


def factor_diagonals(panel, chosen, work_ref):
    per_pack = LANES // PANEL
    start = panel * PANEL
    base, offset = start // LANES * LANES, start % LANES
    lane = lax.broadcasted_iota(jnp.int32, (8, LANES), 1)
    sub = lax.broadcasted_iota(jnp.int32, (8, LANES), 0)
    owner, column = lane // PANEL, lane % PANEL
    tiles = PANEL // 8
    blocks = []
    packs = len(chosen)
    for pack in chosen:
        pieces = []
        for tile in range(tiles):
            merged = None
            for place in range(per_pack):
                region = pack * per_pack + place
                raw = work_ref[
                    region, start + 8 * tile : start + 8 * tile + 8, base : base + LANES
                ]
                shift = (place * PANEL - offset) % LANES
                if shift:
                    raw = pltpu.roll(raw, shift, axis=1)
                merged = raw if merged is None else jnp.where(owner == place, raw, merged)
            pieces.append(merged)
        blocks.append(pieces)
    pivots = [[jnp.ones((8, LANES), F32) for _ in range(tiles)] for _ in range(packs)]
    for home in range(tiles):
        columns = [
            [
                {
                    tile: jnp.take_along_axis(
                        blocks[pack][tile], owner * PANEL + 8 * home + inside,
                        axis=1, mode="promise_in_bounds",
                    )
                    for tile in range(home, tiles)
                }
                for inside in range(8)
            ]
            for pack in range(packs)
        ]
        for inside in range(8):
            at_step = column == 8 * home + inside
            below = sub > inside
            for pack in range(packs):
                pieces = blocks[pack]
                pivot = columns[pack][inside][home][inside : inside + 1, :]
                inverse = 1.0 / pivot
                row = jnp.where(at_step[:1], 1.0, pieces[home][inside : inside + 1, :])
                pivots[pack][home] = jnp.where(sub == inside, pivot, pivots[pack][home])
                later = [
                    columns[pack][other][home][inside : inside + 1, :]
                    for other in range(inside + 1, 8)
                ]
                for tile in range(home, tiles):
                    ratio = columns[pack][inside][tile] * inverse
                    cleared = at_step
                    if tile == home:
                        ratio = jnp.where(below, ratio, 0.0)
                        cleared = at_step & below
                    pieces[tile] = jnp.where(cleared, 0.0, pieces[tile]) - ratio * row
                    for other in range(inside + 1, 8):
                        columns[pack][other][tile] = (
                            columns[pack][other][tile] - ratio * later[other - inside - 1]
                        )
    results = []
    for pack in range(packs):
        rows = []
        for tile in range(tiles):
            index = sub + 8 * tile
            lower = jnp.where(
                column < index, blocks[pack][tile], jnp.where(column == index, 1.0, 0.0)
            )
            rows.append(lower * lax.rsqrt(pivots[pack][tile]))
        results.append(jnp.concatenate(rows, axis=0))
    return results


def six_products(left, right, axis):
    high, mid, low = left
    left = jnp.concatenate([high, high, mid, mid, high, low], axis=axis)
    high, mid, low = right
    right = jnp.concatenate([high, mid, high, mid, low, high], axis=0)
    return lax.dot_general(
        left, right, (((axis,), (0,)), ((), ())), preferred_element_type=F32
    )


def eliminate(panel, pack, lower, work_ref, members):
    per_pack = LANES // PANEL
    start = panel * PANEL
    after = start + PANEL
    first = after // LANES * LANES
    total = work_ref.shape[2]
    owner = lax.broadcasted_iota(jnp.int32, (PANEL, LANES), 1) // PANEL
    spread = jnp.concatenate(
        [jnp.where(owner == place, lower, 0.0) for place in range(per_pack)], axis=0
    )
    stacked = jnp.concatenate(
        [
            work_ref[pack * per_pack + place, start:after, first:]
            for place in range(per_pack)
        ],
        axis=0,
    )
    solved = six_products(split3(spread), split3(stacked), 1)
    for place in range(per_pack):
        region = pack * per_pack + place
        rows = solved[place * PANEL : (place + 1) * PANEL]
        work_ref[region, start:after, members:] = rows[:, members - first :]
        if after < members:
            parts = split3(rows)
            change = six_products(
                [part[:, : members - first] for part in parts], parts, 0
            )
            work_ref[region, after:members, first:total] = (
                work_ref[region, after:members, first:total] - change[after - first :]
            )


def analysis_kernel(first_ref, prior_ref, weight_ref, states_hbm, *rest):
    obs_hbm = rest[: (len(rest) - 6) // 2]
    out_ref, scaled_ref, work_ref, mean_ref, sems, states_ref = rest[
        len(obs_hbm) : len(obs_hbm) + 6
    ]
    obs_refs = rest[len(obs_hbm) + 6 :]
    regions, members = prior_ref.shape
    sources, members_dev = states_ref.shape[0], states_ref.shape[2]
    points = states_ref.shape[3]
    packs = regions * PANEL // LANES
    ways = scaled_ref.shape[0]
    batches = sems.shape[0]
    batch_regions = regions // batches

    def loads(batch):
        copies = []
        pairs = [(states_hbm, states_ref)] + list(zip(obs_hbm, obs_refs))
        for index, (hbm, vmem) in enumerate(pairs):
            size = vmem.shape[1] // batches
            part = pl.ds(batch * size, size)
            copies.append(
                pltpu.make_async_copy(
                    hbm.at[:, part], vmem.at[:, part], sems.at[batch, index]
                )
            )
        return copies

    for batch in range(batches):
        for copy in loads(batch):
            copy.start()

    @pl.loop(0, batches)
    def _(batch):
        for copy in loads(batch):
            copy.wait()

        @pl.loop(0, batch_regions // ways)
        def _(step):
            for way in range(ways):
                region_setup(
                    batch * batch_regions + step * ways + way, first_ref[0], prior_ref,
                    weight_ref, states_ref, obs_refs, scaled_ref.at[way], work_ref, mean_ref,
                )

    halves = [range(packs // 2), range(packs // 2, packs)]
    panels = members // PANEL
    lowers = factor_diagonals(0, halves[0], work_ref)
    for panel in range(panels):
        for half in range(2):
            for pack, lower in zip(halves[half], lowers):
                eliminate(panel, pack, lower, work_ref, members)
            if panel + half < panels:
                lowers = factor_diagonals(panel + half, halves[1 - half], work_ref)

    @pl.loop(0, regions)
    def _(region):
        moved = work_ref[region, :, members : members + points]
        solved = work_ref[region, :, members + points :]
        solved = jnp.concatenate([solved] * (points // LANES), axis=1)
        shift = mean_ref[region, :1] + jnp.sum(solved * moved, axis=0, keepdims=True)
        result = (shift + jnp.sqrt(members - 1.0) * moved).astype(BF16)
        for source in range(sources):
            out_ref[source, region] = result[
                source * members_dev : (source + 1) * members_dev
            ]


def analyse(first, prior_rows, weight_rows, states, obs_parts):
    regions, members = prior_rows.shape
    points = states.shape[3]
    slots = weight_rows.shape[0] // (states.shape[0] * regions)
    width = obs_parts[0].shape[3]
    vmem = pl.BlockSpec(memory_space=pltpu.VMEM)
    loaded = [states] + obs_parts
    return pl.pallas_call(
        analysis_kernel,
        out_shape=jax.ShapeDtypeStruct(states.shape, states.dtype),
        in_specs=[pl.BlockSpec(memory_space=pltpu.SMEM), vmem, vmem]
        + [pl.BlockSpec(memory_space=pl.ANY)] * len(loaded),
        out_specs=vmem,
        scratch_shapes=[
            pltpu.VMEM((2, members, slots * width), BF16),
            pltpu.VMEM((regions, members, members + points + LANES), F32),
            pltpu.VMEM((regions, 8, points), F32),
            pltpu.SemaphoreType.DMA((4, len(loaded))),
        ]
        + [pltpu.VMEM(array.shape, array.dtype) for array in loaded],
        compiler_params=pltpu.CompilerParams(vmem_limit_bytes=56 << 20),
    )(first, prior_rows, weight_rows, *loaded)


def body(
    ensemble_state, obs_ens, innovation, obs_prec, block_list, block_count, loc_weight, prior_weight
):
    spaces = lax.axis_size("space")
    mem_count = lax.axis_size("mem")
    members_dev, regions_dev, points = ensemble_state.shape
    blocks_dev, width = obs_ens.shape[1:]
    group_size = regions_dev // mem_count
    slots = block_list.shape[1]
    piece = members_dev // CHUNKS
    first_row = lax.axis_index("mem") * group_size
    by_block = jnp.transpose(
        obs_ens.reshape(CHUNKS, piece, blocks_dev, width), (0, 2, 1, 3)
    )
    inner = 2 ** ((spaces.bit_length() - 1) // 2)
    all_ids = block_list.reshape(regions_dev * slots)
    source = (all_ids // blocks_dev) ^ lax.axis_index("space")
    places = source * blocks_dev + all_ids % blocks_dev
    own_chunks = [by_block[chunk] for chunk in range(CHUNKS)]
    active = jnp.arange(slots, dtype=jnp.int32)[None, :] < block_count[:, None]
    local = jnp.where(active, loc_weight, 0.0).reshape(regions_dev * slots)
    rows_own = jnp.concatenate([obs_prec, innovation], axis=1)
    by_region = jnp.transpose(ensemble_state, (1, 0, 2)).reshape(
        mem_count, group_size, members_dev, points
    )
    states = lax.all_to_all(by_region, "mem", split_axis=0, concat_axis=0, tiled=True)
    obs_parts = []
    outer_offsets = range(inner, spaces, inner)
    inner_offsets = range(1, inner)
    sources = [[None] * spaces for _ in own_chunks]
    for stage in range(CHUNKS + 1):
        sent = {"next": own_chunks[stage + 1 :], "inner": [], "outer": []}
        payload = []
        if stage < CHUNKS:
            mine = own_chunks[stage]
            sources[stage][0] = (mine, 0)
            payload.append(mine)
            sent["outer"] = [swap(mine, spaces, offset) for offset in outer_offsets]
        if stage > 0:
            payload += [sources[stage - 1][offset][0] for offset in outer_offsets]
        payload = jnp.concatenate(payload, axis=0) if len(payload) > 1 else payload[0]
        sent["inner"] = [swap(payload, spaces, offset) for offset in inner_offsets]
        if stage == 0:
            sent["rows"] = [swap(rows_own, spaces, offset) for offset in outer_offsets]
        if stage == 1:
            rows_outer = jnp.concatenate([rows_own] + rows_outer, axis=0)
            sent["rows"] = [swap(rows_outer, spaces, offset) for offset in inner_offsets]
            sent["states"] = states
        if stage > 1:
            gate = places
            if stage < CHUNKS:
                gate, _ = lax.optimization_barrier((places, sent["outer"][0]))
            picked = pick(gate, weight_rows, spaces * blocks_dev, sources[stage - 2])
            picked = picked.reshape(mem_count, group_size * slots, piece, width)
            sent["picked"] = picked
            obs_parts.append(
                lax.all_to_all(picked, "mem", split_axis=0, concat_axis=0, tiled=True)
            )
        sent = lax.optimization_barrier(sent)
        own_chunks[stage + 1 :] = sent["next"]
        if stage == 0:
            rows_outer = sent["rows"]
        if stage == 1:
            states = sent["states"]
            rows_parts = [rows_outer] + sent["rows"]
            rows = jnp.stack(
                [part.reshape(spaces // inner, blocks_dev, 2 * width) for part in rows_parts],
                axis=1,
            ).reshape(spaces * blocks_dev, 2 * width)
            weight_rows = weights(places, local, rows)
        for offset, array in zip(outer_offsets, sent["outer"]):
            sources[stage][offset] = (array, 0)
        for offset, array in zip(inner_offsets, sent["inner"]):
            start = 0
            if stage < CHUNKS:
                sources[stage][offset] = (array, 0)
                start = blocks_dev
            if stage > 0:
                for index, first in enumerate(outer_offsets):
                    sources[stage - 1][first + offset] = (
                        array, start + index * blocks_dev
                    )
    picked = pick(places, weight_rows, spaces * blocks_dev, sources[CHUNKS - 1])
    picked = picked.reshape(mem_count, group_size * slots, piece, width)
    obs_parts.append(
        lax.all_to_all(picked, "mem", split_axis=0, concat_axis=0, tiled=True)
    )
    result = analyse(
        (first_row * slots).reshape(1),
        lax.dynamic_slice_in_dim(prior_weight, first_row, group_size, 0),
        weight_rows,
        states,
        obs_parts,
    )
    back = lax.all_to_all(result, "mem", split_axis=0, concat_axis=0, tiled=True)
    return jnp.transpose(back.reshape(regions_dev, members_dev, points), (1, 0, 2))


def solution(mesh):
    return jax.shard_map(
        body,
        mesh=mesh,
        in_specs=(
            P("mem", "space", None),
            P("mem", "space", None),
            P("space", None),
            P("space", None),
            P("space", None),
            P("space"),
            P("space", None),
            P("space", None),
        ),
        out_specs=P("mem", "space", None),
        check_vma=False,
    )
```

```python
import functools

import jax
import jax.numpy as jnp
from jax import lax
from jax.experimental import pallas as pl
from jax.experimental.pallas import tpu as pltpu
from jax.sharding import PartitionSpec as P

INFLATION = 1.1
PANEL = 32
LANES = 128
CHUNKS = 2
SPLIT = 2
F32 = jnp.float32
BF16 = jnp.bfloat16
NT = (((1,), (1,)), ((), ()))


def split3(value):
    high = value.astype(BF16)
    rest = value - high.astype(F32)
    mid = rest.astype(BF16)
    low = (rest - mid.astype(F32)).astype(BF16)
    return high, mid, low


def weights_kernel(ids_ref, local_ref, rows_ref, out_ref):
    width = out_ref.shape[1] // 2

    @pl.loop(0, out_ref.shape[0] // 8, unroll=4)
    def _(group):
        prec, innov = [], []
        for inside in range(8):
            entry = group * 8 + inside
            row = rows_ref[pl.ds(ids_ref[entry], 1), :]
            prec.append(local_ref[entry] * row[:, :width])
            innov.append(row[:, width:])
        scale = jnp.sqrt(jnp.concatenate(prec, axis=0))
        first = pl.multiple_of(group * 8, 8)
        out_ref[pl.ds(first, 8), :width] = scale
        out_ref[pl.ds(first, 8), width:] = scale * jnp.concatenate(innov, axis=0)


def weights(ids, local, rows):
    smem = pl.BlockSpec(memory_space=pltpu.SMEM)
    vmem = pl.BlockSpec(memory_space=pltpu.VMEM)
    return pl.pallas_call(
        weights_kernel,
        out_shape=jax.ShapeDtypeStruct((ids.shape[0], rows.shape[1]), F32),
        in_specs=[smem, smem, vmem],
        out_specs=vmem,
    )(ids, local, rows)


def pick_kernel(layout, group_size, first_region, regions, ids_ref, scale_ref, *rest):
    shard_refs, (out_ref, table_ref, sems) = rest[:-3], rest[-3:]
    width = table_ref.shape[2]
    slots = out_ref.shape[1] // regions
    copies = [
        pltpu.make_async_copy(
            shard_refs[operand], table_ref.at[start : start + size], sems.at[operand]
        )
        for operand, (start, size) in enumerate(layout)
    ]
    for copy in copies:
        copy.start()
    for copy in copies:
        copy.wait()

    for member in range(out_ref.shape[0]):

        @pl.loop(0, regions)
        def _(region):
            first = (member * group_size + first_region + region) * slots
            first = pl.multiple_of(first, slots)
            scales = scale_ref[pl.ds(first, slots), :width]
            for slot in range(slots):
                values = table_ref[ids_ref[first + slot]].astype(F32)
                out_ref[member, region * slots + slot] = (
                    values * scales[slot : slot + 1]
                ).astype(BF16)


def pick(ids, scales, shards, mem_count, group_size, first_region, regions):
    slots = ids.shape[0] // (mem_count * group_size)
    layout = []
    total = 0
    for shard in shards:
        layout.append((total, shard.shape[0]))
        total += shard.shape[0]
    row, dtype = shards[0].shape[1:], shards[0].dtype
    entries = regions * slots
    size = row[0] * row[1]
    return pl.pallas_call(
        functools.partial(pick_kernel, layout, group_size, first_region, regions),
        out_shape=jax.ShapeDtypeStruct((mem_count, entries) + row, dtype),
        in_specs=[
            pl.BlockSpec(memory_space=pltpu.SMEM),
            pl.BlockSpec(memory_space=pltpu.VMEM),
        ]
        + [pl.BlockSpec(memory_space=pl.ANY)] * len(shards),
        out_specs=pl.BlockSpec(memory_space=pltpu.VMEM),
        scratch_shapes=[
            pltpu.VMEM((total,) + row, dtype),
            pltpu.SemaphoreType.DMA((len(shards),)),
        ],
        cost_estimate=pl.CostEstimate(
            flops=mem_count * entries * size,
            bytes_accessed=4 * (mem_count * entries + total) * size,
            transcendentals=0,
        ),
        compiler_params=pltpu.CompilerParams(vmem_limit_bytes=24 << 20),
    )(ids, scales, *shards)


def grid_cycle(outer, inner):
    cells = []
    for row in range(outer):
        columns = range(1, inner) if row % 2 == 0 else range(inner - 1, 0, -1)
        cells += [row * inner + column for column in columns]
    return cells + [row * inner for row in range(outer - 1, -1, -1)]


def row_stack(rows, count):
    length = rows[0].shape[1]
    which = lax.broadcasted_iota(jnp.int32, (count, length), 0)
    stack = jnp.zeros((count, length), F32)
    for index, row in enumerate(rows):
        stack = jnp.where(which == index, row.astype(F32), stack)
    return stack.astype(BF16)


def region_setup(
    region, first, prior_ref, column_ref, weight_ref, states_ref, obs_refs, scaled_ref,
    work_ref, mean_ref,
):
    members = prior_ref.shape[1]
    sources, members_dev = states_ref.shape[0], states_ref.shape[2]
    points = states_ref.shape[3]
    slots = obs_refs[0].shape[1] // prior_ref.shape[0]
    width = obs_refs[0].shape[3]
    for slot in range(slots):
        for source in range(sources):
            start = source * members_dev
            for obs_ref in obs_refs:
                stop = start + obs_ref.shape[2]
                scaled_ref[start:stop, slot * width : (slot + 1) * width] = (
                    obs_ref[source, region * slots + slot]
                )
                start = stop
    scaled = scaled_ref[...]
    gram = lax.dot_general(scaled, scaled, NT, preferred_element_type=F32)
    prior_row = prior_ref[pl.ds(region, 1), :]
    whole = 1.0 / jnp.sum(prior_row, axis=1, keepdims=True)
    share_row = prior_row * whole
    share_col = column_ref[region] * whole
    root_row = jnp.sqrt(members * share_row)
    root_col = jnp.sqrt(members * share_col)
    average = jnp.sum(
        jnp.dot(
            row_stack(split3(share_row), 16), scaled, preferred_element_type=F32
        ),
        axis=0, keepdims=True,
    )
    own = weight_ref[pl.ds(pl.multiple_of(first + region * slots, slots), slots), width:]
    innov = jnp.concatenate([own[slot : slot + 1] for slot in range(slots)], axis=1)
    sums = lax.dot_general(
        scaled, row_stack(split3(innov) + split3(average), 16), NT,
        preferred_element_type=F32,
    )
    kind = lax.broadcasted_iota(jnp.int32, (16, 2 * LANES), 0) // 3
    side = lax.broadcasted_iota(jnp.int32, (16, 2 * LANES), 1) // LANES
    spread = jnp.where(kind == side, 1.0, 0.0).astype(BF16)
    sums = sum(
        jnp.dot(part, spread, preferred_element_type=F32) for part in split3(sums)
    )
    projection, left_col = sums[:, :LANES], sums[:, LANES:]
    total = jnp.sum(share_col * left_col, axis=0, keepdims=True)
    left_col = left_col - total
    vector = root_col * (
        projection - jnp.sum(share_col * projection, axis=0, keepdims=True)
    )
    work_ref[region, :, members + points :] = vector
    for start in range(0, members, LANES):
        tile = slice(start, start + LANES)
        part = gram[:, tile]
        left_row = jnp.sum(share_col * part, axis=0, keepdims=True)
        system = root_col * ((part - left_row) - left_col) * root_row[:, tile]
        on_diag = lax.broadcasted_iota(jnp.int32, (members, LANES), 0) == (
            lax.broadcasted_iota(jnp.int32, (members, LANES), 1) + start
        )
        work_ref[region, :, tile] = system + jnp.where(
            on_diag, (members - 1) / INFLATION, 0.0
        )
    for start in range(0, points, LANES):
        states = jnp.concatenate(
            [
                states_ref[source, region, :, start : start + LANES].astype(F32)
                for source in range(sources)
            ],
            axis=0,
        )
        mean = jnp.sum(share_col * states, axis=0, keepdims=True)
        mean_ref[region, :, start : start + LANES] = jnp.broadcast_to(mean, (8, LANES))
        work_ref[region, :, members + start : members + start + LANES] = root_col * (
            states - mean
        )


def reciprocal(value):
    guess = pl.reciprocal(value, approx=True)
    guess = guess * (2.0 - value * guess)
    return guess * (2.0 - value * guess)


def factor_diagonals(panel, chosen, work_ref):
    per_pack = LANES // PANEL
    start = panel * PANEL
    base, offset = start // LANES * LANES, start % LANES
    lane = lax.broadcasted_iota(jnp.int32, (8, LANES), 1)
    sub = lax.broadcasted_iota(jnp.int32, (8, LANES), 0)
    owner, column = lane // PANEL, lane % PANEL
    tiles = PANEL // 8
    packs = len(chosen)
    blocks = []
    for pack in chosen:
        pieces = []
        for tile in range(tiles):
            merged = None
            for place in range(per_pack):
                region = pack * per_pack + place
                raw = work_ref[
                    region, start + 8 * tile : start + 8 * tile + 8, base : base + LANES
                ]
                shift = (place * PANEL - offset) % LANES
                if shift:
                    raw = pltpu.roll(raw, shift, axis=1)
                merged = raw if merged is None else jnp.where(owner == place, raw, merged)
            pieces.append(merged)
        blocks.append(pieces)
    pivots = [[jnp.ones((8, LANES), F32) for _ in range(tiles)] for _ in range(packs)]
    for home in range(tiles):
        columns = [
            [
                {
                    tile: jnp.take_along_axis(
                        blocks[pack][tile], owner * PANEL + 8 * home + inside,
                        axis=1, mode="promise_in_bounds",
                    )
                    for tile in range(home, tiles)
                }
                for inside in range(8)
            ]
            for pack in range(packs)
        ]
        for inside in range(8):
            at_step = column == 8 * home + inside
            below = sub > inside
            for pack in range(packs):
                pieces = blocks[pack]
                pivot = columns[pack][inside][home][inside : inside + 1, :]
                inverse = reciprocal(pivot)
                row = jnp.where(at_step[:1], 1.0, pieces[home][inside : inside + 1, :])
                pivots[pack][home] = jnp.where(sub == inside, pivot, pivots[pack][home])
                later = [
                    columns[pack][other][home][inside : inside + 1, :]
                    for other in range(inside + 1, 8)
                ]
                for tile in range(home, tiles):
                    ratio = columns[pack][inside][tile] * inverse
                    cleared = at_step
                    if tile == home:
                        ratio = jnp.where(below, ratio, 0.0)
                        cleared = at_step & below
                    pieces[tile] = jnp.where(cleared, 0.0, pieces[tile]) - ratio * row
                    for other in range(inside + 1, 8):
                        columns[pack][other][tile] = (
                            columns[pack][other][tile] - ratio * later[other - inside - 1]
                        )
    results = []
    for pack in range(packs):
        rows = []
        for tile in range(tiles):
            index = sub + 8 * tile
            lower = jnp.where(
                column < index, blocks[pack][tile], jnp.where(column == index, 1.0, 0.0)
            )
            rows.append(lower * lax.rsqrt(pivots[pack][tile]))
        results.append(jnp.concatenate(rows, axis=0))
    return results


def six_products(left, right, axis):
    high, mid, low = left
    left = jnp.concatenate([high, high, mid, mid, high, low], axis=axis)
    high, mid, low = right
    right = jnp.concatenate([high, mid, high, mid, low, high], axis=0)
    return lax.dot_general(
        left, right, (((axis,), (0,)), ((), ())), preferred_element_type=F32
    )


def eliminate(panel, pack, lower, work_ref, members):
    per_pack = LANES // PANEL
    start = panel * PANEL
    after = start + PANEL
    first = after // LANES * LANES
    total = work_ref.shape[2]
    owner = lax.broadcasted_iota(jnp.int32, (PANEL, LANES), 1) // PANEL
    spread = jnp.concatenate(
        [jnp.where(owner == place, lower, 0.0) for place in range(per_pack)], axis=0
    )
    stacked = jnp.concatenate(
        [
            work_ref[pack * per_pack + place, start:after, first:]
            for place in range(per_pack)
        ],
        axis=0,
    )
    solved = six_products(split3(spread), split3(stacked), 1)
    for place in range(per_pack):
        region = pack * per_pack + place
        rows = solved[place * PANEL : (place + 1) * PANEL]
        work_ref[region, start:after, members:] = rows[:, members - first :]
        if after < members:
            parts = split3(rows)
            change = six_products(
                [part[:, : members - first] for part in parts], parts, 0
            )
            work_ref[region, after:members, first:total] = (
                work_ref[region, after:members, first:total] - change[after - first :]
            )


def analysis_kernel(offsets, first_ref, prior_ref, column_ref, weight_ref, *rest):
    count = len(offsets)
    hbm_refs = rest[:count]
    out_ref, scaled_ref, work_ref, mean_ref, sems = rest[count : count + 5]
    vmem_refs = rest[count + 5 :]
    states_ref, obs_refs = vmem_refs[0], vmem_refs[1:]
    regions, members = prior_ref.shape
    sources, members_dev = states_ref.shape[0], states_ref.shape[2]
    points = states_ref.shape[3]
    packs = regions * PANEL // LANES
    ways = scaled_ref.shape[0]
    batches = sems.shape[0]
    batch_regions = regions // batches

    def loads(batch):
        copies = []
        for index, (hbm, vmem) in enumerate(zip(hbm_refs, vmem_refs)):
            size = vmem.shape[1] // batches
            copies.append(
                pltpu.make_async_copy(
                    hbm.at[:, pl.ds(offsets[index] + batch * size, size)],
                    vmem.at[:, pl.ds(batch * size, size)],
                    sems.at[batch, index],
                )
            )
        return copies

    for batch in range(batches):
        for copy in loads(batch):
            copy.start()

    @pl.loop(0, batches)
    def _(batch):
        for copy in loads(batch):
            copy.wait()

        @pl.loop(0, batch_regions // ways)
        def _(step):
            for way in range(ways):
                region_setup(
                    batch * batch_regions + step * ways + way, first_ref[0], prior_ref,
                    column_ref, weight_ref, states_ref, obs_refs, scaled_ref.at[way],
                    work_ref, mean_ref,
                )

    halves = [range(packs // 2), range(packs // 2, packs)]
    panels = members // PANEL
    lowers = factor_diagonals(0, halves[0], work_ref)
    for panel in range(panels):
        for half in range(2):
            for pack, lower in zip(halves[half], lowers):
                eliminate(panel, pack, lower, work_ref, members)
            if panel + half < panels:
                lowers = factor_diagonals(panel + half, halves[1 - half], work_ref)

    @pl.loop(0, regions)
    def _(region):
        moved = work_ref[region, :, members : members + points]
        solved = work_ref[region, :, members + points :]
        solved = jnp.concatenate([solved] * (points // LANES), axis=1)
        shift = mean_ref[region, :1] + jnp.sum(solved * moved, axis=0, keepdims=True)
        result = (shift + jnp.sqrt(members - 1.0) * moved).astype(BF16)
        for source in range(sources):
            out_ref[source, region] = result[
                source * members_dev : (source + 1) * members_dev
            ]


def analyse(first, prior_rows, weight_rows, states, obs_parts, slots):
    regions, members = prior_rows.shape
    sources, _, members_dev, points = states[0].shape
    width = obs_parts[0][0].shape[3]
    vmem = pl.BlockSpec(memory_space=pltpu.VMEM)
    loaded = [states] + obs_parts
    sizes = [regions] + [regions * slots] * len(obs_parts)
    columns = jnp.broadcast_to(prior_rows[:, :, None], (regions, members, LANES))
    return pl.pallas_call(
        functools.partial(analysis_kernel, [offset for _, offset in loaded]),
        out_shape=jax.ShapeDtypeStruct((sources, regions, members_dev, points), BF16),
        in_specs=[pl.BlockSpec(memory_space=pltpu.SMEM), vmem, vmem, vmem]
        + [pl.BlockSpec(memory_space=pl.ANY)] * len(loaded),
        out_specs=vmem,
        scratch_shapes=[
            pltpu.VMEM((2, members, slots * width), BF16),
            pltpu.VMEM((regions, members, members + points + LANES), F32),
            pltpu.VMEM((regions, 8, points), F32),
            pltpu.SemaphoreType.DMA((regions // 2, len(loaded))),
        ]
        + [
            pltpu.VMEM(array.shape[:1] + (size,) + array.shape[2:], array.dtype)
            for (array, _), size in zip(loaded, sizes)
        ],
        cost_estimate=pl.CostEstimate(
            flops=16 * regions * members * members * (slots * width + points),
            bytes_accessed=2 * regions * members * (slots * width + 2 * points),
            transcendentals=0,
        ),
        compiler_params=pltpu.CompilerParams(vmem_limit_bytes=48 << 20),
    )(first, prior_rows, columns, weight_rows, *[array for array, _ in loaded])


def body(
    ensemble_state, obs_ens, innovation, obs_prec, block_list, block_count, loc_weight, prior_weight
):
    spaces = lax.axis_size("space")
    mem_count = lax.axis_size("mem")
    members_dev, regions_dev, points = ensemble_state.shape
    blocks_dev, width = obs_ens.shape[1:]
    group_size = regions_dev // mem_count
    slots = block_list.shape[1]
    piece = members_dev // CHUNKS
    part = group_size // SPLIT
    first_row = lax.axis_index("mem") * group_size

    inner = 2 ** ((spaces.bit_length() - 1) // 2)
    cycle = grid_cycle(spaces // inner, inner)
    forward = [(cycle[k], cycle[(k + 1) % spaces]) for k in range(spaces)]
    backward = [(to, start) for start, to in forward]
    position = [cycle.index(space) for space in range(spaces)]
    half_way = spaces // 2

    def place_of(space):
        return sum(
            jnp.where(space == index, position[index], 0) for index in range(spaces)
        )

    all_ids = block_list.reshape(regions_dev * slots)
    behind = place_of(lax.axis_index("space")) - place_of(all_ids // blocks_dev)
    places = (behind + spaces) % spaces * blocks_dev + all_ids % blocks_dev
    active = jnp.arange(slots, dtype=jnp.int32)[None, :] < block_count[:, None]
    local = jnp.where(active, loc_weight, 0.0).reshape(regions_dev * slots)
    rows = jnp.concatenate([obs_prec, innovation], axis=1)
    rows = lax.all_to_all(
        jnp.broadcast_to(rows, (spaces,) + rows.shape), "space",
        split_axis=0, concat_axis=0, tiled=True,
    ).reshape(spaces * blocks_dev, 2 * width)
    by_region = jnp.transpose(ensemble_state, (1, 0, 2)).reshape(
        mem_count, group_size, members_dev, points
    )
    by_block = jnp.transpose(
        obs_ens.reshape(CHUNKS, piece, blocks_dev, width), (0, 2, 1, 3)
    )

    def ring_step(step, ahead, back):
        if step < half_way - 1:
            return lax.ppermute(ahead, "space", forward), lax.ppermute(
                back, "space", backward
            )
        middle = blocks_dev // 2
        return (
            lax.ppermute(ahead[:middle], "space", forward),
            lax.ppermute(back[middle:], "space", backward),
        )

    def exchange(picked):
        return lax.all_to_all(picked, "mem", split_axis=0, concat_axis=0, tiled=True)

    waiting = [by_block[chunk] for chunk in range(CHUNKS)]
    running = []
    obs_parts = [[] for _ in range(SPLIT)]
    stage = 0
    while waiting or running:
        if waiting and (not running or running[-1]["step"] == half_way - 1):
            own = waiting.pop(0)
            running.append({"step": 0, "ahead": [own], "back": [own]})
        moved = [
            ring_step(ring["step"], ring["ahead"][-1], ring["back"][-1])
            for ring in running
        ]
        tied = {"moved": moved, "waiting": waiting}
        if stage == 0:
            tied["rows"], tied["by_region"] = rows, by_region
        if stage == half_way - 1:
            tied["states"] = states
        tied = lax.optimization_barrier(tied)
        waiting = tied["waiting"]
        for ring, (ahead, back) in zip(running, tied["moved"]):
            ring["ahead"].append(ahead)
            ring["back"].append(back)
            ring["step"] += 1
        if stage == 0:
            weight_rows = weights(
                all_ids, local, tied["rows"]
            )
            states = exchange(tied["by_region"])
        if stage == half_way - 1:
            states = tied["states"]
        if running[0]["step"] == half_way:
            ring = running.pop(0)
            shards = ring["ahead"] + ring["back"][:0:-1]
            last = not (waiting or running)
            if last:
                for index in range(SPLIT):
                    picked = pick(
                        places, weight_rows, shards, mem_count, group_size,
                        index * part, part,
                    )
                    obs_parts[index].append((exchange(picked), 0))
            else:
                picked = exchange(
                    pick(
                        places, weight_rows, shards, mem_count, group_size, 0, group_size
                    )
                )
                for index in range(SPLIT):
                    obs_parts[index].append((picked, index * part * slots))
        stage += 1

    results = []
    for index in range(SPLIT):
        start = first_row + index * part
        result = analyse(
            (start * slots).reshape(1),
            lax.dynamic_slice_in_dim(prior_weight, start, part, 0),
            weight_rows,
            (states, index * part),
            obs_parts[index],
            slots,
        )
        results.append(exchange(result))
    back = jnp.concatenate(results, axis=1)
    return jnp.transpose(back.reshape(regions_dev, members_dev, points), (1, 0, 2))


def solution(mesh):
    return jax.shard_map(
        body,
        mesh=mesh,
        in_specs=(
            P("mem", "space", None),
            P("mem", "space", None),
            P("space", None),
            P("space", None),
            P("space", None),
            P("space"),
            P("space", None),
            P("space", None),
        ),
        out_specs=P("mem", "space", None),
        check_vma=False,
    )
```

```python
import functools

import jax
import jax.numpy as jnp
from jax import lax
from jax.experimental import pallas as pl
from jax.experimental.pallas import tpu as pltpu
from jax.sharding import PartitionSpec as P

INFLATION = 1.1
PANEL = 32
LANES = 128
CHUNKS = (4, 4, 2)
SPLIT = 2
F32 = jnp.float32
BF16 = jnp.bfloat16
NT = (((1,), (1,)), ((), ()))


def split3(value):
    high = value.astype(BF16)
    rest = value - high.astype(F32)
    mid = rest.astype(BF16)
    low = (rest - mid.astype(F32)).astype(BF16)
    return high, mid, low


def weights_kernel(ids_ref, local_ref, rows_ref, out_ref):
    width = out_ref.shape[1] // 2

    @pl.loop(0, out_ref.shape[0] // 8, unroll=4)
    def _(group):
        prec, innov = [], []
        for inside in range(8):
            entry = group * 8 + inside
            row = rows_ref[pl.ds(ids_ref[entry], 1), :]
            prec.append(local_ref[entry] * row[:, :width])
            innov.append(row[:, width:])
        scale = jnp.sqrt(jnp.concatenate(prec, axis=0))
        first = pl.multiple_of(group * 8, 8)
        out_ref[pl.ds(first, 8), :width] = scale
        out_ref[pl.ds(first, 8), width:] = scale * jnp.concatenate(innov, axis=0)


def weights(ids, local, rows):
    smem = pl.BlockSpec(memory_space=pltpu.SMEM)
    vmem = pl.BlockSpec(memory_space=pltpu.VMEM)
    return pl.pallas_call(
        weights_kernel,
        out_shape=jax.ShapeDtypeStruct((ids.shape[0], rows.shape[1]), F32),
        in_specs=[smem, smem, vmem],
        out_specs=vmem,
    )(ids, local, rows)


def pick_kernel(layout, group_size, first_region, regions, ids_ref, scale_ref, *rest):
    shard_refs, (out_ref, table_ref, sems) = rest[:-3], rest[-3:]
    width = table_ref.shape[2]
    slots = out_ref.shape[1] // regions
    copies = [
        pltpu.make_async_copy(
            shard_refs[operand], table_ref.at[start : start + size], sems.at[operand]
        )
        for operand, (start, size) in enumerate(layout)
    ]
    for copy in copies:
        copy.start()
    for copy in copies:
        copy.wait()

    for member in range(out_ref.shape[0]):

        @pl.loop(0, regions)
        def _(region):
            first = (member * group_size + first_region + region) * slots
            first = pl.multiple_of(first, slots)
            scales = scale_ref[pl.ds(first, slots), :width]
            for slot in range(slots):
                values = table_ref[ids_ref[first + slot]].astype(F32)
                out_ref[member, region * slots + slot] = (
                    values * scales[slot : slot + 1]
                ).astype(BF16)


def pick(ids, scales, shards, mem_count, group_size, first_region, regions):
    slots = ids.shape[0] // (mem_count * group_size)
    layout = []
    total = 0
    for shard in shards:
        layout.append((total, shard.shape[0]))
        total += shard.shape[0]
    row, dtype = shards[0].shape[1:], shards[0].dtype
    entries = regions * slots
    size = row[0] * row[1]
    return pl.pallas_call(
        functools.partial(pick_kernel, layout, group_size, first_region, regions),
        out_shape=jax.ShapeDtypeStruct((mem_count, entries) + row, dtype),
        in_specs=[
            pl.BlockSpec(memory_space=pltpu.SMEM),
            pl.BlockSpec(memory_space=pltpu.VMEM),
        ]
        + [pl.BlockSpec(memory_space=pl.ANY)] * len(shards),
        out_specs=pl.BlockSpec(memory_space=pltpu.VMEM),
        scratch_shapes=[
            pltpu.VMEM((total,) + row, dtype),
            pltpu.SemaphoreType.DMA((len(shards),)),
        ],
        cost_estimate=pl.CostEstimate(
            flops=mem_count * entries * size,
            bytes_accessed=4 * (mem_count * entries + total) * size,
            transcendentals=0,
        ),
        compiler_params=pltpu.CompilerParams(vmem_limit_bytes=24 << 20),
    )(ids, scales, *shards)


def grid_cycle(outer, inner):
    cells = []
    for row in range(outer):
        columns = range(1, inner) if row % 2 == 0 else range(inner - 1, 0, -1)
        cells += [row * inner + column for column in columns]
    return cells + [row * inner for row in range(outer - 1, -1, -1)]


def row_stack(rows, count):
    length = rows[0].shape[1]
    which = lax.broadcasted_iota(jnp.int32, (count, length), 0)
    stack = jnp.zeros((count, length), F32)
    for index, row in enumerate(rows):
        stack = jnp.where(which == index, row.astype(F32), stack)
    return stack.astype(BF16)


def region_setup(
    region, first, prior_ref, column_ref, weight_ref, states_ref, obs_refs, scaled_ref,
    work_ref, mean_ref,
):
    members = prior_ref.shape[1]
    sources, members_dev = states_ref.shape[0], states_ref.shape[2]
    points = states_ref.shape[3]
    slots = obs_refs[0].shape[1] // prior_ref.shape[0]
    width = obs_refs[0].shape[3]
    for slot in range(slots):
        for source in range(sources):
            start = source * members_dev
            for obs_ref in obs_refs:
                stop = start + obs_ref.shape[2]
                scaled_ref[start:stop, slot * width : (slot + 1) * width] = (
                    obs_ref[source, region * slots + slot]
                )
                start = stop
    scaled = scaled_ref[...]
    gram = lax.dot_general(scaled, scaled, NT, preferred_element_type=F32)
    prior_row = prior_ref[pl.ds(region, 1), :]
    whole = 1.0 / jnp.sum(prior_row, axis=1, keepdims=True)
    share_row = prior_row * whole
    share_col = column_ref[region] * whole
    root_row = jnp.sqrt(members * share_row)
    root_col = jnp.sqrt(members * share_col)
    average = jnp.sum(
        jnp.dot(
            row_stack(split3(share_row), 16), scaled, preferred_element_type=F32
        ),
        axis=0, keepdims=True,
    )
    own = weight_ref[pl.ds(pl.multiple_of(first + region * slots, slots), slots), width:]
    innov = jnp.concatenate([own[slot : slot + 1] for slot in range(slots)], axis=1)
    sums = lax.dot_general(
        scaled, row_stack(split3(innov) + split3(average), 16), NT,
        preferred_element_type=F32,
    )
    kind = lax.broadcasted_iota(jnp.int32, (16, 2 * LANES), 0) // 3
    side = lax.broadcasted_iota(jnp.int32, (16, 2 * LANES), 1) // LANES
    spread = jnp.where(kind == side, 1.0, 0.0).astype(BF16)
    sums = sum(
        jnp.dot(part, spread, preferred_element_type=F32) for part in split3(sums)
    )
    projection, left_col = sums[:, :LANES], sums[:, LANES:]
    total = jnp.sum(share_col * left_col, axis=0, keepdims=True)
    left_col = left_col - total
    vector = root_col * (
        projection - jnp.sum(share_col * projection, axis=0, keepdims=True)
    )
    work_ref[region, :, members + points :] = vector
    for start in range(0, members, LANES):
        tile = slice(start, start + LANES)
        part = gram[:, tile]
        left_row = jnp.sum(share_col * part, axis=0, keepdims=True)
        system = root_col * ((part - left_row) - left_col) * root_row[:, tile]
        on_diag = lax.broadcasted_iota(jnp.int32, (members, LANES), 0) == (
            lax.broadcasted_iota(jnp.int32, (members, LANES), 1) + start
        )
        work_ref[region, :, tile] = system + jnp.where(
            on_diag, (members - 1) / INFLATION, 0.0
        )
    for start in range(0, points, LANES):
        states = jnp.concatenate(
            [
                states_ref[source, region, :, start : start + LANES].astype(F32)
                for source in range(sources)
            ],
            axis=0,
        )
        mean = jnp.sum(share_col * states, axis=0, keepdims=True)
        mean_ref[region, :, start : start + LANES] = jnp.broadcast_to(mean, (8, LANES))
        work_ref[region, :, members + start : members + start + LANES] = root_col * (
            states - mean
        )


def reciprocal(value):
    guess = pl.reciprocal(value, approx=True)
    guess = guess * (2.0 - value * guess)
    return guess * (2.0 - value * guess)


def factor_diagonals(panel, chosen, work_ref):
    per_pack = LANES // PANEL
    start = panel * PANEL
    base, offset = start // LANES * LANES, start % LANES
    lane = lax.broadcasted_iota(jnp.int32, (8, LANES), 1)
    sub = lax.broadcasted_iota(jnp.int32, (8, LANES), 0)
    owner, column = lane // PANEL, lane % PANEL
    tiles = PANEL // 8
    packs = len(chosen)
    blocks = []
    for pack in chosen:
        pieces = []
        for tile in range(tiles):
            merged = None
            for place in range(per_pack):
                region = pack * per_pack + place
                raw = work_ref[
                    region, start + 8 * tile : start + 8 * tile + 8, base : base + LANES
                ]
                shift = (place * PANEL - offset) % LANES
                if shift:
                    raw = pltpu.roll(raw, shift, axis=1)
                merged = raw if merged is None else jnp.where(owner == place, raw, merged)
            pieces.append(merged)
        blocks.append(pieces)
    pivots = [[jnp.ones((8, LANES), F32) for _ in range(tiles)] for _ in range(packs)]
    for home in range(tiles):
        columns = [
            [
                {
                    tile: jnp.take_along_axis(
                        blocks[pack][tile], owner * PANEL + 8 * home + inside,
                        axis=1, mode="promise_in_bounds",
                    )
                    for tile in range(home, tiles)
                }
                for inside in range(8)
            ]
            for pack in range(packs)
        ]
        for inside in range(8):
            at_step = column == 8 * home + inside
            below = sub > inside
            for pack in range(packs):
                pieces = blocks[pack]
                pivot = columns[pack][inside][home][inside : inside + 1, :]
                inverse = reciprocal(pivot)
                row = jnp.where(at_step[:1], 1.0, pieces[home][inside : inside + 1, :])
                pivots[pack][home] = jnp.where(sub == inside, pivot, pivots[pack][home])
                later = [
                    columns[pack][other][home][inside : inside + 1, :]
                    for other in range(inside + 1, 8)
                ]
                for tile in range(home, tiles):
                    ratio = columns[pack][inside][tile] * inverse
                    cleared = at_step
                    if tile == home:
                        ratio = jnp.where(below, ratio, 0.0)
                        cleared = at_step & below
                    pieces[tile] = jnp.where(cleared, 0.0, pieces[tile]) - ratio * row
                    for other in range(inside + 1, 8):
                        columns[pack][other][tile] = (
                            columns[pack][other][tile] - ratio * later[other - inside - 1]
                        )
    results = []
    for pack in range(packs):
        rows = []
        for tile in range(tiles):
            index = sub + 8 * tile
            lower = jnp.where(
                column < index, blocks[pack][tile], jnp.where(column == index, 1.0, 0.0)
            )
            rows.append(lower * lax.rsqrt(pivots[pack][tile]))
        results.append(jnp.concatenate(rows, axis=0))
    return results


def six_products(left, right, axis):
    high, mid, low = left
    left = jnp.concatenate([high, high, mid, mid, high, low], axis=axis)
    high, mid, low = right
    right = jnp.concatenate([high, mid, high, mid, low, high], axis=0)
    return lax.dot_general(
        left, right, (((axis,), (0,)), ((), ())), preferred_element_type=F32
    )


def eliminate(panel, pack, lower, work_ref, members):
    per_pack = LANES // PANEL
    start = panel * PANEL
    after = start + PANEL
    first = after // LANES * LANES
    total = work_ref.shape[2]
    owner = lax.broadcasted_iota(jnp.int32, (PANEL, LANES), 1) // PANEL
    spread = jnp.concatenate(
        [jnp.where(owner == place, lower, 0.0) for place in range(per_pack)], axis=0
    )
    stacked = jnp.concatenate(
        [
            work_ref[pack * per_pack + place, start:after, first:]
            for place in range(per_pack)
        ],
        axis=0,
    )
    solved = six_products(split3(spread), split3(stacked), 1)
    for place in range(per_pack):
        region = pack * per_pack + place
        rows = solved[place * PANEL : (place + 1) * PANEL]
        work_ref[region, start:after, members:] = rows[:, members - first :]
        if after < members:
            parts = split3(rows)
            change = six_products(
                [part[:, : members - first] for part in parts], parts, 0
            )
            work_ref[region, after:members, first:total] = (
                work_ref[region, after:members, first:total] - change[after - first :]
            )


def analysis_kernel(offsets, first_ref, prior_ref, column_ref, weight_ref, *rest):
    count = len(offsets)
    hbm_refs = rest[:count]
    out_ref, scaled_ref, work_ref, mean_ref, sems = rest[count : count + 5]
    vmem_refs = rest[count + 5 :]
    states_ref, obs_refs = vmem_refs[0], vmem_refs[1:]
    regions, members = prior_ref.shape
    sources, members_dev = states_ref.shape[0], states_ref.shape[2]
    points = states_ref.shape[3]
    packs = regions * PANEL // LANES
    ways = scaled_ref.shape[0]
    batches = sems.shape[0]
    batch_regions = regions // batches

    def loads(batch):
        copies = []
        for index, (hbm, vmem) in enumerate(zip(hbm_refs, vmem_refs)):
            size = vmem.shape[1] // batches
            copies.append(
                pltpu.make_async_copy(
                    hbm.at[:, pl.ds(offsets[index] + batch * size, size)],
                    vmem.at[:, pl.ds(batch * size, size)],
                    sems.at[batch, index],
                )
            )
        return copies

    for batch in range(batches):
        for copy in loads(batch):
            copy.start()

    @pl.loop(0, batches)
    def _(batch):
        for copy in loads(batch):
            copy.wait()

        @pl.loop(0, batch_regions // ways)
        def _(step):
            for way in range(ways):
                region_setup(
                    batch * batch_regions + step * ways + way, first_ref[0], prior_ref,
                    column_ref, weight_ref, states_ref, obs_refs, scaled_ref.at[way],
                    work_ref, mean_ref,
                )

    for panel in range(members // PANEL):
        lowers = factor_diagonals(panel, range(packs), work_ref)
        for pack in range(packs):
            eliminate(panel, pack, lowers[pack], work_ref, members)

    @pl.loop(0, regions)
    def _(region):
        moved = work_ref[region, :, members : members + points]
        solved = work_ref[region, :, members + points :]
        solved = jnp.concatenate([solved] * (points // LANES), axis=1)
        shift = mean_ref[region, :1] + jnp.sum(solved * moved, axis=0, keepdims=True)
        result = (shift + jnp.sqrt(members - 1.0) * moved).astype(BF16)
        for source in range(sources):
            out_ref[source, region] = result[
                source * members_dev : (source + 1) * members_dev
            ]


def analyse(first, prior_rows, weight_rows, states, obs_parts, slots):
    regions, members = prior_rows.shape
    sources, _, members_dev, points = states[0].shape
    width = obs_parts[0][0].shape[3]
    vmem = pl.BlockSpec(memory_space=pltpu.VMEM)
    loaded = [states] + obs_parts
    sizes = [regions] + [regions * slots] * len(obs_parts)
    columns = jnp.broadcast_to(prior_rows[:, :, None], (regions, members, LANES))
    return pl.pallas_call(
        functools.partial(analysis_kernel, [offset for _, offset in loaded]),
        out_shape=jax.ShapeDtypeStruct((sources, regions, members_dev, points), BF16),
        in_specs=[pl.BlockSpec(memory_space=pltpu.SMEM), vmem, vmem, vmem]
        + [pl.BlockSpec(memory_space=pl.ANY)] * len(loaded),
        out_specs=vmem,
        scratch_shapes=[
            pltpu.VMEM((2, members, slots * width), BF16),
            pltpu.VMEM((regions, members, members + points + LANES), F32),
            pltpu.VMEM((regions, 8, points), F32),
            pltpu.SemaphoreType.DMA((regions // 2, len(loaded))),
        ]
        + [
            pltpu.VMEM(array.shape[:1] + (size,) + array.shape[2:], array.dtype)
            for (array, _), size in zip(loaded, sizes)
        ],
        cost_estimate=pl.CostEstimate(
            flops=16 * regions * members * members * (slots * width + points),
            bytes_accessed=2 * regions * members * (slots * width + 2 * points),
            transcendentals=0,
        ),
        compiler_params=pltpu.CompilerParams(vmem_limit_bytes=48 << 20),
    )(first, prior_rows, columns, weight_rows, *[array for array, _ in loaded])


def body(
    ensemble_state, obs_ens, innovation, obs_prec, block_list, block_count, loc_weight, prior_weight
):
    spaces = lax.axis_size("space")
    mem_count = lax.axis_size("mem")
    members_dev, regions_dev, points = ensemble_state.shape
    blocks_dev, width = obs_ens.shape[1:]
    group_size = regions_dev // mem_count
    slots = block_list.shape[1]
    part = group_size // SPLIT
    first_row = lax.axis_index("mem") * group_size

    inner = 2 ** ((spaces.bit_length() - 1) // 2)
    cycle = grid_cycle(spaces // inner, inner)
    forward = [(cycle[k], cycle[(k + 1) % spaces]) for k in range(spaces)]
    backward = [(to, start) for start, to in forward]
    position = [cycle.index(space) for space in range(spaces)]
    half_way = spaces // 2

    def place_of(space):
        return sum(
            jnp.where(space == index, position[index], 0) for index in range(spaces)
        )

    all_ids = block_list.reshape(regions_dev * slots)
    behind = place_of(lax.axis_index("space")) - place_of(all_ids // blocks_dev)
    places = (behind + spaces) % spaces * blocks_dev + all_ids % blocks_dev
    active = jnp.arange(slots, dtype=jnp.int32)[None, :] < block_count[:, None]
    local = jnp.where(active, loc_weight, 0.0).reshape(regions_dev * slots)
    waiting = []
    start = 0
    for share in CHUNKS:
        stop = start + members_dev // share
        waiting.append(jnp.transpose(obs_ens[start:stop], (1, 0, 2)))
        start = stop
    rows = jnp.concatenate([obs_prec, innovation], axis=1)
    rows = jnp.broadcast_to(rows, (spaces,) + rows.shape)
    waiting[0], rows, ensemble_state = lax.optimization_barrier(
        (waiting[0], rows, ensemble_state)
    )
    rows = lax.all_to_all(rows, "space", split_axis=0, concat_axis=0, tiled=True)
    by_region = jnp.transpose(ensemble_state, (1, 0, 2)).reshape(
        mem_count, group_size, members_dev, points
    )

    def ring_step(step, ahead, back):
        if step < half_way - 1:
            return lax.ppermute(ahead, "space", forward), lax.ppermute(
                back, "space", backward
            )
        middle = blocks_dev // 2
        return (
            lax.ppermute(ahead[:middle], "space", forward),
            lax.ppermute(back[middle:], "space", backward),
        )

    def exchange(picked):
        return lax.all_to_all(picked, "mem", split_axis=0, concat_axis=0, tiled=True)

    by_region, rows = lax.optimization_barrier((by_region, rows))
    latest = states = exchange(by_region)
    running = []
    obs_parts = [[] for _ in range(SPLIT)]
    stage = 0
    ties = {half_way - 1: [states]}
    while waiting or running:
        if waiting and (not running or running[-1]["step"] == half_way - 1):
            own = waiting.pop(0)
            running.append({"step": 0, "ahead": [own], "back": [own]})
        moved = [
            ring_step(ring["step"], ring["ahead"][-1], ring["back"][-1])
            for ring in running
        ]
        tied = {"moved": moved, "waiting": waiting, "ties": ties.pop(stage, [])}
        if stage == 1:
            tied["rows"] = rows
        tied = lax.optimization_barrier(tied)
        waiting = tied["waiting"]
        for ring, (ahead, back) in zip(running, tied["moved"]):
            ring["ahead"].append(ahead)
            ring["back"].append(back)
            ring["step"] += 1
        if stage == 1:
            weight_rows = weights(
                all_ids, local, tied["rows"].reshape(spaces * blocks_dev, 2 * width)
            )
            ties.setdefault(stage + 1, []).append(weight_rows)
        if running[0]["step"] == half_way:
            ring = running.pop(0)
            shards = ring["ahead"] + ring["back"][:0:-1]
            if waiting or running:
                picked = pick(
                    places, weight_rows, shards, mem_count, group_size, 0, group_size
                )
                ties.setdefault(stage + 1, []).append(picked)
                picked, _ = lax.optimization_barrier((picked, latest))
                latest = exchange(picked)
                ties.setdefault(stage + half_way - 1, []).append(latest)
                for index in range(SPLIT):
                    obs_parts[index].append((latest, index * part * slots))
            else:
                for index in range(SPLIT):
                    picked = pick(
                        places, weight_rows, shards, mem_count, group_size,
                        index * part, part,
                    )
                    picked, _ = lax.optimization_barrier((picked, latest))
                    latest = exchange(picked)
                    obs_parts[index].append((latest, 0))
        stage += 1

    results = []
    for index in range(SPLIT):
        start = first_row + index * part
        result = analyse(
            (start * slots).reshape(1),
            lax.dynamic_slice_in_dim(prior_weight, start, part, 0),
            weight_rows,
            (states, index * part),
            obs_parts[index],
            slots,
        )
        results.append(exchange(result))
    back = jnp.concatenate(results, axis=1)
    return jnp.transpose(back.reshape(regions_dev, members_dev, points), (1, 0, 2))


def solution(mesh):
    return jax.shard_map(
        body,
        mesh=mesh,
        in_specs=(
            P("mem", "space", None),
            P("mem", "space", None),
            P("space", None),
            P("space", None),
            P("space", None),
            P("space"),
            P("space", None),
            P("space", None),
        ),
        out_specs=P("mem", "space", None),
        check_vma=False,
    )
```

```python
import functools

import jax
import jax.numpy as jnp
from jax import lax
from jax.experimental import pallas as pl
from jax.experimental.pallas import tpu as pltpu
from jax.sharding import PartitionSpec as P

INFLATION = 1.1
PANEL = 32
GROUP = 4
LANES = 128
CHUNKS = (4, 4, 2)
SPLIT = 2
F32 = jnp.float32
BF16 = jnp.bfloat16
NT = (((1,), (1,)), ((), ()))


def split3(value):
    high = value.astype(BF16)
    rest = value - high.astype(F32)
    mid = rest.astype(BF16)
    low = (rest - mid.astype(F32)).astype(BF16)
    return high, mid, low


def weights_kernel(ids_ref, local_ref, *rest):
    part_refs, (out_ref, rows_ref) = rest[:-2], rest[-2:]
    width = out_ref.shape[1] // 2
    size = part_refs[0].shape[0]
    for index, part_ref in enumerate(part_refs):
        rows_ref[index * size : (index + 1) * size] = part_ref[...]

    @pl.loop(0, out_ref.shape[0] // 8, unroll=4)
    def _(group):
        prec, innov = [], []
        for inside in range(8):
            entry = group * 8 + inside
            row = rows_ref[pl.ds(ids_ref[entry], 1), :]
            prec.append(local_ref[entry] * row[:, :width])
            innov.append(row[:, width:])
        scale = jnp.sqrt(jnp.concatenate(prec, axis=0))
        first = pl.multiple_of(group * 8, 8)
        out_ref[pl.ds(first, 8), :width] = scale
        out_ref[pl.ds(first, 8), width:] = scale * jnp.concatenate(innov, axis=0)


def weights(ids, local, parts):
    smem = pl.BlockSpec(memory_space=pltpu.SMEM)
    vmem = pl.BlockSpec(memory_space=pltpu.VMEM)
    size, length = parts[0].shape
    return pl.pallas_call(
        weights_kernel,
        out_shape=jax.ShapeDtypeStruct((ids.shape[0], length), F32),
        in_specs=[smem, smem] + [vmem] * len(parts),
        out_specs=vmem,
        scratch_shapes=[pltpu.VMEM((len(parts) * size, length), F32)],
    )(ids, local, *parts)


def pick_kernel(layout, group_size, first_region, regions, ids_ref, scale_ref, *rest):
    shard_refs, (out_ref, table_ref, sems) = rest[:-3], rest[-3:]
    width = table_ref.shape[2]
    slots = out_ref.shape[1] // regions
    copies = [
        pltpu.make_async_copy(
            shard_refs[operand], table_ref.at[start : start + size], sems.at[operand]
        )
        for operand, (start, size) in enumerate(layout)
    ]
    for copy in copies:
        copy.start()
    for copy in copies:
        copy.wait()

    for member in range(out_ref.shape[0]):

        @pl.loop(0, regions)
        def _(region):
            first = (member * group_size + first_region + region) * slots
            first = pl.multiple_of(first, slots)
            scales = scale_ref[pl.ds(first, slots), :width]
            for slot in range(slots):
                values = table_ref[ids_ref[first + slot]].astype(F32)
                out_ref[member, region * slots + slot] = (
                    values * scales[slot : slot + 1]
                ).astype(BF16)


def pick(ids, scales, shards, mem_count, group_size, first_region, regions):
    slots = ids.shape[0] // (mem_count * group_size)
    layout = []
    total = 0
    for shard in shards:
        layout.append((total, shard.shape[0]))
        total += shard.shape[0]
    row, dtype = shards[0].shape[1:], shards[0].dtype
    entries = regions * slots
    size = row[0] * row[1]
    return pl.pallas_call(
        functools.partial(pick_kernel, layout, group_size, first_region, regions),
        out_shape=jax.ShapeDtypeStruct((mem_count, entries) + row, dtype),
        in_specs=[
            pl.BlockSpec(memory_space=pltpu.SMEM),
            pl.BlockSpec(memory_space=pltpu.VMEM),
        ]
        + [pl.BlockSpec(memory_space=pl.ANY)] * len(shards),
        out_specs=pl.BlockSpec(memory_space=pltpu.VMEM),
        scratch_shapes=[
            pltpu.VMEM((total,) + row, dtype),
            pltpu.SemaphoreType.DMA((len(shards),)),
        ],
        cost_estimate=pl.CostEstimate(
            flops=mem_count * entries * size,
            bytes_accessed=4 * (mem_count * entries + total) * size,
            transcendentals=0,
        ),
        compiler_params=pltpu.CompilerParams(vmem_limit_bytes=24 << 20),
    )(ids, scales, *shards)


def grid_cycle(outer, inner):
    cells = []
    for row in range(outer):
        columns = range(1, inner) if row % 2 == 0 else range(inner - 1, 0, -1)
        cells += [row * inner + column for column in columns]
    return cells + [row * inner for row in range(outer - 1, -1, -1)]


def row_stack(rows, count):
    length = rows[0].shape[1]
    which = lax.broadcasted_iota(jnp.int32, (count, length), 0)
    stack = jnp.zeros((count, length), F32)
    for index, row in enumerate(rows):
        stack = jnp.where(which == index, row.astype(F32), stack)
    return stack.astype(BF16)


def region_setup(
    region, first, prior_ref, column_ref, weight_ref, states_ref, obs_refs, scaled_ref,
    work_ref, mean_ref,
):
    members = prior_ref.shape[1]
    sources, members_dev = states_ref.shape[0], states_ref.shape[2]
    points = states_ref.shape[3]
    slots = obs_refs[0].shape[1] // prior_ref.shape[0]
    width = obs_refs[0].shape[3]
    for slot in range(slots):
        for source in range(sources):
            start = source * members_dev
            for obs_ref in obs_refs:
                stop = start + obs_ref.shape[2]
                scaled_ref[start:stop, slot * width : (slot + 1) * width] = (
                    obs_ref[source, region * slots + slot]
                )
                start = stop
    scaled = scaled_ref[...]
    gram = lax.dot_general(scaled, scaled, NT, preferred_element_type=F32)
    prior_row = prior_ref[pl.ds(region, 1), :]
    whole = 1.0 / jnp.sum(prior_row, axis=1, keepdims=True)
    share_row = prior_row * whole
    share_col = column_ref[region] * whole
    root_row = jnp.sqrt(members * share_row)
    root_col = jnp.sqrt(members * share_col)
    average = jnp.sum(
        jnp.dot(
            row_stack(split3(share_row), 16), scaled, preferred_element_type=F32
        ),
        axis=0, keepdims=True,
    )
    own = weight_ref[pl.ds(pl.multiple_of(first + region * slots, slots), slots), width:]
    innov = jnp.concatenate([own[slot : slot + 1] for slot in range(slots)], axis=1)
    sums = lax.dot_general(
        scaled, row_stack(split3(innov) + split3(average), 16), NT,
        preferred_element_type=F32,
    )
    kind = lax.broadcasted_iota(jnp.int32, (16, 2 * LANES), 0) // 3
    side = lax.broadcasted_iota(jnp.int32, (16, 2 * LANES), 1) // LANES
    spread = jnp.where(kind == side, 1.0, 0.0).astype(BF16)
    sums = sum(
        jnp.dot(part, spread, preferred_element_type=F32) for part in split3(sums)
    )
    projection, left_col = sums[:, :LANES], sums[:, LANES:]
    total = jnp.sum(share_col * left_col, axis=0, keepdims=True)
    left_col = left_col - total
    vector = root_col * (
        projection - jnp.sum(share_col * projection, axis=0, keepdims=True)
    )
    work_ref[region, :, members + points :] = vector
    for start in range(0, members, LANES):
        tile = slice(start, start + LANES)
        part = gram[:, tile]
        left_row = jnp.sum(share_col * part, axis=0, keepdims=True)
        system = root_col * ((part - left_row) - left_col) * root_row[:, tile]
        on_diag = lax.broadcasted_iota(jnp.int32, (members, LANES), 0) == (
            lax.broadcasted_iota(jnp.int32, (members, LANES), 1) + start
        )
        work_ref[region, :, tile] = system + jnp.where(
            on_diag, (members - 1) / INFLATION, 0.0
        )
    for start in range(0, points, LANES):
        states = jnp.concatenate(
            [
                states_ref[source, region, :, start : start + LANES].astype(F32)
                for source in range(sources)
            ],
            axis=0,
        )
        mean = jnp.sum(share_col * states, axis=0, keepdims=True)
        mean_ref[region, :, start : start + LANES] = jnp.broadcast_to(mean, (8, LANES))
        work_ref[region, :, members + start : members + start + LANES] = root_col * (
            states - mean
        )


def reciprocal(value):
    guess = pl.reciprocal(value, approx=True)
    guess = guess * (2.0 - value * guess)
    return guess * (2.0 - value * guess)


def factor_diagonals(panel, chosen, work_ref):
    per_pack = LANES // PANEL
    start = panel * PANEL
    base, offset = start // LANES * LANES, start % LANES
    lane = lax.broadcasted_iota(jnp.int32, (8, LANES), 1)
    sub = lax.broadcasted_iota(jnp.int32, (8, LANES), 0)
    owner, column = lane // PANEL, lane % PANEL
    tiles = PANEL // 8
    packs = len(chosen)
    blocks = []
    for pack in chosen:
        pieces = []
        for tile in range(tiles):
            merged = None
            for place in range(per_pack):
                region = pack * per_pack + place
                raw = work_ref[
                    region, start + 8 * tile : start + 8 * tile + 8, base : base + LANES
                ]
                shift = (place * PANEL - offset) % LANES
                if shift:
                    raw = pltpu.roll(raw, shift, axis=1)
                merged = raw if merged is None else jnp.where(owner == place, raw, merged)
            pieces.append(merged)
        blocks.append(pieces)
    pivots = [[jnp.ones((8, LANES), F32) for _ in range(tiles)] for _ in range(packs)]
    for first in range(0, PANEL, GROUP):
        home = first // 8
        columns = [
            [
                {
                    tile: jnp.take_along_axis(
                        blocks[pack][tile], owner * PANEL + first + step,
                        axis=1, mode="promise_in_bounds",
                    )
                    for tile in range(home, tiles)
                }
                for step in range(GROUP)
            ]
            for pack in range(packs)
        ]
        for step in range(GROUP):
            inside = first % 8 + step
            at_step = column == first + step
            below = sub > inside
            for pack in range(packs):
                pieces = blocks[pack]
                pivot = columns[pack][step][home][inside : inside + 1, :]
                inverse = reciprocal(pivot)
                row = jnp.where(at_step[:1], 1.0, pieces[home][inside : inside + 1, :])
                pivots[pack][home] = jnp.where(sub == inside, pivot, pivots[pack][home])
                later = {
                    other: columns[pack][other][home][inside : inside + 1, :]
                    for other in range(step + 1, GROUP)
                }
                for tile in range(home, tiles):
                    ratio = columns[pack][step][tile] * inverse
                    cleared = at_step
                    if tile == home:
                        ratio = jnp.where(below, ratio, 0.0)
                        cleared = at_step & below
                    for other in later:
                        columns[pack][other][tile] = (
                            columns[pack][other][tile] - ratio * later[other]
                        )
                    pieces[tile] = jnp.where(cleared, 0.0, pieces[tile]) - ratio * row
    results = []
    for pack in range(packs):
        rows = []
        for tile in range(tiles):
            index = sub + 8 * tile
            lower = jnp.where(
                column < index, blocks[pack][tile], jnp.where(column == index, 1.0, 0.0)
            )
            rows.append(lower * lax.rsqrt(pivots[pack][tile]))
        results.append(jnp.concatenate(rows, axis=0))
    return results


def six_products(left, right, axis):
    high, mid, low = left
    left = jnp.concatenate([high, high, mid, mid, high, low], axis=axis)
    high, mid, low = right
    right = jnp.concatenate([high, mid, high, mid, low, high], axis=0)
    return lax.dot_general(
        left, right, (((axis,), (0,)), ((), ())), preferred_element_type=F32
    )


def eliminate(panel, pack, lower, work_ref, members):
    per_pack = LANES // PANEL
    start = panel * PANEL
    after = start + PANEL
    first = after // LANES * LANES
    total = work_ref.shape[2]
    owner = lax.broadcasted_iota(jnp.int32, (PANEL, LANES), 1) // PANEL
    spread = jnp.concatenate(
        [jnp.where(owner == place, lower, 0.0) for place in range(per_pack)], axis=0
    )
    stacked = jnp.concatenate(
        [
            work_ref[pack * per_pack + place, start:after, first:]
            for place in range(per_pack)
        ],
        axis=0,
    )
    solved = six_products(split3(spread), split3(stacked), 1)
    for place in range(per_pack):
        region = pack * per_pack + place
        rows = solved[place * PANEL : (place + 1) * PANEL]
        work_ref[region, start:after, members:] = rows[:, members - first :]
        if after < members:
            parts = split3(rows)
            change = six_products(
                [part[:, : members - first] for part in parts], parts, 0
            )
            work_ref[region, after:members, first:total] = (
                work_ref[region, after:members, first:total] - change[after - first :]
            )


def analysis_kernel(offsets, first_ref, prior_ref, column_ref, weight_ref, *rest):
    count = len(offsets)
    hbm_refs = rest[:count]
    out_ref, scaled_ref, work_ref, mean_ref, sems = rest[count : count + 5]
    vmem_refs = rest[count + 5 :]
    states_ref, obs_refs = vmem_refs[0], vmem_refs[1:]
    regions, members = prior_ref.shape
    sources, members_dev = states_ref.shape[0], states_ref.shape[2]
    points = states_ref.shape[3]
    packs = regions * PANEL // LANES
    ways = scaled_ref.shape[0]
    batches = sems.shape[0]
    batch_regions = regions // batches

    def loads(batch):
        copies = []
        for index, (hbm, vmem) in enumerate(zip(hbm_refs, vmem_refs)):
            size = vmem.shape[1] // batches
            copies.append(
                pltpu.make_async_copy(
                    hbm.at[:, pl.ds(offsets[index] + batch * size, size)],
                    vmem.at[:, pl.ds(batch * size, size)],
                    sems.at[batch, index],
                )
            )
        return copies

    for batch in range(batches):
        for copy in loads(batch):
            copy.start()

    @pl.loop(0, batches)
    def _(batch):
        for copy in loads(batch):
            copy.wait()

        @pl.loop(0, batch_regions // ways)
        def _(step):
            for way in range(ways):
                region_setup(
                    batch * batch_regions + step * ways + way, first_ref[0], prior_ref,
                    column_ref, weight_ref, states_ref, obs_refs, scaled_ref.at[way],
                    work_ref, mean_ref,
                )

    halves = [range(packs // 2), range(packs // 2, packs)]
    panels = members // PANEL
    lowers = factor_diagonals(0, halves[0], work_ref)
    for panel in range(panels):
        for half in range(2):
            for pack, lower in zip(halves[half], lowers):
                eliminate(panel, pack, lower, work_ref, members)
            if panel + half < panels:
                lowers = factor_diagonals(panel + half, halves[1 - half], work_ref)

    @pl.loop(0, regions)
    def _(region):
        moved = work_ref[region, :, members : members + points]
        solved = work_ref[region, :, members + points :]
        solved = jnp.concatenate([solved] * (points // LANES), axis=1)
        shift = mean_ref[region, :1] + jnp.sum(solved * moved, axis=0, keepdims=True)
        result = (shift + jnp.sqrt(members - 1.0) * moved).astype(BF16)
        for source in range(sources):
            out_ref[source, region] = result[
                source * members_dev : (source + 1) * members_dev
            ]


def analyse(first, prior_rows, weight_rows, states, obs_parts, slots):
    regions, members = prior_rows.shape
    sources, _, members_dev, points = states[0].shape
    width = obs_parts[0][0].shape[3]
    vmem = pl.BlockSpec(memory_space=pltpu.VMEM)
    loaded = [states] + obs_parts
    sizes = [regions] + [regions * slots] * len(obs_parts)
    columns = jnp.broadcast_to(prior_rows[:, :, None], (regions, members, LANES))
    return pl.pallas_call(
        functools.partial(analysis_kernel, [offset for _, offset in loaded]),
        out_shape=jax.ShapeDtypeStruct((sources, regions, members_dev, points), BF16),
        in_specs=[pl.BlockSpec(memory_space=pltpu.SMEM), vmem, vmem, vmem]
        + [pl.BlockSpec(memory_space=pl.ANY)] * len(loaded),
        out_specs=vmem,
        scratch_shapes=[
            pltpu.VMEM((2, members, slots * width), BF16),
            pltpu.VMEM((regions, members, members + points + LANES), F32),
            pltpu.VMEM((regions, 8, points), F32),
            pltpu.SemaphoreType.DMA((regions // 2, len(loaded))),
        ]
        + [
            pltpu.VMEM(array.shape[:1] + (size,) + array.shape[2:], array.dtype)
            for (array, _), size in zip(loaded, sizes)
        ],
        cost_estimate=pl.CostEstimate(
            flops=16 * regions * members * members * (slots * width + points),
            bytes_accessed=2 * regions * members * (slots * width + 2 * points),
            transcendentals=0,
        ),
        compiler_params=pltpu.CompilerParams(vmem_limit_bytes=48 << 20),
    )(first, prior_rows, columns, weight_rows, *[array for array, _ in loaded])


def body(
    ensemble_state, obs_ens, innovation, obs_prec, block_list, block_count, loc_weight, prior_weight
):
    spaces = lax.axis_size("space")
    mem_count = lax.axis_size("mem")
    members_dev, regions_dev, points = ensemble_state.shape
    blocks_dev, width = obs_ens.shape[1:]
    group_size = regions_dev // mem_count
    slots = block_list.shape[1]
    part = group_size // SPLIT
    first_row = lax.axis_index("mem") * group_size

    inner = 2 ** ((spaces.bit_length() - 1) // 2)
    cycle = grid_cycle(spaces // inner, inner)
    forward = [(cycle[k], cycle[(k + 1) % spaces]) for k in range(spaces)]
    backward = [(to, start) for start, to in forward]
    position = [cycle.index(space) for space in range(spaces)]
    half_way = spaces // 2

    def place_of(space):
        return sum(
            jnp.where(space == index, position[index], 0) for index in range(spaces)
        )

    all_ids = block_list.reshape(regions_dev * slots)
    behind = place_of(lax.axis_index("space")) - place_of(all_ids // blocks_dev)
    places = (behind + spaces) % spaces * blocks_dev + all_ids % blocks_dev
    active = jnp.arange(slots, dtype=jnp.int32)[None, :] < block_count[:, None]
    local = jnp.where(active, loc_weight, 0.0).reshape(regions_dev * slots)
    waiting = []
    start = 0
    for share in CHUNKS:
        stop = start + members_dev // share
        waiting.append(jnp.transpose(obs_ens[start:stop], (1, 0, 2)))
        start = stop
    rows = jnp.concatenate([obs_prec, innovation], axis=1)
    rows_ahead, rows_back = [rows], [rows]

    def ring_step(step, ahead, back):
        if step < half_way - 1:
            return lax.ppermute(ahead, "space", forward), lax.ppermute(
                back, "space", backward
            )
        middle = blocks_dev // 2
        return (
            lax.ppermute(ahead[:middle], "space", forward),
            lax.ppermute(back[middle:], "space", backward),
        )

    def exchange(picked):
        return lax.all_to_all(picked, "mem", split_axis=0, concat_axis=0, tiled=True)

    running = []
    obs_parts = [[] for _ in range(SPLIT)]
    stage = 0
    ready = None
    due = {}
    while waiting or running:
        if waiting and (not running or running[-1]["step"] == half_way - 1):
            own = waiting.pop(0)
            running.append({"step": 0, "ahead": [own], "back": [own]})
        moved = [
            ring_step(ring["step"], ring["ahead"][-1], ring["back"][-1])
            for ring in running
        ]
        tied = {"moved": moved, "waiting": waiting, "picked": ready, "due": due.pop(stage, None)}
        if stage < half_way:
            tied["ahead"] = lax.ppermute(rows_ahead[-1], "space", forward)
        if stage < half_way - 1:
            tied["back"] = lax.ppermute(rows_back[-1], "space", backward)
        if stage == 0:
            tied["state"] = ensemble_state
        if stage == half_way - 1:
            tied["states"] = states
        tied = lax.optimization_barrier(tied)
        waiting = tied["waiting"]
        for ring, (ahead, back) in zip(running, tied["moved"]):
            ring["ahead"].append(ahead)
            ring["back"].append(back)
            ring["step"] += 1
        if stage < half_way:
            rows_ahead.append(tied["ahead"])
        if stage < half_way - 1:
            rows_back.append(tied["back"])
        if stage == 0:
            by_region = jnp.transpose(tied["state"], (1, 0, 2)).reshape(
                mem_count, group_size, members_dev, points
            )
            states = exchange(by_region)
        if stage == half_way - 1:
            latest = states = tied["states"]
            weight_rows = weights(places, local, rows_ahead + rows_back[:0:-1])
        if ready is not None:
            picked, _ = lax.optimization_barrier((tied["picked"], latest))
            latest = exchange(picked)
            for index in range(SPLIT):
                obs_parts[index].append((latest, index * part * slots))
            ready = None
            due[stage + half_way - 2] = latest
        if running[0]["step"] == half_way:
            ring = running.pop(0)
            shards = ring["ahead"] + ring["back"][:0:-1]
            if waiting or running:
                ready = pick(
                    places, weight_rows, shards, mem_count, group_size, 0, group_size
                )
            else:
                for index in range(SPLIT):
                    picked = pick(
                        places, weight_rows, shards, mem_count, group_size,
                        index * part, part,
                    )
                    picked, _ = lax.optimization_barrier((picked, latest))
                    latest = exchange(picked)
                    obs_parts[index].append((latest, 0))
        stage += 1

    results = []
    for index in range(SPLIT):
        start = first_row + index * part
        result = analyse(
            (start * slots).reshape(1),
            lax.dynamic_slice_in_dim(prior_weight, start, part, 0),
            weight_rows,
            (states, index * part),
            obs_parts[index],
            slots,
        )
        results.append(exchange(result))
    back = jnp.concatenate(results, axis=1)
    return jnp.transpose(back.reshape(regions_dev, members_dev, points), (1, 0, 2))


def solution(mesh):
    return jax.shard_map(
        body,
        mesh=mesh,
        in_specs=(
            P("mem", "space", None),
            P("mem", "space", None),
            P("space", None),
            P("space", None),
            P("space", None),
            P("space"),
            P("space", None),
            P("space", None),
        ),
        out_specs=P("mem", "space", None),
        check_vma=False,
    )
```

```python
import functools

import jax
import jax.numpy as jnp
from jax import lax
from jax.experimental import pallas as pl
from jax.experimental.pallas import tpu as pltpu
from jax.sharding import PartitionSpec as P

INFLATION = 1.1
PANEL = 32
GROUP = 4
LANES = 128
CHUNKS = (2, 2)
SPLIT = 2
F32 = jnp.float32
BF16 = jnp.bfloat16
NT = (((1,), (1,)), ((), ()))


def split3(value):
    high = value.astype(BF16)
    rest = value - high.astype(F32)
    mid = rest.astype(BF16)
    low = (rest - mid.astype(F32)).astype(BF16)
    return high, mid, low


def weights_kernel(ids_ref, local_ref, *rest):
    part_refs, (out_ref, rows_ref) = rest[:-2], rest[-2:]
    width = out_ref.shape[1] // 2
    size = part_refs[0].shape[0]
    for index, part_ref in enumerate(part_refs):
        rows_ref[index * size : (index + 1) * size] = part_ref[...]

    @pl.loop(0, out_ref.shape[0] // 8, unroll=4)
    def _(group):
        prec, innov = [], []
        for inside in range(8):
            entry = group * 8 + inside
            row = rows_ref[pl.ds(ids_ref[entry], 1), :]
            prec.append(local_ref[entry] * row[:, :width])
            innov.append(row[:, width:])
        scale = jnp.sqrt(jnp.concatenate(prec, axis=0))
        first = pl.multiple_of(group * 8, 8)
        out_ref[pl.ds(first, 8), :width] = scale
        out_ref[pl.ds(first, 8), width:] = scale * jnp.concatenate(innov, axis=0)


def weights(ids, local, parts):
    smem = pl.BlockSpec(memory_space=pltpu.SMEM)
    vmem = pl.BlockSpec(memory_space=pltpu.VMEM)
    size, length = parts[0].shape
    return pl.pallas_call(
        weights_kernel,
        out_shape=jax.ShapeDtypeStruct((ids.shape[0], length), F32),
        in_specs=[smem, smem] + [vmem] * len(parts),
        out_specs=vmem,
        scratch_shapes=[pltpu.VMEM((len(parts) * size, length), F32)],
    )(ids, local, *parts)


def pick_kernel(layout, group_size, first_region, regions, ids_ref, scale_ref, *rest):
    shard_refs, (out_ref, table_ref) = rest[:-2], rest[-2:]
    width = table_ref.shape[2]
    slots = out_ref.shape[1] // regions
    for shard_ref, (start, size) in zip(shard_refs, layout):
        table_ref[start : start + size] = shard_ref[...]

    for member in range(out_ref.shape[0]):

        @pl.loop(0, regions)
        def _(region):
            first = (member * group_size + first_region + region) * slots
            first = pl.multiple_of(first, slots)
            scales = scale_ref[pl.ds(first, slots), :width]
            for slot in range(slots):
                values = table_ref[ids_ref[first + slot]].astype(F32)
                out_ref[member, region * slots + slot] = (
                    values * scales[slot : slot + 1]
                ).astype(BF16)


def pick(ids, scales, shards, mem_count, group_size, first_region, regions):
    slots = ids.shape[0] // (mem_count * group_size)
    layout = []
    total = 0
    for shard in shards:
        layout.append((total, shard.shape[0]))
        total += shard.shape[0]
    row, dtype = shards[0].shape[1:], shards[0].dtype
    entries = regions * slots
    size = row[0] * row[1]
    return pl.pallas_call(
        functools.partial(pick_kernel, layout, group_size, first_region, regions),
        out_shape=jax.ShapeDtypeStruct((mem_count, entries) + row, dtype),
        in_specs=[
            pl.BlockSpec(memory_space=pltpu.SMEM),
        ]
        + [pl.BlockSpec(memory_space=pltpu.VMEM)] * (1 + len(shards)),
        out_specs=pl.BlockSpec(memory_space=pltpu.VMEM),
        scratch_shapes=[pltpu.VMEM((total,) + row, dtype)],
        cost_estimate=pl.CostEstimate(
            flops=mem_count * entries * size,
            bytes_accessed=4 * (mem_count * entries + total) * size,
            transcendentals=0,
        ),
        compiler_params=pltpu.CompilerParams(vmem_limit_bytes=24 << 20),
    )(ids, scales, *shards)


def grid_cycle(outer, inner):
    cells = []
    for row in range(outer):
        columns = range(1, inner) if row % 2 == 0 else range(inner - 1, 0, -1)
        cells += [row * inner + column for column in columns]
    return cells + [row * inner for row in range(outer - 1, -1, -1)]


def row_stack(rows, count):
    length = rows[0].shape[1]
    which = lax.broadcasted_iota(jnp.int32, (count, length), 0)
    stack = jnp.zeros((count, length), F32)
    for index, row in enumerate(rows):
        stack = jnp.where(which == index, row.astype(F32), stack)
    return stack.astype(BF16)


def region_setup(
    region, first, prior_ref, column_ref, weight_ref, states_ref, obs_refs, scaled_ref,
    work_ref, mean_ref,
):
    members = prior_ref.shape[1]
    sources, members_dev = states_ref.shape[0], states_ref.shape[2]
    points = states_ref.shape[3]
    slots = obs_refs[0].shape[1] // prior_ref.shape[0]
    width = obs_refs[0].shape[3]
    for slot in range(slots):
        for source in range(sources):
            start = source * members_dev
            for obs_ref in obs_refs:
                stop = start + obs_ref.shape[2]
                scaled_ref[start:stop, slot * width : (slot + 1) * width] = (
                    obs_ref[source, region * slots + slot]
                )
                start = stop
    scaled = scaled_ref[...]
    gram = lax.dot_general(scaled, scaled, NT, preferred_element_type=F32)
    prior_row = prior_ref[pl.ds(region, 1), :]
    whole = 1.0 / jnp.sum(prior_row, axis=1, keepdims=True)
    share_row = prior_row * whole
    share_col = column_ref[region] * whole
    root_row = jnp.sqrt(members * share_row)
    root_col = jnp.sqrt(members * share_col)
    average = jnp.sum(
        jnp.dot(
            row_stack(split3(share_row), 16), scaled, preferred_element_type=F32
        ),
        axis=0, keepdims=True,
    )
    own = weight_ref[pl.ds(pl.multiple_of(first + region * slots, slots), slots), width:]
    innov = jnp.concatenate([own[slot : slot + 1] for slot in range(slots)], axis=1)
    sums = lax.dot_general(
        scaled, row_stack(split3(innov) + split3(average), 16), NT,
        preferred_element_type=F32,
    )
    kind = lax.broadcasted_iota(jnp.int32, (16, 2 * LANES), 0) // 3
    side = lax.broadcasted_iota(jnp.int32, (16, 2 * LANES), 1) // LANES
    spread = jnp.where(kind == side, 1.0, 0.0).astype(BF16)
    sums = sum(
        jnp.dot(part, spread, preferred_element_type=F32) for part in split3(sums)
    )
    projection, left_col = sums[:, :LANES], sums[:, LANES:]
    total = jnp.sum(share_col * left_col, axis=0, keepdims=True)
    left_col = left_col - total
    vector = root_col * (
        projection - jnp.sum(share_col * projection, axis=0, keepdims=True)
    )
    work_ref[region, :, members + points :] = vector
    for start in range(0, members, LANES):
        tile = slice(start, start + LANES)
        part = gram[:, tile]
        left_row = jnp.sum(share_col * part, axis=0, keepdims=True)
        system = root_col * ((part - left_row) - left_col) * root_row[:, tile]
        on_diag = lax.broadcasted_iota(jnp.int32, (members, LANES), 0) == (
            lax.broadcasted_iota(jnp.int32, (members, LANES), 1) + start
        )
        work_ref[region, :, tile] = system + jnp.where(
            on_diag, (members - 1) / INFLATION, 0.0
        )
    for start in range(0, points, LANES):
        states = jnp.concatenate(
            [
                states_ref[source, region, :, start : start + LANES].astype(F32)
                for source in range(sources)
            ],
            axis=0,
        )
        mean = jnp.sum(share_col * states, axis=0, keepdims=True)
        mean_ref[region, :, start : start + LANES] = jnp.broadcast_to(mean, (8, LANES))
        work_ref[region, :, members + start : members + start + LANES] = root_col * (
            states - mean
        )


def reciprocal(value):
    guess = pl.reciprocal(value, approx=True)
    guess = guess * (2.0 - value * guess)
    return guess * (2.0 - value * guess)


def factor_diagonals(panel, chosen, work_ref):
    per_pack = LANES // PANEL
    start = panel * PANEL
    base, offset = start // LANES * LANES, start % LANES
    lane = lax.broadcasted_iota(jnp.int32, (8, LANES), 1)
    sub = lax.broadcasted_iota(jnp.int32, (8, LANES), 0)
    owner, column = lane // PANEL, lane % PANEL
    tiles = PANEL // 8
    packs = len(chosen)
    blocks = []
    for pack in chosen:
        pieces = []
        for tile in range(tiles):
            merged = None
            for place in range(per_pack):
                region = pack * per_pack + place
                raw = work_ref[
                    region, start + 8 * tile : start + 8 * tile + 8, base : base + LANES
                ]
                shift = (place * PANEL - offset) % LANES
                if shift:
                    raw = pltpu.roll(raw, shift, axis=1)
                merged = raw if merged is None else jnp.where(owner == place, raw, merged)
            pieces.append(merged)
        blocks.append(pieces)
    pivots = [[jnp.ones((8, LANES), F32) for _ in range(tiles)] for _ in range(packs)]
    for first in range(0, PANEL, GROUP):
        home = first // 8
        columns = [
            [
                {
                    tile: jnp.take_along_axis(
                        blocks[pack][tile], owner * PANEL + first + step,
                        axis=1, mode="promise_in_bounds",
                    )
                    for tile in range(home, tiles)
                }
                for step in range(GROUP)
            ]
            for pack in range(packs)
        ]
        second = {}
        for step in range(GROUP):
            inside = first % 8 + step
            at_step = column == first + step
            below = sub > inside
            for pack in range(packs):
                pieces = blocks[pack]
                if step % 2 == 0:
                    pivot = columns[pack][step][home][inside : inside + 1, :]
                    cross = columns[pack][step + 1][home][inside : inside + 1, :]
                    other = columns[pack][step + 1][home][inside + 1 : inside + 2, :]
                    product = pivot * other - cross * cross
                    inverse = reciprocal(pivot)
                    second[pack] = product * inverse, pivot * reciprocal(product)
                else:
                    pivot, inverse = second[pack]
                row = jnp.where(at_step[:1], 1.0, pieces[home][inside : inside + 1, :])
                pivots[pack][home] = jnp.where(sub == inside, pivot, pivots[pack][home])
                later = {
                    other: columns[pack][other][home][inside : inside + 1, :]
                    for other in range(step + 1, GROUP)
                }
                for tile in range(home, tiles):
                    ratio = columns[pack][step][tile] * inverse
                    cleared = at_step
                    if tile == home:
                        ratio = jnp.where(below, ratio, 0.0)
                        cleared = at_step & below
                    for other in later:
                        columns[pack][other][tile] = (
                            columns[pack][other][tile] - ratio * later[other]
                        )
                    pieces[tile] = jnp.where(cleared, 0.0, pieces[tile]) - ratio * row
    results = []
    for pack in range(packs):
        rows = []
        for tile in range(tiles):
            index = sub + 8 * tile
            lower = jnp.where(
                column < index, blocks[pack][tile], jnp.where(column == index, 1.0, 0.0)
            )
            rows.append(lower * lax.rsqrt(pivots[pack][tile]))
        results.append(jnp.concatenate(rows, axis=0))
    return results


def six_products(left, right, axis):
    high, mid, low = left
    left = jnp.concatenate([high, high, mid, mid, high, low], axis=axis)
    high, mid, low = right
    right = jnp.concatenate([high, mid, high, mid, low, high], axis=0)
    return lax.dot_general(
        left, right, (((axis,), (0,)), ((), ())), preferred_element_type=F32
    )


def eliminate(panel, pack, lower, work_ref, members):
    per_pack = LANES // PANEL
    start = panel * PANEL
    after = start + PANEL
    first = after // LANES * LANES
    total = work_ref.shape[2]
    owner = lax.broadcasted_iota(jnp.int32, (PANEL, LANES), 1) // PANEL
    spread = jnp.concatenate(
        [jnp.where(owner == place, lower, 0.0) for place in range(per_pack)], axis=0
    )
    stacked = jnp.concatenate(
        [
            work_ref[pack * per_pack + place, start:after, first:]
            for place in range(per_pack)
        ],
        axis=0,
    )
    solved = six_products(split3(spread), split3(stacked), 1)
    for place in range(per_pack):
        region = pack * per_pack + place
        rows = solved[place * PANEL : (place + 1) * PANEL]
        work_ref[region, start:after, members:] = rows[:, members - first :]
        if after < members:
            parts = split3(rows)
            change = six_products(
                [part[:, : members - first] for part in parts], parts, 0
            )
            work_ref[region, after:members, first:total] = (
                work_ref[region, after:members, first:total] - change[after - first :]
            )


def analysis_kernel(offsets, first_ref, prior_ref, column_ref, weight_ref, *rest):
    count = len(offsets)
    hbm_refs = rest[:count]
    out_ref, scaled_ref, work_ref, mean_ref, sems = rest[count : count + 5]
    vmem_refs = rest[count + 5 :]
    states_ref, obs_refs = vmem_refs[0], vmem_refs[1:]
    regions, members = prior_ref.shape
    sources, members_dev = states_ref.shape[0], states_ref.shape[2]
    points = states_ref.shape[3]
    packs = regions * PANEL // LANES
    ways = scaled_ref.shape[0]
    batches = sems.shape[0]
    batch_regions = regions // batches

    def loads(batch):
        copies = []
        for index, (hbm, vmem) in enumerate(zip(hbm_refs, vmem_refs)):
            size = vmem.shape[1] // batches
            copies.append(
                pltpu.make_async_copy(
                    hbm.at[:, pl.ds(offsets[index] + batch * size, size)],
                    vmem.at[:, pl.ds(batch * size, size)],
                    sems.at[batch, index],
                )
            )
        return copies

    for batch in range(batches):
        for copy in loads(batch):
            copy.start()

    @pl.loop(0, batches)
    def _(batch):
        for copy in loads(batch):
            copy.wait()

        @pl.loop(0, batch_regions // ways)
        def _(step):
            for way in range(ways):
                region_setup(
                    batch * batch_regions + step * ways + way, first_ref[0], prior_ref,
                    column_ref, weight_ref, states_ref, obs_refs, scaled_ref.at[way],
                    work_ref, mean_ref,
                )

    for panel in range(members // PANEL):
        lowers = factor_diagonals(panel, range(packs), work_ref)
        for pack in range(packs):
            eliminate(panel, pack, lowers[pack], work_ref, members)

    @pl.loop(0, regions)
    def _(region):
        moved = work_ref[region, :, members : members + points]
        solved = work_ref[region, :, members + points :]
        solved = jnp.concatenate([solved] * (points // LANES), axis=1)
        shift = mean_ref[region, :1] + jnp.sum(solved * moved, axis=0, keepdims=True)
        result = (shift + jnp.sqrt(members - 1.0) * moved).astype(BF16)
        for source in range(sources):
            out_ref[source, region] = result[
                source * members_dev : (source + 1) * members_dev
            ]


def analyse(first, prior_rows, weight_rows, states, obs_parts, slots):
    regions, members = prior_rows.shape
    sources, _, members_dev, points = states[0].shape
    width = obs_parts[0][0].shape[3]
    vmem = pl.BlockSpec(memory_space=pltpu.VMEM)
    loaded = [states] + obs_parts
    sizes = [regions] + [regions * slots] * len(obs_parts)
    columns = jnp.broadcast_to(prior_rows[:, :, None], (regions, members, LANES))
    return pl.pallas_call(
        functools.partial(analysis_kernel, [offset for _, offset in loaded]),
        out_shape=jax.ShapeDtypeStruct((sources, regions, members_dev, points), BF16),
        in_specs=[pl.BlockSpec(memory_space=pltpu.SMEM), vmem, vmem, vmem]
        + [pl.BlockSpec(memory_space=pl.ANY)] * len(loaded),
        out_specs=vmem,
        scratch_shapes=[
            pltpu.VMEM((2, members, slots * width), BF16),
            pltpu.VMEM((regions, members, members + points + LANES), F32),
            pltpu.VMEM((regions, 8, points), F32),
            pltpu.SemaphoreType.DMA((regions // 2, len(loaded))),
        ]
        + [
            pltpu.VMEM(array.shape[:1] + (size,) + array.shape[2:], array.dtype)
            for (array, _), size in zip(loaded, sizes)
        ],
        cost_estimate=pl.CostEstimate(
            flops=16 * regions * members * members * (slots * width + points),
            bytes_accessed=2 * regions * members * (slots * width + 2 * points),
            transcendentals=0,
        ),
        compiler_params=pltpu.CompilerParams(vmem_limit_bytes=48 << 20),
    )(first, prior_rows, columns, weight_rows, *[array for array, _ in loaded])


def body(
    ensemble_state, obs_ens, innovation, obs_prec, block_list, block_count, loc_weight, prior_weight
):
    spaces = lax.axis_size("space")
    mem_count = lax.axis_size("mem")
    members_dev, regions_dev, points = ensemble_state.shape
    blocks_dev, width = obs_ens.shape[1:]
    group_size = regions_dev // mem_count
    slots = block_list.shape[1]
    part = group_size // SPLIT
    first_row = lax.axis_index("mem") * group_size

    inner = 2 ** ((spaces.bit_length() - 1) // 2)
    cycle = grid_cycle(spaces // inner, inner)
    forward = [(cycle[k], cycle[(k + 1) % spaces]) for k in range(spaces)]
    backward = [(to, start) for start, to in forward]
    position = [cycle.index(space) for space in range(spaces)]
    half_way = spaces // 2

    def place_of(space):
        return sum(
            jnp.where(space == index, position[index], 0) for index in range(spaces)
        )

    all_ids = block_list.reshape(regions_dev * slots)
    behind = place_of(lax.axis_index("space")) - place_of(all_ids // blocks_dev)
    places = (behind + spaces) % spaces * blocks_dev + all_ids % blocks_dev
    active = jnp.arange(slots, dtype=jnp.int32)[None, :] < block_count[:, None]
    local = jnp.where(active, loc_weight, 0.0).reshape(regions_dev * slots)
    waiting = []
    start = 0
    for share in CHUNKS:
        stop = start + members_dev // share
        waiting.append(jnp.transpose(obs_ens[start:stop], (1, 0, 2)))
        start = stop
    rows = jnp.concatenate([obs_prec, innovation], axis=1)
    rows_ahead, rows_back = [rows], [rows]

    def ring_step(step, ahead, back):
        if step < half_way - 1:
            return lax.ppermute(ahead, "space", forward), lax.ppermute(
                back, "space", backward
            )
        middle = blocks_dev // 2
        return (
            lax.ppermute(ahead[:middle], "space", forward),
            lax.ppermute(back[middle:], "space", backward),
        )

    def exchange(picked):
        return lax.all_to_all(picked, "mem", split_axis=0, concat_axis=0, tiled=True)

    running = []
    obs_parts = [[] for _ in range(SPLIT)]
    stage = 0
    due = {}
    while waiting or running:
        if waiting and (not running or running[-1]["step"] == half_way - 1):
            own = waiting.pop(0)
            running.append({"step": 0, "ahead": [own], "back": [own]})
        moved = [
            ring_step(ring["step"], ring["ahead"][-1], ring["back"][-1])
            for ring in running
        ]
        tied = {"moved": moved, "waiting": waiting, "due": due.pop(stage, None)}
        if stage < half_way:
            tied["ahead"] = lax.ppermute(rows_ahead[-1], "space", forward)
        if stage < half_way - 1:
            tied["back"] = lax.ppermute(rows_back[-1], "space", backward)
        if stage == 0:
            tied["state"] = ensemble_state
        if stage == half_way - 1:
            tied["states"] = states
            tied["weights"] = weights(
                places, local, rows_ahead + [tied.pop("ahead")] + rows_back[:0:-1]
            )
        tied = lax.optimization_barrier(tied)
        waiting = tied["waiting"]
        for ring, (ahead, back) in zip(running, tied["moved"]):
            ring["ahead"].append(ahead)
            ring["back"].append(back)
            ring["step"] += 1
        if stage < half_way - 1:
            rows_ahead.append(tied["ahead"])
            rows_back.append(tied["back"])
        if stage == 0:
            by_region = jnp.transpose(tied["state"], (1, 0, 2)).reshape(
                mem_count, group_size, members_dev, points
            )
            states = exchange(by_region)
        if stage == half_way - 1:
            latest = states = tied["states"]
            weight_rows = tied["weights"]
        if running[0]["step"] == half_way:
            ring = running.pop(0)
            shards = ring["ahead"] + ring["back"][:0:-1]
            if waiting or running:
                picked = pick(
                    places, weight_rows, shards, mem_count, group_size, 0, group_size
                )
                due[stage + 1] = picked
                picked, _ = lax.optimization_barrier((picked, latest))
                latest = exchange(picked)
                due[stage + half_way - 1] = latest
                for index in range(SPLIT):
                    obs_parts[index].append((latest, index * part * slots))
            else:
                for index in range(SPLIT):
                    picked = pick(
                        places, weight_rows, shards, mem_count, group_size,
                        index * part, part,
                    )
                    picked, _ = lax.optimization_barrier((picked, latest))
                    latest = exchange(picked)
                    obs_parts[index].append((latest, 0))
        stage += 1

    results = []
    for index in range(SPLIT):
        start = first_row + index * part
        result = analyse(
            (start * slots).reshape(1),
            lax.dynamic_slice_in_dim(prior_weight, start, part, 0),
            weight_rows,
            (states, index * part),
            obs_parts[index],
            slots,
        )
        results.append(exchange(result))
    back = jnp.concatenate(results, axis=1)
    return jnp.transpose(back.reshape(regions_dev, members_dev, points), (1, 0, 2))


def solution(mesh):
    return jax.shard_map(
        body,
        mesh=mesh,
        in_specs=(
            P("mem", "space", None),
            P("mem", "space", None),
            P("space", None),
            P("space", None),
            P("space", None),
            P("space"),
            P("space", None),
            P("space", None),
        ),
        out_specs=P("mem", "space", None),
        check_vma=False,
    )
```

```python
import functools

import jax
import jax.numpy as jnp
from jax import lax
from jax.experimental import pallas as pl
from jax.experimental.pallas import tpu as pltpu
from jax.sharding import PartitionSpec as P

INFLATION = 1.1
PANEL = 32
GROUP = 8
LANES = 128
CHUNKS = (2, 2)
SPLIT = 2
F32 = jnp.float32
BF16 = jnp.bfloat16
NT = (((1,), (1,)), ((), ()))


def split3(value):
    high = value.astype(BF16)
    rest = value - high.astype(F32)
    mid = rest.astype(BF16)
    low = (rest - mid.astype(F32)).astype(BF16)
    return high, mid, low


def weights_kernel(ids_ref, local_ref, *rest):
    part_refs, (out_ref, rows_ref) = rest[:-2], rest[-2:]
    width = out_ref.shape[1] // 2
    size = part_refs[0].shape[0]
    for index, part_ref in enumerate(part_refs):
        rows_ref[index * size : (index + 1) * size] = part_ref[...]

    @pl.loop(0, out_ref.shape[0] // 8, unroll=4)
    def _(group):
        prec, innov = [], []
        for inside in range(8):
            entry = group * 8 + inside
            row = rows_ref[pl.ds(ids_ref[entry], 1), :]
            prec.append(local_ref[entry] * row[:, :width])
            innov.append(row[:, width:])
        scale = jnp.sqrt(jnp.concatenate(prec, axis=0))
        first = pl.multiple_of(group * 8, 8)
        out_ref[pl.ds(first, 8), :width] = scale
        out_ref[pl.ds(first, 8), width:] = scale * jnp.concatenate(innov, axis=0)


def weights(ids, local, parts):
    smem = pl.BlockSpec(memory_space=pltpu.SMEM)
    vmem = pl.BlockSpec(memory_space=pltpu.VMEM)
    size, length = parts[0].shape
    return pl.pallas_call(
        weights_kernel,
        out_shape=jax.ShapeDtypeStruct((ids.shape[0], length), F32),
        in_specs=[smem, smem] + [vmem] * len(parts),
        out_specs=vmem,
        scratch_shapes=[pltpu.VMEM((len(parts) * size, length), F32)],
    )(ids, local, *parts)


def pick_kernel(layout, group_size, first_region, regions, ids_ref, scale_ref, *rest):
    shard_refs, (out_ref, table_ref) = rest[:-2], rest[-2:]
    width = table_ref.shape[2]
    slots = out_ref.shape[1] // regions
    for shard_ref, (start, size) in zip(shard_refs, layout):
        table_ref[start : start + size] = shard_ref[...]

    for member in range(out_ref.shape[0]):

        @pl.loop(0, regions)
        def _(region):
            first = (member * group_size + first_region + region) * slots
            first = pl.multiple_of(first, slots)
            scales = scale_ref[pl.ds(first, slots), :width]
            for slot in range(slots):
                values = table_ref[ids_ref[first + slot]].astype(F32)
                out_ref[member, region * slots + slot] = (
                    values * scales[slot : slot + 1]
                ).astype(BF16)


def pick(ids, scales, shards, mem_count, group_size, first_region, regions):
    slots = ids.shape[0] // (mem_count * group_size)
    layout = []
    total = 0
    for shard in shards:
        layout.append((total, shard.shape[0]))
        total += shard.shape[0]
    row, dtype = shards[0].shape[1:], shards[0].dtype
    entries = regions * slots
    size = row[0] * row[1]
    return pl.pallas_call(
        functools.partial(pick_kernel, layout, group_size, first_region, regions),
        out_shape=jax.ShapeDtypeStruct((mem_count, entries) + row, dtype),
        in_specs=[
            pl.BlockSpec(memory_space=pltpu.SMEM),
        ]
        + [pl.BlockSpec(memory_space=pltpu.VMEM)] * (1 + len(shards)),
        out_specs=pl.BlockSpec(memory_space=pltpu.VMEM),
        scratch_shapes=[pltpu.VMEM((total,) + row, dtype)],
        cost_estimate=pl.CostEstimate(
            flops=mem_count * entries * size,
            bytes_accessed=4 * (mem_count * entries + total) * size,
            transcendentals=0,
        ),
        compiler_params=pltpu.CompilerParams(vmem_limit_bytes=24 << 20),
    )(ids, scales, *shards)


def grid_cycle(outer, inner):
    cells = []
    for row in range(outer):
        columns = range(1, inner) if row % 2 == 0 else range(inner - 1, 0, -1)
        cells += [row * inner + column for column in columns]
    return cells + [row * inner for row in range(outer - 1, -1, -1)]


def row_stack(rows, count):
    length = rows[0].shape[1]
    which = lax.broadcasted_iota(jnp.int32, (count, length), 0)
    stack = jnp.zeros((count, length), F32)
    for index, row in enumerate(rows):
        stack = jnp.where(which == index, row.astype(F32), stack)
    return stack.astype(BF16)


def region_setup(
    region, first, prior_ref, column_ref, weight_ref, states_ref, obs_refs, scaled_ref,
    work_ref, lead_ref, mean_ref,
):
    members = prior_ref.shape[1]
    sources, members_dev = states_ref.shape[0], states_ref.shape[2]
    points = states_ref.shape[3]
    slots = obs_refs[0].shape[1] // prior_ref.shape[0]
    width = obs_refs[0].shape[3]
    for slot in range(slots):
        for source in range(sources):
            start = source * members_dev
            for obs_ref in obs_refs:
                stop = start + obs_ref.shape[2]
                scaled_ref[start:stop, slot * width : (slot + 1) * width] = (
                    obs_ref[source, region * slots + slot]
                )
                start = stop
    scaled = scaled_ref[...]
    gram = lax.dot_general(scaled, scaled, NT, preferred_element_type=F32)
    prior_row = prior_ref[pl.ds(region, 1), :]
    whole = 1.0 / jnp.sum(prior_row, axis=1, keepdims=True)
    share_row = prior_row * whole
    share_col = column_ref[region] * whole
    root_row = jnp.sqrt(members * share_row)
    root_col = jnp.sqrt(members * share_col)
    average = jnp.sum(
        jnp.dot(
            row_stack(split3(share_row), 16), scaled, preferred_element_type=F32
        ),
        axis=0, keepdims=True,
    )
    own = weight_ref[pl.ds(pl.multiple_of(first + region * slots, slots), slots), width:]
    innov = jnp.concatenate([own[slot : slot + 1] for slot in range(slots)], axis=1)
    sums = lax.dot_general(
        scaled, row_stack(split3(innov) + split3(average), 16), NT,
        preferred_element_type=F32,
    )
    kind = lax.broadcasted_iota(jnp.int32, (16, 2 * LANES), 0) // 3
    side = lax.broadcasted_iota(jnp.int32, (16, 2 * LANES), 1) // LANES
    spread = jnp.where(kind == side, 1.0, 0.0).astype(BF16)
    sums = sum(
        jnp.dot(part, spread, preferred_element_type=F32) for part in split3(sums)
    )
    projection, left_col = sums[:, :LANES], sums[:, LANES:]
    total = jnp.sum(share_col * left_col, axis=0, keepdims=True)
    left_col = left_col - total
    vector = root_col * (
        projection - jnp.sum(share_col * projection, axis=0, keepdims=True)
    )
    lead_ref[region] = vector[:PANEL]
    carried = lax.broadcasted_iota(jnp.int32, (members, LANES), 1) < PANEL
    carried &= lax.broadcasted_iota(jnp.int32, (members, LANES), 0) >= PANEL
    for start in range(0, members, LANES):
        tile = slice(start, start + LANES)
        part = gram[:, tile]
        left_row = jnp.sum(share_col * part, axis=0, keepdims=True)
        system = root_col * ((part - left_row) - left_col) * root_row[:, tile]
        on_diag = lax.broadcasted_iota(jnp.int32, (members, LANES), 0) == (
            lax.broadcasted_iota(jnp.int32, (members, LANES), 1) + start
        )
        system = system + jnp.where(on_diag, (members - 1) / INFLATION, 0.0)
        if start == 0:
            system = jnp.where(carried, vector, system)
        work_ref[region, :, tile] = system
    for start in range(0, points, LANES):
        states = jnp.concatenate(
            [
                states_ref[source, region, :, start : start + LANES].astype(F32)
                for source in range(sources)
            ],
            axis=0,
        )
        mean = jnp.sum(share_col * states, axis=0, keepdims=True)
        mean_ref[region, :, start : start + LANES] = jnp.broadcast_to(mean, (8, LANES))
        work_ref[region, :, members + start : members + start + LANES] = root_col * (
            states - mean
        )


def reciprocal(value):
    guess = pl.reciprocal(value, approx=True)
    guess = guess * (2.0 - value * guess)
    return guess * (2.0 - value * guess)


def factor_diagonals(panel, chosen, work_ref):
    per_pack = LANES // PANEL
    start = panel * PANEL
    base, offset = start // LANES * LANES, start % LANES
    lane = lax.broadcasted_iota(jnp.int32, (8, LANES), 1)
    sub = lax.broadcasted_iota(jnp.int32, (8, LANES), 0)
    owner, column = lane // PANEL, lane % PANEL
    tiles = PANEL // 8
    packs = len(chosen)
    blocks = []
    for pack in chosen:
        pieces = []
        for tile in range(tiles):
            merged = None
            for place in range(per_pack):
                region = pack * per_pack + place
                raw = work_ref[
                    region, start + 8 * tile : start + 8 * tile + 8, base : base + LANES
                ]
                shift = (place * PANEL - offset) % LANES
                if shift:
                    raw = pltpu.roll(raw, shift, axis=1)
                merged = raw if merged is None else jnp.where(owner == place, raw, merged)
            pieces.append(merged)
        blocks.append(pieces)
    pivots = [[jnp.ones((8, LANES), F32) for _ in range(tiles)] for _ in range(packs)]
    for first in range(0, PANEL, GROUP):
        home = first // 8
        columns = [
            [
                {
                    tile: jnp.take_along_axis(
                        blocks[pack][tile], owner * PANEL + first + step,
                        axis=1, mode="promise_in_bounds",
                    )
                    for tile in range(home, tiles)
                }
                for step in range(GROUP)
            ]
            for pack in range(packs)
        ]
        second = {}
        for step in range(GROUP):
            inside = first % 8 + step
            at_step = column == first + step
            below = sub > inside
            for pack in range(packs):
                pieces = blocks[pack]
                if step % 2 == 0:
                    pivot = columns[pack][step][home][inside : inside + 1, :]
                    cross = columns[pack][step + 1][home][inside : inside + 1, :]
                    other = columns[pack][step + 1][home][inside + 1 : inside + 2, :]
                    product = pivot * other - cross * cross
                    inverse = reciprocal(pivot)
                    second[pack] = product * inverse, pivot * reciprocal(product)
                else:
                    pivot, inverse = second[pack]
                row = jnp.where(at_step[:1], 1.0, pieces[home][inside : inside + 1, :])
                pivots[pack][home] = jnp.where(sub == inside, pivot, pivots[pack][home])
                later = {
                    other: columns[pack][other][home][inside : inside + 1, :]
                    for other in range(step + 1, GROUP)
                }
                for tile in range(home, tiles):
                    ratio = columns[pack][step][tile] * inverse
                    cleared = at_step
                    if tile == home:
                        ratio = jnp.where(below, ratio, 0.0)
                        cleared = at_step & below
                    for other in later:
                        columns[pack][other][tile] = (
                            columns[pack][other][tile] - ratio * later[other]
                        )
                    pieces[tile] = jnp.where(cleared, 0.0, pieces[tile]) - ratio * row
    results = []
    for pack in range(packs):
        rows = []
        for tile in range(tiles):
            index = sub + 8 * tile
            lower = jnp.where(
                column < index, blocks[pack][tile], jnp.where(column == index, 1.0, 0.0)
            )
            rows.append(lower * lax.rsqrt(pivots[pack][tile]))
        results.append(jnp.concatenate(rows, axis=0))
    return results


def six_products(left, right, axis):
    high, mid, low = left
    left = jnp.concatenate([high, high, mid, mid, high, low], axis=axis)
    high, mid, low = right
    right = jnp.concatenate([high, mid, high, mid, low, high], axis=0)
    return lax.dot_general(
        left, right, (((axis,), (0,)), ((), ())), preferred_element_type=F32
    )


def eliminate(panel, pack, lower, work_ref, lead_ref, members):
    per_pack = LANES // PANEL
    start = panel * PANEL
    after = start + PANEL
    first = start // LANES * LANES
    kept = after // LANES * LANES
    owner = lax.broadcasted_iota(jnp.int32, (PANEL, LANES), 1) // PANEL

    def carry(region, rows, block):
        if start % LANES:
            return block
        if start == 0:
            source = lead_ref[region]
        else:
            source = work_ref[region, rows, first - LANES : first]
        lane = lax.broadcasted_iota(jnp.int32, source.shape, 1)
        head = jnp.where(lane < PANEL, source, block[:, :LANES])
        return jnp.concatenate([head, block[:, LANES:]], axis=1)

    spread = jnp.concatenate(
        [jnp.where(owner == place, lower, 0.0) for place in range(per_pack)], axis=0
    )
    here, rest = slice(start, after), slice(after, members)
    stacked = []
    for place in range(per_pack):
        region = pack * per_pack + place
        stacked.append(carry(region, here, work_ref[region, here, first:]))
    stacked = jnp.concatenate(stacked, axis=0)
    solved = six_products(split3(spread), split3(stacked), 1)
    for place in range(per_pack):
        region = pack * per_pack + place
        rows = solved[place * PANEL : (place + 1) * PANEL]
        work_ref[region, here, first : first + LANES] = rows[:, :LANES]
        work_ref[region, here, members:] = rows[:, members - first :]
        if after < members:
            parts = split3(rows)
            change = six_products(
                [part[:, kept - first : members - first] for part in parts], parts, 0
            )
            old = work_ref[region, rest, first:]
            if start:
                old = carry(region, rest, old)
            work_ref[region, rest, first:] = old - change[after - kept :]


def analysis_kernel(offsets, first_ref, prior_ref, column_ref, weight_ref, *rest):
    count = len(offsets)
    hbm_refs = rest[:count]
    out_ref, scaled_ref, work_ref, lead_ref, mean_ref, sems = rest[count : count + 6]
    vmem_refs = rest[count + 6 :]
    states_ref, obs_refs = vmem_refs[0], vmem_refs[1:]
    regions, members = prior_ref.shape
    sources, members_dev = states_ref.shape[0], states_ref.shape[2]
    points = states_ref.shape[3]
    packs = regions * PANEL // LANES
    ways = scaled_ref.shape[0]
    batches = sems.shape[0]
    batch_regions = regions // batches

    def loads(batch):
        copies = []
        for index, (hbm, vmem) in enumerate(zip(hbm_refs, vmem_refs)):
            size = vmem.shape[1] // batches
            copies.append(
                pltpu.make_async_copy(
                    hbm.at[:, pl.ds(offsets[index] + batch * size, size)],
                    vmem.at[:, pl.ds(batch * size, size)],
                    sems.at[batch, index],
                )
            )
        return copies

    for batch in range(batches):
        for copy in loads(batch):
            copy.start()

    @pl.loop(0, batches)
    def _(batch):
        for copy in loads(batch):
            copy.wait()

        @pl.loop(0, batch_regions // ways)
        def _(step):
            for way in range(ways):
                region_setup(
                    batch * batch_regions + step * ways + way, first_ref[0], prior_ref,
                    column_ref, weight_ref, states_ref, obs_refs, scaled_ref.at[way],
                    work_ref, lead_ref, mean_ref,
                )

    for panel in range(members // PANEL):
        lowers = factor_diagonals(panel, range(packs), work_ref)
        for pack in range(packs):
            eliminate(panel, pack, lowers[pack], work_ref, lead_ref, members)

    @pl.loop(0, regions)
    def _(region):
        moved = work_ref[region, :, members : members + points]
        solved = jnp.concatenate(
            [
                work_ref[region, start : start + LANES, start : start + 1]
                for start in range(0, members, LANES)
            ],
            axis=0,
        )
        shift = mean_ref[region, :1] + jnp.sum(solved * moved, axis=0, keepdims=True)
        result = (shift + jnp.sqrt(members - 1.0) * moved).astype(BF16)
        for source in range(sources):
            out_ref[source, region] = result[
                source * members_dev : (source + 1) * members_dev
            ]


def analyse(first, prior_rows, weight_rows, states, obs_parts, slots):
    regions, members = prior_rows.shape
    sources, _, members_dev, points = states[0].shape
    width = obs_parts[0][0].shape[3]
    vmem = pl.BlockSpec(memory_space=pltpu.VMEM)
    loaded = [states] + obs_parts
    sizes = [regions] + [regions * slots] * len(obs_parts)
    columns = jnp.broadcast_to(prior_rows[:, :, None], (regions, members, LANES))
    return pl.pallas_call(
        functools.partial(analysis_kernel, [offset for _, offset in loaded]),
        out_shape=jax.ShapeDtypeStruct((sources, regions, members_dev, points), BF16),
        in_specs=[pl.BlockSpec(memory_space=pltpu.SMEM), vmem, vmem, vmem]
        + [pl.BlockSpec(memory_space=pl.ANY)] * len(loaded),
        out_specs=vmem,
        scratch_shapes=[
            pltpu.VMEM((2, members, slots * width), BF16),
            pltpu.VMEM((regions, members, members + points), F32),
            pltpu.VMEM((regions, PANEL, LANES), F32),
            pltpu.VMEM((regions, 8, points), F32),
            pltpu.SemaphoreType.DMA((regions // 2, len(loaded))),
        ]
        + [
            pltpu.VMEM(array.shape[:1] + (size,) + array.shape[2:], array.dtype)
            for (array, _), size in zip(loaded, sizes)
        ],
        cost_estimate=pl.CostEstimate(
            flops=16 * regions * members * members * (slots * width + points),
            bytes_accessed=2 * regions * members * (slots * width + 2 * points),
            transcendentals=0,
        ),
        compiler_params=pltpu.CompilerParams(vmem_limit_bytes=48 << 20),
    )(first, prior_rows, columns, weight_rows, *[array for array, _ in loaded])


def body(
    ensemble_state, obs_ens, innovation, obs_prec, block_list, block_count, loc_weight, prior_weight
):
    spaces = lax.axis_size("space")
    mem_count = lax.axis_size("mem")
    members_dev, regions_dev, points = ensemble_state.shape
    blocks_dev, width = obs_ens.shape[1:]
    group_size = regions_dev // mem_count
    slots = block_list.shape[1]
    part = group_size // SPLIT
    first_row = lax.axis_index("mem") * group_size

    inner = 2 ** ((spaces.bit_length() - 1) // 2)
    cycle = grid_cycle(spaces // inner, inner)
    forward = [(cycle[k], cycle[(k + 1) % spaces]) for k in range(spaces)]
    backward = [(to, start) for start, to in forward]
    position = [cycle.index(space) for space in range(spaces)]
    half_way = spaces // 2

    def place_of(space):
        return sum(
            jnp.where(space == index, position[index], 0) for index in range(spaces)
        )

    all_ids = block_list.reshape(regions_dev * slots)
    behind = place_of(lax.axis_index("space")) - place_of(all_ids // blocks_dev)
    places = (behind + spaces) % spaces * blocks_dev + all_ids % blocks_dev
    active = jnp.arange(slots, dtype=jnp.int32)[None, :] < block_count[:, None]
    local = jnp.where(active, loc_weight, 0.0).reshape(regions_dev * slots)
    waiting = []
    start = 0
    for share in CHUNKS:
        stop = start + members_dev // share
        waiting.append(jnp.transpose(obs_ens[start:stop], (1, 0, 2)))
        start = stop
    rows = jnp.concatenate([obs_prec, innovation], axis=1)
    rows_ahead, rows_back = [rows], [rows]

    def ring_step(step, ahead, back):
        if step < half_way - 1:
            return lax.ppermute(ahead, "space", forward), lax.ppermute(
                back, "space", backward
            )
        middle = blocks_dev // 2
        return (
            lax.ppermute(ahead[:middle], "space", forward),
            lax.ppermute(back[middle:], "space", backward),
        )

    def exchange(picked):
        return lax.all_to_all(picked, "mem", split_axis=0, concat_axis=0, tiled=True)

    running = []
    obs_parts = [[] for _ in range(SPLIT)]
    stage = 0
    due = {}
    while waiting or running:
        if waiting and (not running or running[-1]["step"] == half_way - 1):
            own = waiting.pop(0)
            running.append({"step": 0, "ahead": [own], "back": [own]})
        moved = [
            ring_step(ring["step"], ring["ahead"][-1], ring["back"][-1])
            for ring in running
        ]
        tied = {"moved": moved, "waiting": waiting, "due": due.pop(stage, None)}
        if stage < half_way:
            tied["ahead"] = lax.ppermute(rows_ahead[-1], "space", forward)
        if stage < half_way - 1:
            tied["back"] = lax.ppermute(rows_back[-1], "space", backward)
        if stage == 0:
            tied["state"] = ensemble_state
        if stage == half_way - 1:
            tied["states"] = states
            tied["weights"] = weights(
                places, local, rows_ahead + [tied.pop("ahead")] + rows_back[:0:-1]
            )
        tied = lax.optimization_barrier(tied)
        waiting = tied["waiting"]
        for ring, (ahead, back) in zip(running, tied["moved"]):
            ring["ahead"].append(ahead)
            ring["back"].append(back)
            ring["step"] += 1
        if stage < half_way - 1:
            rows_ahead.append(tied["ahead"])
            rows_back.append(tied["back"])
        if stage == 0:
            by_region = jnp.transpose(tied["state"], (1, 0, 2)).reshape(
                mem_count, group_size, members_dev, points
            )
            states = exchange(by_region)
        if stage == half_way - 1:
            latest = states = tied["states"]
            weight_rows = tied["weights"]
        if tied["due"] is not None:
            picked, _ = lax.optimization_barrier((tied["due"], latest))
            latest = exchange(picked)
            for index in range(SPLIT):
                obs_parts[index].append((latest, index * part * slots))
        if running[0]["step"] == half_way:
            ring = running.pop(0)
            shards = ring["ahead"] + ring["back"][:0:-1]
            if waiting or running:
                picked = pick(
                    places, weight_rows, shards, mem_count, group_size, 0, group_size
                )
                due[stage + 1] = picked
            else:
                for index in range(SPLIT):
                    picked = pick(
                        places, weight_rows, shards, mem_count, group_size,
                        index * part, part,
                    )
                    picked, _ = lax.optimization_barrier((picked, latest))
                    latest = exchange(picked)
                    obs_parts[index].append((latest, 0))
        stage += 1

    results = []
    for index in range(SPLIT):
        start = first_row + index * part
        if results:
            start, results[-1] = lax.optimization_barrier((start, results[-1]))
            results[-1] = exchange(results[-1])
        result = analyse(
            (start * slots).reshape(1),
            lax.dynamic_slice_in_dim(prior_weight, start, part, 0),
            weight_rows,
            (states, index * part),
            obs_parts[index],
            slots,
        )
        results.append(result)
    results[-1] = exchange(results[-1])
    back = jnp.concatenate(results, axis=1)
    return jnp.transpose(back.reshape(regions_dev, members_dev, points), (1, 0, 2))


def solution(mesh):
    return jax.shard_map(
        body,
        mesh=mesh,
        in_specs=(
            P("mem", "space", None),
            P("mem", "space", None),
            P("space", None),
            P("space", None),
            P("space", None),
            P("space"),
            P("space", None),
            P("space", None),
        ),
        out_specs=P("mem", "space", None),
        check_vma=False,
    )
```

```python
import functools

import jax
import jax.numpy as jnp
from jax import lax
from jax.experimental import pallas as pl
from jax.experimental.pallas import tpu as pltpu
from jax.sharding import PartitionSpec as P

INFLATION = 1.1
PANEL = 32
GROUP = 8
LANES = 128
CHUNKS = (1,)
SPLIT = 2
F32 = jnp.float32
BF16 = jnp.bfloat16
NT = (((1,), (1,)), ((), ()))


def split3(value):
    high = value.astype(BF16)
    rest = value - high.astype(F32)
    mid = rest.astype(BF16)
    low = (rest - mid.astype(F32)).astype(BF16)
    return high, mid, low


def weights_kernel(ids_ref, local_ref, *rest):
    part_refs, (out_ref, rows_ref) = rest[:-2], rest[-2:]
    width = out_ref.shape[1] // 2
    size = part_refs[0].shape[0]
    for index, part_ref in enumerate(part_refs):
        rows_ref[index * size : (index + 1) * size] = part_ref[...]

    @pl.loop(0, out_ref.shape[0] // 8, unroll=4)
    def _(group):
        prec, innov = [], []
        for inside in range(8):
            entry = group * 8 + inside
            row = rows_ref[pl.ds(ids_ref[entry], 1), :]
            prec.append(local_ref[entry] * row[:, :width])
            innov.append(row[:, width:])
        scale = jnp.sqrt(jnp.concatenate(prec, axis=0))
        first = pl.multiple_of(group * 8, 8)
        out_ref[pl.ds(first, 8), :width] = scale
        out_ref[pl.ds(first, 8), width:] = scale * jnp.concatenate(innov, axis=0)


def weights(ids, local, parts):
    smem = pl.BlockSpec(memory_space=pltpu.SMEM)
    vmem = pl.BlockSpec(memory_space=pltpu.VMEM)
    size, length = parts[0].shape
    return pl.pallas_call(
        weights_kernel,
        out_shape=jax.ShapeDtypeStruct((ids.shape[0], length), F32),
        in_specs=[smem, smem] + [vmem] * len(parts),
        out_specs=vmem,
        scratch_shapes=[pltpu.VMEM((len(parts) * size, length), F32)],
    )(ids, local, *parts)


def pick_kernel(layout, group_size, first_region, regions, ids_ref, scale_ref, *rest):
    shard_refs, (out_ref, table_ref) = rest[:-2], rest[-2:]
    width = table_ref.shape[2]
    slots = out_ref.shape[1] // regions
    for shard_ref, (start, size) in zip(shard_refs, layout):
        table_ref[start : start + size] = shard_ref[...]

    for member in range(out_ref.shape[0]):

        @pl.loop(0, regions)
        def _(region):
            first = (member * group_size + first_region + region) * slots
            first = pl.multiple_of(first, slots)
            scales = scale_ref[pl.ds(first, slots), :width]
            for slot in range(slots):
                values = table_ref[ids_ref[first + slot]].astype(F32)
                out_ref[member, region * slots + slot] = (
                    values * scales[slot : slot + 1]
                ).astype(BF16)


def pick(ids, scales, shards, mem_count, group_size, first_region, regions):
    slots = ids.shape[0] // (mem_count * group_size)
    layout = []
    total = 0
    for shard in shards:
        layout.append((total, shard.shape[0]))
        total += shard.shape[0]
    row, dtype = shards[0].shape[1:], shards[0].dtype
    entries = regions * slots
    size = row[0] * row[1]
    return pl.pallas_call(
        functools.partial(pick_kernel, layout, group_size, first_region, regions),
        out_shape=jax.ShapeDtypeStruct((mem_count, entries) + row, dtype),
        in_specs=[
            pl.BlockSpec(memory_space=pltpu.SMEM),
        ]
        + [pl.BlockSpec(memory_space=pltpu.VMEM)] * (1 + len(shards)),
        out_specs=pl.BlockSpec(memory_space=pltpu.VMEM),
        scratch_shapes=[pltpu.VMEM((total,) + row, dtype)],
        cost_estimate=pl.CostEstimate(
            flops=mem_count * entries * size,
            bytes_accessed=4 * (mem_count * entries + total) * size,
            transcendentals=0,
        ),
        compiler_params=pltpu.CompilerParams(vmem_limit_bytes=40 << 20),
    )(ids, scales, *shards)


def grid_cycle(outer, inner):
    cells = []
    for row in range(outer):
        columns = range(1, inner) if row % 2 == 0 else range(inner - 1, 0, -1)
        cells += [row * inner + column for column in columns]
    return cells + [row * inner for row in range(outer - 1, -1, -1)]


def row_stack(rows, count):
    length = rows[0].shape[1]
    which = lax.broadcasted_iota(jnp.int32, (count, length), 0)
    stack = jnp.zeros((count, length), F32)
    for index, row in enumerate(rows):
        stack = jnp.where(which == index, row.astype(F32), stack)
    return stack.astype(BF16)


def region_setup(
    region, first, prior_ref, column_ref, weight_ref, states_ref, obs_refs, scaled_ref,
    work_ref, lead_ref, mean_ref,
):
    members = prior_ref.shape[1]
    sources, members_dev = states_ref.shape[0], states_ref.shape[2]
    points = states_ref.shape[3]
    slots = obs_refs[0].shape[1] // prior_ref.shape[0]
    width = obs_refs[0].shape[3]
    for slot in range(slots):
        for source in range(sources):
            start = source * members_dev
            for obs_ref in obs_refs:
                stop = start + obs_ref.shape[2]
                scaled_ref[start:stop, slot * width : (slot + 1) * width] = (
                    obs_ref[source, region * slots + slot]
                )
                start = stop
    scaled = scaled_ref[...]
    gram = lax.dot_general(scaled, scaled, NT, preferred_element_type=F32)
    prior_row = prior_ref[pl.ds(region, 1), :]
    whole = 1.0 / jnp.sum(prior_row, axis=1, keepdims=True)
    share_row = prior_row * whole
    share_col = column_ref[region] * whole
    root_row = jnp.sqrt(members * share_row)
    root_col = jnp.sqrt(members * share_col)
    average = jnp.sum(
        jnp.dot(
            row_stack(split3(share_row), 16), scaled, preferred_element_type=F32
        ),
        axis=0, keepdims=True,
    )
    own = weight_ref[pl.ds(pl.multiple_of(first + region * slots, slots), slots), width:]
    innov = jnp.concatenate([own[slot : slot + 1] for slot in range(slots)], axis=1)
    sums = lax.dot_general(
        row_stack(split3(innov) + split3(average), 16), scaled, NT,
        preferred_element_type=F32,
    )
    kind = lax.broadcasted_iota(jnp.int32, (16, 2 * LANES), 0) // 3
    side = lax.broadcasted_iota(jnp.int32, (16, 2 * LANES), 1) // LANES
    spread = jnp.where(kind == side, 1.0, 0.0).astype(BF16)
    sums = sum(
        lax.dot_general(
            part, spread, (((0,), (0,)), ((), ())), preferred_element_type=F32
        )
        for part in split3(sums)
    )
    projection, left_col = sums[:, :LANES], sums[:, LANES:]
    total = jnp.sum(share_col * left_col, axis=0, keepdims=True)
    left_col = left_col - total
    vector = root_col * (
        projection - jnp.sum(share_col * projection, axis=0, keepdims=True)
    )
    lead_ref[region] = vector[:PANEL]
    carried = lax.broadcasted_iota(jnp.int32, (members, LANES), 1) < PANEL
    carried &= lax.broadcasted_iota(jnp.int32, (members, LANES), 0) >= PANEL
    for start in range(0, members, LANES):
        tile = slice(start, start + LANES)
        part = gram[:, tile]
        left_row = jnp.sum(share_col * part, axis=0, keepdims=True)
        system = root_col * ((part - left_row) - left_col) * root_row[:, tile]
        on_diag = lax.broadcasted_iota(jnp.int32, (members, LANES), 0) == (
            lax.broadcasted_iota(jnp.int32, (members, LANES), 1) + start
        )
        system = system + jnp.where(on_diag, (members - 1) / INFLATION, 0.0)
        if start == 0:
            system = jnp.where(carried, vector, system)
        work_ref[region, :, tile] = system
    for start in range(0, points, LANES):
        states = jnp.concatenate(
            [
                states_ref[source, region, :, start : start + LANES].astype(F32)
                for source in range(sources)
            ],
            axis=0,
        )
        mean = jnp.sum(share_col * states, axis=0, keepdims=True)
        mean_ref[region, :, start : start + LANES] = jnp.broadcast_to(mean, (8, LANES))
        work_ref[region, :, members + start : members + start + LANES] = root_col * (
            states - mean
        )


def reciprocal(value):
    guess = pl.reciprocal(value, approx=True)
    guess = guess * (2.0 - value * guess)
    return guess * (2.0 - value * guess)


def factor_diagonals(panel, chosen, work_ref):
    per_pack = LANES // PANEL
    start = panel * PANEL
    base, offset = start // LANES * LANES, start % LANES
    lane = lax.broadcasted_iota(jnp.int32, (8, LANES), 1)
    sub = lax.broadcasted_iota(jnp.int32, (8, LANES), 0)
    owner, column = lane // PANEL, lane % PANEL
    tiles = PANEL // 8
    packs = len(chosen)
    blocks = []
    for pack in chosen:
        pieces = []
        for tile in range(tiles):
            merged = None
            for place in range(per_pack):
                region = pack * per_pack + place
                raw = work_ref[
                    region, start + 8 * tile : start + 8 * tile + 8, base : base + LANES
                ]
                shift = (place * PANEL - offset) % LANES
                if shift:
                    raw = pltpu.roll(raw, shift, axis=1)
                merged = raw if merged is None else jnp.where(owner == place, raw, merged)
            pieces.append(merged)
        blocks.append(pieces)
    pivots = [[jnp.ones((8, LANES), F32) for _ in range(tiles)] for _ in range(packs)]
    for first in range(0, PANEL, GROUP):
        home = first // 8
        columns = [
            [
                {
                    tile: jnp.take_along_axis(
                        blocks[pack][tile], owner * PANEL + first + step,
                        axis=1, mode="promise_in_bounds",
                    )
                    for tile in range(home, tiles)
                }
                for step in range(GROUP)
            ]
            for pack in range(packs)
        ]
        second = {}
        for step in range(GROUP):
            inside = first % 8 + step
            at_step = column == first + step
            below = sub > inside
            for pack in range(packs):
                pieces = blocks[pack]
                if step % 2 == 0:
                    pivot = columns[pack][step][home][inside : inside + 1, :]
                    cross = columns[pack][step + 1][home][inside : inside + 1, :]
                    other = columns[pack][step + 1][home][inside + 1 : inside + 2, :]
                    product = pivot * other - cross * cross
                    inverse = reciprocal(pivot)
                    second[pack] = product * inverse, pivot * reciprocal(product)
                else:
                    pivot, inverse = second[pack]
                row = jnp.where(at_step[:1], 1.0, pieces[home][inside : inside + 1, :])
                pivots[pack][home] = jnp.where(sub == inside, pivot, pivots[pack][home])
                later = {
                    other: columns[pack][other][home][inside : inside + 1, :]
                    for other in range(step + 1, GROUP)
                }
                for tile in range(home, tiles):
                    ratio = columns[pack][step][tile] * inverse
                    cleared = at_step
                    if tile == home:
                        ratio = jnp.where(below, ratio, 0.0)
                        cleared = at_step & below
                    for other in later:
                        columns[pack][other][tile] = (
                            columns[pack][other][tile] - ratio * later[other]
                        )
                    pieces[tile] = jnp.where(cleared, 0.0, pieces[tile]) - ratio * row
    results = []
    for pack in range(packs):
        rows = []
        for tile in range(tiles):
            index = sub + 8 * tile
            lower = jnp.where(
                column < index, blocks[pack][tile], jnp.where(column == index, 1.0, 0.0)
            )
            rows.append(lower * lax.rsqrt(pivots[pack][tile]))
        results.append(jnp.concatenate(rows, axis=0))
    return results


def six_products(left, right, axis):
    high, mid, low = left
    left = jnp.concatenate([high, high, mid, mid, high, low], axis=axis)
    high, mid, low = right
    right = jnp.concatenate([high, mid, high, mid, low, high], axis=0)
    return lax.dot_general(
        left, right, (((axis,), (0,)), ((), ())), preferred_element_type=F32
    )


def eliminate(panel, pack, lower, work_ref, lead_ref, members):
    per_pack = LANES // PANEL
    start = panel * PANEL
    after = start + PANEL
    first = start // LANES * LANES
    kept = after // LANES * LANES
    owner = lax.broadcasted_iota(jnp.int32, (PANEL, LANES), 1) // PANEL

    def carry(region, rows, block):
        if start % LANES:
            return block
        if start == 0:
            source = lead_ref[region]
        else:
            source = work_ref[region, rows, first - LANES : first]
        lane = lax.broadcasted_iota(jnp.int32, source.shape, 1)
        head = jnp.where(lane < PANEL, source, block[:, :LANES])
        return jnp.concatenate([head, block[:, LANES:]], axis=1)

    spread = jnp.concatenate(
        [jnp.where(owner == place, lower, 0.0) for place in range(per_pack)], axis=0
    )
    here, rest = slice(start, after), slice(after, members)
    stacked = []
    for place in range(per_pack):
        region = pack * per_pack + place
        stacked.append(carry(region, here, work_ref[region, here, first:]))
    stacked = jnp.concatenate(stacked, axis=0)
    solved = six_products(split3(spread), split3(stacked), 1)
    for place in range(per_pack):
        region = pack * per_pack + place
        rows = solved[place * PANEL : (place + 1) * PANEL]
        work_ref[region, here, first : first + LANES] = rows[:, :LANES]
        work_ref[region, here, members:] = rows[:, members - first :]
        if after < members:
            parts = split3(rows)
            change = six_products(
                [part[:, kept - first : members - first] for part in parts], parts, 0
            )
            old = work_ref[region, rest, first:]
            if start:
                old = carry(region, rest, old)
            work_ref[region, rest, first:] = old - change[after - kept :]


def analysis_kernel(offsets, first_ref, prior_ref, column_ref, weight_ref, *rest):
    count = len(offsets)
    hbm_refs = rest[:count]
    out_ref, scaled_ref, work_ref, lead_ref, mean_ref, sems = rest[count : count + 6]
    vmem_refs = rest[count + 6 :]
    states_ref, obs_refs = vmem_refs[0], vmem_refs[1:]
    regions, members = prior_ref.shape
    sources, members_dev = states_ref.shape[0], states_ref.shape[2]
    points = states_ref.shape[3]
    packs = regions * PANEL // LANES
    ways = scaled_ref.shape[0]
    batches = sems.shape[0]
    batch_regions = regions // batches

    def loads(batch):
        copies = []
        for index, (hbm, vmem) in enumerate(zip(hbm_refs, vmem_refs)):
            size = vmem.shape[1] // batches
            copies.append(
                pltpu.make_async_copy(
                    hbm.at[:, pl.ds(offsets[index] + batch * size, size)],
                    vmem.at[:, pl.ds(batch * size, size)],
                    sems.at[batch, index],
                )
            )
        return copies

    for batch in range(batches):
        for copy in loads(batch):
            copy.start()

    @pl.loop(0, batches)
    def _(batch):
        for copy in loads(batch):
            copy.wait()

        @pl.loop(0, batch_regions // ways)
        def _(step):
            for way in range(ways):
                region_setup(
                    batch * batch_regions + step * ways + way, first_ref[0], prior_ref,
                    column_ref, weight_ref, states_ref, obs_refs, scaled_ref.at[way],
                    work_ref, lead_ref, mean_ref,
                )

    for panel in range(members // PANEL):
        lowers = factor_diagonals(panel, range(packs), work_ref)
        for pack in range(packs):
            eliminate(panel, pack, lowers[pack], work_ref, lead_ref, members)

    @pl.loop(0, regions)
    def _(region):
        moved = work_ref[region, :, members : members + points]
        solved = jnp.concatenate(
            [
                work_ref[region, start : start + LANES, start : start + 1]
                for start in range(0, members, LANES)
            ],
            axis=0,
        )
        shift = mean_ref[region, :1] + jnp.sum(solved * moved, axis=0, keepdims=True)
        result = (shift + jnp.sqrt(members - 1.0) * moved).astype(BF16)
        for source in range(sources):
            out_ref[source, region] = result[
                source * members_dev : (source + 1) * members_dev
            ]


def analyse(first, prior_rows, weight_rows, states, obs_parts, slots):
    regions, members = prior_rows.shape
    sources, _, members_dev, points = states[0].shape
    width = obs_parts[0][0].shape[3]
    vmem = pl.BlockSpec(memory_space=pltpu.VMEM)
    loaded = [states] + obs_parts
    sizes = [regions] + [regions * slots] * len(obs_parts)
    columns = jnp.broadcast_to(prior_rows[:, :, None], (regions, members, LANES))
    return pl.pallas_call(
        functools.partial(analysis_kernel, [offset for _, offset in loaded]),
        out_shape=jax.ShapeDtypeStruct((sources, regions, members_dev, points), BF16),
        in_specs=[pl.BlockSpec(memory_space=pltpu.SMEM), vmem, vmem, vmem]
        + [pl.BlockSpec(memory_space=pl.ANY)] * len(loaded),
        out_specs=vmem,
        scratch_shapes=[
            pltpu.VMEM((2, members, slots * width), BF16),
            pltpu.VMEM((regions, members, members + points), F32),
            pltpu.VMEM((regions, PANEL, LANES), F32),
            pltpu.VMEM((regions, 8, points), F32),
            pltpu.SemaphoreType.DMA((regions // 2, len(loaded))),
        ]
        + [
            pltpu.VMEM(array.shape[:1] + (size,) + array.shape[2:], array.dtype)
            for (array, _), size in zip(loaded, sizes)
        ],
        cost_estimate=pl.CostEstimate(
            flops=16 * regions * members * members * (slots * width + points),
            bytes_accessed=2 * regions * members * (slots * width + 2 * points),
            transcendentals=0,
        ),
        compiler_params=pltpu.CompilerParams(vmem_limit_bytes=48 << 20),
    )(first, prior_rows, columns, weight_rows, *[array for array, _ in loaded])


def body(
    ensemble_state, obs_ens, innovation, obs_prec, block_list, block_count, loc_weight, prior_weight
):
    spaces = lax.axis_size("space")
    mem_count = lax.axis_size("mem")
    members_dev, regions_dev, points = ensemble_state.shape
    blocks_dev, width = obs_ens.shape[1:]
    group_size = regions_dev // mem_count
    slots = block_list.shape[1]
    part = group_size // SPLIT
    first_row = lax.axis_index("mem") * group_size

    inner = 2 ** ((spaces.bit_length() - 1) // 2)
    cycle = grid_cycle(spaces // inner, inner)
    forward = [(cycle[k], cycle[(k + 1) % spaces]) for k in range(spaces)]
    backward = [(to, start) for start, to in forward]
    position = [cycle.index(space) for space in range(spaces)]
    half_way = spaces // 2
    across = [(cycle[k], cycle[(k + half_way) % spaces]) for k in range(spaces)]

    def place_of(space):
        return sum(
            jnp.where(space == index, position[index], 0) for index in range(spaces)
        )

    all_ids = block_list.reshape(regions_dev * slots)
    behind = place_of(lax.axis_index("space")) - place_of(all_ids // blocks_dev)
    places = (behind + spaces) % spaces * blocks_dev + all_ids % blocks_dev
    active = jnp.arange(slots, dtype=jnp.int32)[None, :] < block_count[:, None]
    local = jnp.where(active, loc_weight, 0.0).reshape(regions_dev * slots)
    waiting = []
    start = 0
    for share in CHUNKS:
        stop = start + members_dev // share
        waiting.append(jnp.transpose(obs_ens[start:stop], (1, 0, 2)))
        start = stop
    rows = jnp.concatenate([obs_prec, innovation], axis=1)
    rows_ahead, rows_back = [rows], [rows]

    def ring_step(step, ahead, back):
        if step < half_way - 1:
            return lax.ppermute(ahead, "space", forward), lax.ppermute(
                back, "space", backward
            )
        middle = blocks_dev // 2
        return (
            lax.ppermute(ahead[:middle], "space", forward),
            lax.ppermute(back[middle:], "space", backward),
        )

    def exchange(picked):
        return lax.all_to_all(picked, "mem", split_axis=0, concat_axis=0, tiled=True)

    running = []
    obs_parts = [[] for _ in range(SPLIT)]
    stage = 0
    due = {}
    while waiting or running:
        if waiting and (not running or running[-1]["step"] == half_way - 1):
            own = waiting.pop(0)
            running.append({"step": 0, "ahead": [own], "back": [own]})
        moved = [
            ring_step(ring["step"], ring["ahead"][-1], ring["back"][-1])
            for ring in running
        ]
        tied = {"moved": moved, "waiting": waiting, "due": due.pop(stage, None)}
        if stage < half_way - 1:
            tied["ahead"] = lax.ppermute(rows_ahead[-1], "space", forward)
            tied["back"] = lax.ppermute(rows_back[-1], "space", backward)
        if stage == 0:
            tied["across"] = lax.ppermute(rows, "space", across)
        if stage == 1:
            state, _ = lax.optimization_barrier((ensemble_state, tied["ahead"]))
            by_region = jnp.transpose(state, (1, 0, 2)).reshape(
                mem_count, group_size, members_dev, points
            )
            states = exchange(by_region)
        if stage == half_way - 1:
            tied["states"] = states
            tied["weights"] = weights(
                places, local, rows_ahead + [rows_across] + rows_back[:0:-1]
            )
        tied = lax.optimization_barrier(tied)
        waiting = tied["waiting"]
        for ring, (ahead, back) in zip(running, tied["moved"]):
            ring["ahead"].append(ahead)
            ring["back"].append(back)
            ring["step"] += 1
        if stage < half_way - 1:
            rows_ahead.append(tied["ahead"])
            rows_back.append(tied["back"])
        if stage == 0:
            rows_across = tied["across"]
        if stage == half_way - 1:
            latest = states = tied["states"]
            weight_rows = tied["weights"]
        if tied["due"] is not None:
            picked, _ = lax.optimization_barrier((tied["due"], latest))
            latest = exchange(picked)
            for index in range(SPLIT):
                obs_parts[index].append((latest, index * part * slots))
        if running[0]["step"] == half_way:
            ring = running.pop(0)
            shards = ring["ahead"] + ring["back"][:0:-1]
            if waiting or running:
                picked = pick(
                    places, weight_rows, shards, mem_count, group_size, 0, group_size
                )
                due[stage + 1] = picked
            else:
                for index in range(SPLIT):
                    picked = pick(
                        places, weight_rows, shards, mem_count, group_size,
                        index * part, part,
                    )
                    picked, _ = lax.optimization_barrier((picked, latest))
                    latest = exchange(picked)
                    obs_parts[index].append((latest, 0))
        stage += 1

    results = []
    for index in range(SPLIT):
        start = first_row + index * part
        if results:
            start, results[-1] = lax.optimization_barrier((start, results[-1]))
            results[-1] = exchange(results[-1])
        result = analyse(
            (start * slots).reshape(1),
            lax.dynamic_slice_in_dim(prior_weight, start, part, 0),
            weight_rows,
            (states, index * part),
            obs_parts[index],
            slots,
        )
        results.append(result)
    results[-1] = exchange(results[-1])
    back = jnp.concatenate(results, axis=1)
    return jnp.transpose(back.reshape(regions_dev, members_dev, points), (1, 0, 2))


def solution(mesh):
    return jax.shard_map(
        body,
        mesh=mesh,
        in_specs=(
            P("mem", "space", None),
            P("mem", "space", None),
            P("space", None),
            P("space", None),
            P("space", None),
            P("space"),
            P("space", None),
            P("space", None),
        ),
        out_specs=P("mem", "space", None),
        check_vma=False,
    )
```

```python
import functools

import jax
import jax.numpy as jnp
from jax import lax
from jax.experimental import pallas as pl
from jax.experimental.pallas import tpu as pltpu
from jax.sharding import PartitionSpec as P

INFLATION = 1.1
PANEL = 32
GROUP = 8
LANES = 128
CHUNKS = (2, 2)
SPLIT = 2
F32 = jnp.float32
BF16 = jnp.bfloat16
NT = (((1,), (1,)), ((), ()))


def split3(value):
    high = value.astype(BF16)
    rest = value - high.astype(F32)
    mid = rest.astype(BF16)
    low = (rest - mid.astype(F32)).astype(BF16)
    return high, mid, low


def weights_kernel(ids_ref, local_ref, *rest):
    part_refs, (out_ref, rows_ref) = rest[:-2], rest[-2:]
    width = out_ref.shape[1] // 2
    size = part_refs[0].shape[0]
    for index, part_ref in enumerate(part_refs):
        rows_ref[index * size : (index + 1) * size] = part_ref[...]

    @pl.loop(0, out_ref.shape[0] // 8, unroll=4)
    def _(group):
        prec, innov = [], []
        for inside in range(8):
            entry = group * 8 + inside
            row = rows_ref[pl.ds(ids_ref[entry], 1), :]
            prec.append(local_ref[entry] * row[:, :width])
            innov.append(row[:, width:])
        scale = jnp.sqrt(jnp.concatenate(prec, axis=0))
        first = pl.multiple_of(group * 8, 8)
        out_ref[pl.ds(first, 8), :width] = scale
        out_ref[pl.ds(first, 8), width:] = scale * jnp.concatenate(innov, axis=0)


def weights(ids, local, parts):
    smem = pl.BlockSpec(memory_space=pltpu.SMEM)
    vmem = pl.BlockSpec(memory_space=pltpu.VMEM)
    size, length = parts[0].shape
    return pl.pallas_call(
        weights_kernel,
        out_shape=jax.ShapeDtypeStruct((ids.shape[0], length), F32),
        in_specs=[smem, smem] + [vmem] * len(parts),
        out_specs=vmem,
        scratch_shapes=[pltpu.VMEM((len(parts) * size, length), F32)],
    )(ids, local, *parts)


def pick_kernel(layout, group_size, first_region, regions, ids_ref, scale_ref, *rest):
    shard_refs, (out_ref, table_ref) = rest[:-2], rest[-2:]
    width = table_ref.shape[2]
    slots = out_ref.shape[1] // regions
    for shard_ref, (start, size) in zip(shard_refs, layout):
        table_ref[start : start + size] = shard_ref[...]

    for member in range(out_ref.shape[0]):

        @pl.loop(0, regions)
        def _(region):
            first = (member * group_size + first_region + region) * slots
            first = pl.multiple_of(first, slots)
            scales = scale_ref[pl.ds(first, slots), :width]
            for slot in range(slots):
                values = table_ref[ids_ref[first + slot]].astype(F32)
                out_ref[member, region * slots + slot] = (
                    values * scales[slot : slot + 1]
                ).astype(BF16)


def pick(ids, scales, shards, mem_count, group_size, first_region, regions):
    slots = ids.shape[0] // (mem_count * group_size)
    layout = []
    total = 0
    for shard in shards:
        layout.append((total, shard.shape[0]))
        total += shard.shape[0]
    row, dtype = shards[0].shape[1:], shards[0].dtype
    entries = regions * slots
    size = row[0] * row[1]
    return pl.pallas_call(
        functools.partial(pick_kernel, layout, group_size, first_region, regions),
        out_shape=jax.ShapeDtypeStruct((mem_count, entries) + row, dtype),
        in_specs=[
            pl.BlockSpec(memory_space=pltpu.SMEM),
        ]
        + [pl.BlockSpec(memory_space=pltpu.VMEM)] * (1 + len(shards)),
        out_specs=pl.BlockSpec(memory_space=pltpu.VMEM),
        scratch_shapes=[pltpu.VMEM((total,) + row, dtype)],
        cost_estimate=pl.CostEstimate(
            flops=mem_count * entries * size,
            bytes_accessed=4 * (mem_count * entries + total) * size,
            transcendentals=0,
        ),
        compiler_params=pltpu.CompilerParams(vmem_limit_bytes=24 << 20),
    )(ids, scales, *shards)


def grid_cycle(outer, inner):
    cells = []
    for row in range(outer):
        columns = range(1, inner) if row % 2 == 0 else range(inner - 1, 0, -1)
        cells += [row * inner + column for column in columns]
    return cells + [row * inner for row in range(outer - 1, -1, -1)]


def row_stack(rows, count):
    length = rows[0].shape[1]
    which = lax.broadcasted_iota(jnp.int32, (count, length), 0)
    stack = jnp.zeros((count, length), F32)
    for index, row in enumerate(rows):
        stack = jnp.where(which == index, row.astype(F32), stack)
    return stack.astype(BF16)


def region_setup(
    region, first, prior_ref, column_ref, weight_ref, states_ref, obs_refs, scaled_ref,
    work_ref, lead_ref, mean_ref,
):
    members = prior_ref.shape[1]
    sources, members_dev = states_ref.shape[0], states_ref.shape[2]
    points = states_ref.shape[3]
    slots = obs_refs[0].shape[1] // prior_ref.shape[0]
    width = obs_refs[0].shape[3]
    for slot in range(slots):
        for source in range(sources):
            start = source * members_dev
            for obs_ref in obs_refs:
                stop = start + obs_ref.shape[2]
                scaled_ref[start:stop, slot * width : (slot + 1) * width] = (
                    obs_ref[source, region * slots + slot]
                )
                start = stop
    scaled = scaled_ref[...]
    gram = lax.dot_general(scaled, scaled, NT, preferred_element_type=F32)
    prior_row = prior_ref[pl.ds(region, 1), :]
    whole = 1.0 / jnp.sum(prior_row, axis=1, keepdims=True)
    share_row = prior_row * whole
    share_col = column_ref[region] * whole
    root_row = jnp.sqrt(members * share_row)
    root_col = jnp.sqrt(members * share_col)
    average = jnp.sum(
        jnp.dot(
            row_stack(split3(share_row), 16), scaled, preferred_element_type=F32
        ),
        axis=0, keepdims=True,
    )
    own = weight_ref[pl.ds(pl.multiple_of(first + region * slots, slots), slots), width:]
    innov = jnp.concatenate([own[slot : slot + 1] for slot in range(slots)], axis=1)
    sums = lax.dot_general(
        scaled, row_stack(split3(innov) + split3(average), 16), NT,
        preferred_element_type=F32,
    )
    kind = lax.broadcasted_iota(jnp.int32, (16, 2 * LANES), 0) // 3
    side = lax.broadcasted_iota(jnp.int32, (16, 2 * LANES), 1) // LANES
    spread = jnp.where(kind == side, 1.0, 0.0).astype(BF16)
    sums = sum(
        jnp.dot(part, spread, preferred_element_type=F32) for part in split3(sums)
    )
    projection, left_col = sums[:, :LANES], sums[:, LANES:]
    total = jnp.sum(share_col * left_col, axis=0, keepdims=True)
    left_col = left_col - total
    vector = root_col * (
        projection - jnp.sum(share_col * projection, axis=0, keepdims=True)
    )
    lead_ref[region] = vector[:PANEL]
    carried = lax.broadcasted_iota(jnp.int32, (members, LANES), 1) < PANEL
    carried &= lax.broadcasted_iota(jnp.int32, (members, LANES), 0) >= PANEL
    for start in range(0, members, LANES):
        tile = slice(start, start + LANES)
        part = gram[:, tile]
        left_row = jnp.sum(share_col * part, axis=0, keepdims=True)
        system = root_col * ((part - left_row) - left_col) * root_row[:, tile]
        on_diag = lax.broadcasted_iota(jnp.int32, (members, LANES), 0) == (
            lax.broadcasted_iota(jnp.int32, (members, LANES), 1) + start
        )
        system = system + jnp.where(on_diag, (members - 1) / INFLATION, 0.0)
        if start == 0:
            system = jnp.where(carried, vector, system)
        work_ref[region, :, tile] = system
    for start in range(0, points, LANES):
        states = jnp.concatenate(
            [
                states_ref[source, region, :, start : start + LANES].astype(F32)
                for source in range(sources)
            ],
            axis=0,
        )
        mean = jnp.sum(share_col * states, axis=0, keepdims=True)
        mean_ref[region, :, start : start + LANES] = jnp.broadcast_to(mean, (8, LANES))
        work_ref[region, :, members + start : members + start + LANES] = root_col * (
            states - mean
        )


def reciprocal(value):
    guess = pl.reciprocal(value, approx=True)
    guess = guess * (2.0 - value * guess)
    return guess * (2.0 - value * guess)


def factor_diagonals(panel, chosen, work_ref):
    per_pack = LANES // PANEL
    start = panel * PANEL
    base, offset = start // LANES * LANES, start % LANES
    lane = lax.broadcasted_iota(jnp.int32, (8, LANES), 1)
    sub = lax.broadcasted_iota(jnp.int32, (8, LANES), 0)
    owner, column = lane // PANEL, lane % PANEL
    tiles = PANEL // 8
    packs = len(chosen)
    blocks = []
    for pack in chosen:
        pieces = []
        for tile in range(tiles):
            merged = None
            for place in range(per_pack):
                region = pack * per_pack + place
                raw = work_ref[
                    region, start + 8 * tile : start + 8 * tile + 8, base : base + LANES
                ]
                shift = (place * PANEL - offset) % LANES
                if shift:
                    raw = pltpu.roll(raw, shift, axis=1)
                merged = raw if merged is None else jnp.where(owner == place, raw, merged)
            pieces.append(merged)
        blocks.append(pieces)
    pivots = [[jnp.ones((8, LANES), F32) for _ in range(tiles)] for _ in range(packs)]
    for first in range(0, PANEL, GROUP):
        home = first // 8
        columns = [
            [
                {
                    tile: jnp.take_along_axis(
                        blocks[pack][tile], owner * PANEL + first + step,
                        axis=1, mode="promise_in_bounds",
                    )
                    for tile in range(home, tiles)
                }
                for step in range(GROUP)
            ]
            for pack in range(packs)
        ]
        second = {}
        for step in range(GROUP):
            inside = first % 8 + step
            at_step = column == first + step
            below = sub > inside
            for pack in range(packs):
                pieces = blocks[pack]
                if step % 2 == 0:
                    pivot = columns[pack][step][home][inside : inside + 1, :]
                    cross = columns[pack][step + 1][home][inside : inside + 1, :]
                    other = columns[pack][step + 1][home][inside + 1 : inside + 2, :]
                    product = pivot * other - cross * cross
                    inverse = reciprocal(pivot)
                    second[pack] = product * inverse, pivot * reciprocal(product)
                else:
                    pivot, inverse = second[pack]
                row = jnp.where(at_step[:1], 1.0, pieces[home][inside : inside + 1, :])
                pivots[pack][home] = jnp.where(sub == inside, pivot, pivots[pack][home])
                later = {
                    other: columns[pack][other][home][inside : inside + 1, :]
                    for other in range(step + 1, GROUP)
                }
                for tile in range(home, tiles):
                    ratio = columns[pack][step][tile] * inverse
                    cleared = at_step
                    if tile == home:
                        ratio = jnp.where(below, ratio, 0.0)
                        cleared = at_step & below
                    for other in later:
                        columns[pack][other][tile] = (
                            columns[pack][other][tile] - ratio * later[other]
                        )
                    pieces[tile] = jnp.where(cleared, 0.0, pieces[tile]) - ratio * row
    results = []
    for pack in range(packs):
        rows = []
        for tile in range(tiles):
            index = sub + 8 * tile
            lower = jnp.where(
                column < index, blocks[pack][tile], jnp.where(column == index, 1.0, 0.0)
            )
            rows.append(lower * lax.rsqrt(pivots[pack][tile]))
        results.append(jnp.concatenate(rows, axis=0))
    return results


def six_products(left, right, axis):
    high, mid, low = left
    left = jnp.concatenate([high, high, mid, mid, high, low], axis=axis)
    high, mid, low = right
    right = jnp.concatenate([high, mid, high, mid, low, high], axis=0)
    return lax.dot_general(
        left, right, (((axis,), (0,)), ((), ())), preferred_element_type=F32
    )


def eliminate(panel, pack, lower, work_ref, lead_ref, members):
    per_pack = LANES // PANEL
    start = panel * PANEL
    after = start + PANEL
    first = start // LANES * LANES
    kept = after // LANES * LANES
    owner = lax.broadcasted_iota(jnp.int32, (PANEL, LANES), 1) // PANEL

    def carry(region, rows, block):
        if start % LANES:
            return block
        if start == 0:
            source = lead_ref[region]
        else:
            source = work_ref[region, rows, first - LANES : first]
        lane = lax.broadcasted_iota(jnp.int32, source.shape, 1)
        head = jnp.where(lane < PANEL, source, block[:, :LANES])
        return jnp.concatenate([head, block[:, LANES:]], axis=1)

    spread = jnp.concatenate(
        [jnp.where(owner == place, lower, 0.0) for place in range(per_pack)], axis=0
    )
    here, rest = slice(start, after), slice(after, members)
    stacked = []
    for place in range(per_pack):
        region = pack * per_pack + place
        stacked.append(carry(region, here, work_ref[region, here, first:]))
    stacked = jnp.concatenate(stacked, axis=0)
    solved = six_products(split3(spread), split3(stacked), 1)
    for place in range(per_pack):
        region = pack * per_pack + place
        rows = solved[place * PANEL : (place + 1) * PANEL]
        work_ref[region, here, first : first + LANES] = rows[:, :LANES]
        work_ref[region, here, members:] = rows[:, members - first :]
        if after < members:
            parts = split3(rows)
            change = six_products(
                [part[:, kept - first : members - first] for part in parts], parts, 0
            )
            old = work_ref[region, rest, first:]
            if start:
                old = carry(region, rest, old)
            work_ref[region, rest, first:] = old - change[after - kept :]


def analysis_kernel(offsets, first_ref, prior_ref, column_ref, weight_ref, *rest):
    count = len(offsets)
    hbm_refs = rest[:count]
    out_ref, scaled_ref, work_ref, lead_ref, mean_ref, sems = rest[count : count + 6]
    vmem_refs = rest[count + 6 :]
    states_ref, obs_refs = vmem_refs[0], vmem_refs[1:]
    regions, members = prior_ref.shape
    sources, members_dev = states_ref.shape[0], states_ref.shape[2]
    points = states_ref.shape[3]
    packs = regions * PANEL // LANES
    ways = scaled_ref.shape[0]
    batches = sems.shape[0]
    batch_regions = regions // batches

    def loads(batch):
        copies = []
        for index, (hbm, vmem) in enumerate(zip(hbm_refs, vmem_refs)):
            size = vmem.shape[1] // batches
            copies.append(
                pltpu.make_async_copy(
                    hbm.at[:, pl.ds(offsets[index] + batch * size, size)],
                    vmem.at[:, pl.ds(batch * size, size)],
                    sems.at[batch, index],
                )
            )
        return copies

    for batch in range(batches):
        for copy in loads(batch):
            copy.start()

    @pl.loop(0, batches)
    def _(batch):
        for copy in loads(batch):
            copy.wait()

        @pl.loop(0, batch_regions // ways)
        def _(step):
            for way in range(ways):
                region_setup(
                    batch * batch_regions + step * ways + way, first_ref[0], prior_ref,
                    column_ref, weight_ref, states_ref, obs_refs, scaled_ref.at[way],
                    work_ref, lead_ref, mean_ref,
                )

    for panel in range(members // PANEL):
        lowers = factor_diagonals(panel, range(packs), work_ref)
        for pack in range(packs):
            eliminate(panel, pack, lowers[pack], work_ref, lead_ref, members)

    @pl.loop(0, regions)
    def _(region):
        moved = work_ref[region, :, members : members + points]
        solved = jnp.concatenate(
            [
                work_ref[region, start : start + LANES, start : start + 1]
                for start in range(0, members, LANES)
            ],
            axis=0,
        )
        shift = mean_ref[region, :1] + jnp.sum(solved * moved, axis=0, keepdims=True)
        result = (shift + jnp.sqrt(members - 1.0) * moved).astype(BF16)
        for source in range(sources):
            out_ref[source, region] = result[
                source * members_dev : (source + 1) * members_dev
            ]


def analyse(first, prior_rows, weight_rows, states, obs_parts, slots):
    regions, members = prior_rows.shape
    sources, _, members_dev, points = states[0].shape
    width = obs_parts[0][0].shape[3]
    vmem = pl.BlockSpec(memory_space=pltpu.VMEM)
    loaded = [states] + obs_parts
    sizes = [regions] + [regions * slots] * len(obs_parts)
    columns = jnp.broadcast_to(prior_rows[:, :, None], (regions, members, LANES))
    return pl.pallas_call(
        functools.partial(analysis_kernel, [offset for _, offset in loaded]),
        out_shape=jax.ShapeDtypeStruct((sources, regions, members_dev, points), BF16),
        in_specs=[pl.BlockSpec(memory_space=pltpu.SMEM), vmem, vmem, vmem]
        + [pl.BlockSpec(memory_space=pl.ANY)] * len(loaded),
        out_specs=vmem,
        scratch_shapes=[
            pltpu.VMEM((2, members, slots * width), BF16),
            pltpu.VMEM((regions, members, members + points), F32),
            pltpu.VMEM((regions, PANEL, LANES), F32),
            pltpu.VMEM((regions, 8, points), F32),
            pltpu.SemaphoreType.DMA((regions // 2, len(loaded))),
        ]
        + [
            pltpu.VMEM(array.shape[:1] + (size,) + array.shape[2:], array.dtype)
            for (array, _), size in zip(loaded, sizes)
        ],
        cost_estimate=pl.CostEstimate(
            flops=16 * regions * members * members * (slots * width + points),
            bytes_accessed=2 * regions * members * (slots * width + 2 * points),
            transcendentals=0,
        ),
        compiler_params=pltpu.CompilerParams(vmem_limit_bytes=48 << 20),
    )(first, prior_rows, columns, weight_rows, *[array for array, _ in loaded])


def body(
    ensemble_state, obs_ens, innovation, obs_prec, block_list, block_count, loc_weight, prior_weight
):
    spaces = lax.axis_size("space")
    mem_count = lax.axis_size("mem")
    members_dev, regions_dev, points = ensemble_state.shape
    blocks_dev, width = obs_ens.shape[1:]
    group_size = regions_dev // mem_count
    slots = block_list.shape[1]
    part = group_size // SPLIT
    first_row = lax.axis_index("mem") * group_size

    inner = 2 ** ((spaces.bit_length() - 1) // 2)
    cycle = grid_cycle(spaces // inner, inner)
    forward = [(cycle[k], cycle[(k + 1) % spaces]) for k in range(spaces)]
    backward = [(to, start) for start, to in forward]
    position = [cycle.index(space) for space in range(spaces)]
    half_way = spaces // 2
    across = [(cycle[k], cycle[(k + half_way) % spaces]) for k in range(spaces)]

    def place_of(space):
        return sum(
            jnp.where(space == index, position[index], 0) for index in range(spaces)
        )

    all_ids = block_list.reshape(regions_dev * slots)
    behind = place_of(lax.axis_index("space")) - place_of(all_ids // blocks_dev)
    places = (behind + spaces) % spaces * blocks_dev + all_ids % blocks_dev
    active = jnp.arange(slots, dtype=jnp.int32)[None, :] < block_count[:, None]
    local = jnp.where(active, loc_weight, 0.0).reshape(regions_dev * slots)
    waiting = []
    start = 0
    for share in CHUNKS:
        stop = start + members_dev // share
        waiting.append(jnp.transpose(obs_ens[start:stop], (1, 0, 2)))
        start = stop
    rows = jnp.concatenate([obs_prec, innovation], axis=1)
    rows_ahead, rows_back = [rows], [rows]
    by_region = jnp.transpose(ensemble_state, (1, 0, 2)).reshape(
        mem_count, group_size, members_dev, points
    )

    def ring_step(step, ahead, back):
        if step < half_way - 1:
            return lax.ppermute(ahead, "space", forward), lax.ppermute(
                back, "space", backward
            )
        middle = blocks_dev // 2
        return (
            lax.ppermute(ahead[:middle], "space", forward),
            lax.ppermute(back[middle:], "space", backward),
        )

    def exchange(picked):
        return lax.all_to_all(picked, "mem", split_axis=0, concat_axis=0, tiled=True)

    running = []
    obs_parts = [[] for _ in range(SPLIT)]
    stage = 0
    due = {}
    while waiting or running:
        if waiting and not running:
            own = waiting.pop(0)
            running.append({"step": 0, "ahead": [own], "back": [own]})
        moved = [
            ring_step(ring["step"], ring["ahead"][-1], ring["back"][-1])
            for ring in running
        ]
        tied = {"moved": moved, "waiting": waiting, "due": due.pop(stage, None)}
        if stage < half_way - 1:
            tied["ahead"] = lax.ppermute(rows_ahead[-1], "space", forward)
            tied["back"] = lax.ppermute(rows_back[-1], "space", backward)
        if stage == 0:
            tied["across"] = lax.ppermute(rows, "space", across)
            tied["by_region"] = by_region
        if stage == half_way - 1:
            tied["states"] = states
            tied["weights"] = weights(
                places, local, rows_ahead + [rows_across] + rows_back[:0:-1]
            )
        tied = lax.optimization_barrier(tied)
        waiting = tied["waiting"]
        for ring, (ahead, back) in zip(running, tied["moved"]):
            ring["ahead"].append(ahead)
            ring["back"].append(back)
            ring["step"] += 1
        if stage < half_way - 1:
            rows_ahead.append(tied["ahead"])
            rows_back.append(tied["back"])
        if stage == 0:
            rows_across = tied["across"]
            states = exchange(tied["by_region"])
        if stage == half_way - 1:
            latest = states = tied["states"]
            weight_rows = tied["weights"]
        if tied["due"] is not None:
            picked, _ = lax.optimization_barrier((tied["due"], latest))
            latest = exchange(picked)
            for index in range(SPLIT):
                obs_parts[index].append((latest, index * part * slots))
        if running[0]["step"] == half_way:
            ring = running.pop(0)
            shards = ring["ahead"] + ring["back"][:0:-1]
            if waiting or running:
                picked = pick(
                    places, weight_rows, shards, mem_count, group_size, 0, group_size
                )
                due[stage + 1] = picked
            else:
                for index in range(SPLIT):
                    picked = pick(
                        places, weight_rows, shards, mem_count, group_size,
                        index * part, part,
                    )
                    picked, _ = lax.optimization_barrier((picked, latest))
                    latest = exchange(picked)
                    obs_parts[index].append((latest, 0))
        stage += 1

    results = []
    for index in range(SPLIT):
        start = first_row + index * part
        if results:
            start, results[-1] = lax.optimization_barrier((start, results[-1]))
            results[-1] = exchange(results[-1])
        result = analyse(
            (start * slots).reshape(1),
            lax.dynamic_slice_in_dim(prior_weight, start, part, 0),
            weight_rows,
            (states, index * part),
            obs_parts[index],
            slots,
        )
        results.append(result)
    results[-1] = exchange(results[-1])
    back = jnp.concatenate(results, axis=1)
    return jnp.transpose(back.reshape(regions_dev, members_dev, points), (1, 0, 2))


def solution(mesh):
    return jax.shard_map(
        body,
        mesh=mesh,
        in_specs=(
            P("mem", "space", None),
            P("mem", "space", None),
            P("space", None),
            P("space", None),
            P("space", None),
            P("space"),
            P("space", None),
            P("space", None),
        ),
        out_specs=P("mem", "space", None),
        check_vma=False,
    )
```

```python
import functools

import jax
import jax.numpy as jnp
from jax import lax
from jax.experimental import pallas as pl
from jax.experimental.pallas import tpu as pltpu
from jax.sharding import PartitionSpec as P

INFLATION = 1.1
PANEL = 32
GROUP = 8
LANES = 128
CHUNKS = (2, 2)
SPLIT = 2
F32 = jnp.float32
BF16 = jnp.bfloat16
NT = (((1,), (1,)), ((), ()))


def split3(value):
    high = value.astype(BF16)
    rest = value - high.astype(F32)
    mid = rest.astype(BF16)
    low = (rest - mid.astype(F32)).astype(BF16)
    return high, mid, low


def weights_kernel(ids_ref, local_ref, *rest):
    part_refs, (out_ref, rows_ref) = rest[:-2], rest[-2:]
    width = out_ref.shape[1] // 2
    size = part_refs[0].shape[0]
    for index, part_ref in enumerate(part_refs):
        rows_ref[index * size : (index + 1) * size] = part_ref[...]

    @pl.loop(0, out_ref.shape[0] // 8, unroll=4)
    def _(group):
        prec, innov = [], []
        for inside in range(8):
            entry = group * 8 + inside
            row = rows_ref[pl.ds(ids_ref[entry], 1), :]
            prec.append(local_ref[entry] * row[:, :width])
            innov.append(row[:, width:])
        scale = jnp.sqrt(jnp.concatenate(prec, axis=0))
        first = pl.multiple_of(group * 8, 8)
        out_ref[pl.ds(first, 8), :width] = scale
        out_ref[pl.ds(first, 8), width:] = scale * jnp.concatenate(innov, axis=0)


def weights(ids, local, parts):
    smem = pl.BlockSpec(memory_space=pltpu.SMEM)
    vmem = pl.BlockSpec(memory_space=pltpu.VMEM)
    size, length = parts[0].shape
    return pl.pallas_call(
        weights_kernel,
        out_shape=jax.ShapeDtypeStruct((ids.shape[0], length), F32),
        in_specs=[smem, smem] + [vmem] * len(parts),
        out_specs=vmem,
        scratch_shapes=[pltpu.VMEM((len(parts) * size, length), F32)],
    )(ids, local, *parts)


def pick_kernel(layout, group_size, first_region, regions, ids_ref, scale_ref, *rest):
    shard_refs, (out_ref, table_ref) = rest[:-2], rest[-2:]
    width = table_ref.shape[2]
    slots = out_ref.shape[1] // regions
    for shard_ref, (start, size) in zip(shard_refs, layout):
        table_ref[start : start + size] = shard_ref[...]

    for member in range(out_ref.shape[0]):

        @pl.loop(0, regions)
        def _(region):
            first = (member * group_size + first_region + region) * slots
            first = pl.multiple_of(first, slots)
            scales = scale_ref[pl.ds(first, slots), :width]
            for slot in range(slots):
                values = table_ref[ids_ref[first + slot]].astype(F32)
                out_ref[member, region * slots + slot] = (
                    values * scales[slot : slot + 1]
                ).astype(BF16)


def pick(ids, scales, shards, mem_count, group_size, first_region, regions):
    slots = ids.shape[0] // (mem_count * group_size)
    layout = []
    total = 0
    for shard in shards:
        layout.append((total, shard.shape[0]))
        total += shard.shape[0]
    row, dtype = shards[0].shape[1:], shards[0].dtype
    entries = regions * slots
    size = row[0] * row[1]
    return pl.pallas_call(
        functools.partial(pick_kernel, layout, group_size, first_region, regions),
        out_shape=jax.ShapeDtypeStruct((mem_count, entries) + row, dtype),
        in_specs=[
            pl.BlockSpec(memory_space=pltpu.SMEM),
        ]
        + [pl.BlockSpec(memory_space=pltpu.VMEM)] * (1 + len(shards)),
        out_specs=pl.BlockSpec(memory_space=pltpu.VMEM),
        scratch_shapes=[pltpu.VMEM((total,) + row, dtype)],
        cost_estimate=pl.CostEstimate(
            flops=mem_count * entries * size,
            bytes_accessed=4 * (mem_count * entries + total) * size,
            transcendentals=0,
        ),
        compiler_params=pltpu.CompilerParams(vmem_limit_bytes=24 << 20),
    )(ids, scales, *shards)


def grid_cycle(outer, inner):
    cells = []
    for row in range(outer):
        columns = range(1, inner) if row % 2 == 0 else range(inner - 1, 0, -1)
        cells += [row * inner + column for column in columns]
    return cells + [row * inner for row in range(outer - 1, -1, -1)]


def row_stack(rows, count):
    length = rows[0].shape[1]
    which = lax.broadcasted_iota(jnp.int32, (count, length), 0)
    stack = jnp.zeros((count, length), F32)
    for index, row in enumerate(rows):
        stack = jnp.where(which == index, row.astype(F32), stack)
    return stack.astype(BF16)


def region_setup(
    region, first, prior_ref, column_ref, weight_ref, states_ref, obs_refs, scaled_ref,
    work_ref, lead_ref, mean_ref,
):
    members = prior_ref.shape[1]
    sources, members_dev = states_ref.shape[0], states_ref.shape[2]
    points = states_ref.shape[3]
    slots = obs_refs[0].shape[1] // prior_ref.shape[0]
    width = obs_refs[0].shape[3]
    for slot in range(slots):
        for source in range(sources):
            start = source * members_dev
            for obs_ref in obs_refs:
                stop = start + obs_ref.shape[2]
                scaled_ref[start:stop, slot * width : (slot + 1) * width] = (
                    obs_ref[source, region * slots + slot]
                )
                start = stop
    scaled = scaled_ref[...]
    gram = lax.dot_general(scaled, scaled, NT, preferred_element_type=F32)
    prior_row = prior_ref[pl.ds(region, 1), :]
    whole = 1.0 / jnp.sum(prior_row, axis=1, keepdims=True)
    share_row = prior_row * whole
    share_col = column_ref[region] * whole
    root_row = jnp.sqrt(members * share_row)
    root_col = jnp.sqrt(members * share_col)
    average = jnp.sum(
        jnp.dot(
            row_stack(split3(share_row), 16), scaled, preferred_element_type=F32
        ),
        axis=0, keepdims=True,
    )
    own = weight_ref[pl.ds(pl.multiple_of(first + region * slots, slots), slots), width:]
    innov = jnp.concatenate([own[slot : slot + 1] for slot in range(slots)], axis=1)
    sums = lax.dot_general(
        scaled, row_stack(split3(innov) + split3(average), 16), NT,
        preferred_element_type=F32,
    )
    kind = lax.broadcasted_iota(jnp.int32, (16, 2 * LANES), 0) // 3
    side = lax.broadcasted_iota(jnp.int32, (16, 2 * LANES), 1) // LANES
    spread = jnp.where(kind == side, 1.0, 0.0).astype(BF16)
    sums = sum(
        jnp.dot(part, spread, preferred_element_type=F32) for part in split3(sums)
    )
    projection, left_col = sums[:, :LANES], sums[:, LANES:]
    total = jnp.sum(share_col * left_col, axis=0, keepdims=True)
    left_col = left_col - total
    vector = root_col * (
        projection - jnp.sum(share_col * projection, axis=0, keepdims=True)
    )
    lead_ref[region] = vector[:PANEL]
    carried = lax.broadcasted_iota(jnp.int32, (members, LANES), 1) < PANEL
    carried &= lax.broadcasted_iota(jnp.int32, (members, LANES), 0) >= PANEL
    for start in range(0, members, LANES):
        tile = slice(start, start + LANES)
        part = gram[:, tile]
        left_row = jnp.sum(share_col * part, axis=0, keepdims=True)
        system = root_col * ((part - left_row) - left_col) * root_row[:, tile]
        on_diag = lax.broadcasted_iota(jnp.int32, (members, LANES), 0) == (
            lax.broadcasted_iota(jnp.int32, (members, LANES), 1) + start
        )
        system = system + jnp.where(on_diag, (members - 1) / INFLATION, 0.0)
        if start == 0:
            system = jnp.where(carried, vector, system)
        work_ref[region, :, tile] = system
    for start in range(0, points, LANES):
        states = jnp.concatenate(
            [
                states_ref[source, region, :, start : start + LANES].astype(F32)
                for source in range(sources)
            ],
            axis=0,
        )
        mean = jnp.sum(share_col * states, axis=0, keepdims=True)
        mean_ref[region, :, start : start + LANES] = jnp.broadcast_to(mean, (8, LANES))
        work_ref[region, :, members + start : members + start + LANES] = root_col * (
            states - mean
        )


def reciprocal(value):
    guess = pl.reciprocal(value, approx=True)
    guess = guess * (2.0 - value * guess)
    return guess * (2.0 - value * guess)


def factor_diagonals(panel, chosen, work_ref):
    per_pack = LANES // PANEL
    start = panel * PANEL
    base, offset = start // LANES * LANES, start % LANES
    lane = lax.broadcasted_iota(jnp.int32, (8, LANES), 1)
    sub = lax.broadcasted_iota(jnp.int32, (8, LANES), 0)
    owner, column = lane // PANEL, lane % PANEL
    tiles = PANEL // 8
    packs = len(chosen)
    blocks = []
    for pack in chosen:
        pieces = []
        for tile in range(tiles):
            merged = None
            for place in range(per_pack):
                region = pack * per_pack + place
                raw = work_ref[
                    region, start + 8 * tile : start + 8 * tile + 8, base : base + LANES
                ]
                shift = (place * PANEL - offset) % LANES
                if shift:
                    raw = pltpu.roll(raw, shift, axis=1)
                merged = raw if merged is None else jnp.where(owner == place, raw, merged)
            pieces.append(merged)
        blocks.append(pieces)
    pivots = [[jnp.ones((8, LANES), F32) for _ in range(tiles)] for _ in range(packs)]
    for first in range(0, PANEL, GROUP):
        home = first // 8
        columns = [
            [
                {
                    tile: jnp.take_along_axis(
                        blocks[pack][tile], owner * PANEL + first + step,
                        axis=1, mode="promise_in_bounds",
                    )
                    for tile in range(home, tiles)
                }
                for step in range(GROUP)
            ]
            for pack in range(packs)
        ]
        second = {}
        for step in range(GROUP):
            inside = first % 8 + step
            at_step = column == first + step
            below = sub > inside
            for pack in range(packs):
                pieces = blocks[pack]
                if step % 2 == 0:
                    pivot = columns[pack][step][home][inside : inside + 1, :]
                    cross = columns[pack][step + 1][home][inside : inside + 1, :]
                    other = columns[pack][step + 1][home][inside + 1 : inside + 2, :]
                    product = pivot * other - cross * cross
                    inverse = reciprocal(pivot)
                    second[pack] = product * inverse, pivot * reciprocal(product)
                else:
                    pivot, inverse = second[pack]
                row = jnp.where(at_step[:1], 1.0, pieces[home][inside : inside + 1, :])
                pivots[pack][home] = jnp.where(sub == inside, pivot, pivots[pack][home])
                later = {
                    other: columns[pack][other][home][inside : inside + 1, :]
                    for other in range(step + 1, GROUP)
                }
                for tile in range(home, tiles):
                    ratio = columns[pack][step][tile] * inverse
                    cleared = at_step
                    if tile == home:
                        ratio = jnp.where(below, ratio, 0.0)
                        cleared = at_step & below
                    for other in later:
                        columns[pack][other][tile] = (
                            columns[pack][other][tile] - ratio * later[other]
                        )
                    pieces[tile] = jnp.where(cleared, 0.0, pieces[tile]) - ratio * row
    results = []
    for pack in range(packs):
        rows = []
        for tile in range(tiles):
            index = sub + 8 * tile
            lower = jnp.where(
                column < index, blocks[pack][tile], jnp.where(column == index, 1.0, 0.0)
            )
            rows.append(lower * lax.rsqrt(pivots[pack][tile]))
        results.append(jnp.concatenate(rows, axis=0))
    return results


def six_products(left, right, axis):
    high, mid, low = left
    left = jnp.concatenate([high, high, mid, mid, high, low], axis=axis)
    high, mid, low = right
    right = jnp.concatenate([high, mid, high, mid, low, high], axis=0)
    return lax.dot_general(
        left, right, (((axis,), (0,)), ((), ())), preferred_element_type=F32
    )


def eliminate(panel, pack, lower, work_ref, lead_ref, members):
    per_pack = LANES // PANEL
    start = panel * PANEL
    after = start + PANEL
    first = start // LANES * LANES
    kept = after // LANES * LANES
    owner = lax.broadcasted_iota(jnp.int32, (PANEL, LANES), 1) // PANEL

    def carry(region, rows, block):
        if start % LANES:
            return block
        if start == 0:
            source = lead_ref[region]
        else:
            source = work_ref[region, rows, first - LANES : first]
        lane = lax.broadcasted_iota(jnp.int32, source.shape, 1)
        head = jnp.where(lane < PANEL, source, block[:, :LANES])
        return jnp.concatenate([head, block[:, LANES:]], axis=1)

    spread = jnp.concatenate(
        [jnp.where(owner == place, lower, 0.0) for place in range(per_pack)], axis=0
    )
    here, rest = slice(start, after), slice(after, members)
    stacked = []
    for place in range(per_pack):
        region = pack * per_pack + place
        stacked.append(carry(region, here, work_ref[region, here, first:]))
    stacked = jnp.concatenate(stacked, axis=0)
    solved = six_products(split3(spread), split3(stacked), 1)
    for place in range(per_pack):
        region = pack * per_pack + place
        rows = solved[place * PANEL : (place + 1) * PANEL]
        work_ref[region, here, first : first + LANES] = rows[:, :LANES]
        work_ref[region, here, members:] = rows[:, members - first :]
        if after < members:
            parts = split3(rows)
            change = six_products(
                [part[:, kept - first : members - first] for part in parts], parts, 0
            )
            old = work_ref[region, rest, first:]
            if start:
                old = carry(region, rest, old)
            work_ref[region, rest, first:] = old - change[after - kept :]


def analysis_kernel(offsets, first_ref, prior_ref, column_ref, weight_ref, *rest):
    count = len(offsets)
    hbm_refs = rest[:count]
    out_ref, scaled_ref, work_ref, lead_ref, mean_ref, sems = rest[count : count + 6]
    vmem_refs = rest[count + 6 :]
    states_ref, obs_refs = vmem_refs[0], vmem_refs[1:]
    regions, members = prior_ref.shape
    sources, members_dev = states_ref.shape[0], states_ref.shape[2]
    points = states_ref.shape[3]
    packs = regions * PANEL // LANES
    ways = scaled_ref.shape[0]
    batches = sems.shape[0]
    batch_regions = regions // batches

    def loads(batch):
        copies = []
        for index, (hbm, vmem) in enumerate(zip(hbm_refs, vmem_refs)):
            size = vmem.shape[1] // batches
            copies.append(
                pltpu.make_async_copy(
                    hbm.at[:, pl.ds(offsets[index] + batch * size, size)],
                    vmem.at[:, pl.ds(batch * size, size)],
                    sems.at[batch, index],
                )
            )
        return copies

    for batch in range(batches):
        for copy in loads(batch):
            copy.start()

    @pl.loop(0, batches)
    def _(batch):
        for copy in loads(batch):
            copy.wait()

        @pl.loop(0, batch_regions // ways)
        def _(step):
            for way in range(ways):
                region_setup(
                    batch * batch_regions + step * ways + way, first_ref[0], prior_ref,
                    column_ref, weight_ref, states_ref, obs_refs, scaled_ref.at[way],
                    work_ref, lead_ref, mean_ref,
                )

    for panel in range(members // PANEL):
        lowers = factor_diagonals(panel, range(packs), work_ref)
        for pack in range(packs):
            eliminate(panel, pack, lowers[pack], work_ref, lead_ref, members)

    @pl.loop(0, regions)
    def _(region):
        moved = work_ref[region, :, members : members + points]
        solved = jnp.concatenate(
            [
                work_ref[region, start : start + LANES, start : start + 1]
                for start in range(0, members, LANES)
            ],
            axis=0,
        )
        shift = mean_ref[region, :1] + jnp.sum(solved * moved, axis=0, keepdims=True)
        result = (shift + jnp.sqrt(members - 1.0) * moved).astype(BF16)
        for source in range(sources):
            out_ref[source, region] = result[
                source * members_dev : (source + 1) * members_dev
            ]


def analyse(first, prior_rows, weight_rows, states, obs_parts, slots):
    regions, members = prior_rows.shape
    sources, _, members_dev, points = states[0].shape
    width = obs_parts[0][0].shape[3]
    vmem = pl.BlockSpec(memory_space=pltpu.VMEM)
    loaded = [states] + obs_parts
    sizes = [regions] + [regions * slots] * len(obs_parts)
    columns = jnp.broadcast_to(prior_rows[:, :, None], (regions, members, LANES))
    return pl.pallas_call(
        functools.partial(analysis_kernel, [offset for _, offset in loaded]),
        out_shape=jax.ShapeDtypeStruct((sources, regions, members_dev, points), BF16),
        in_specs=[pl.BlockSpec(memory_space=pltpu.SMEM), vmem, vmem, vmem]
        + [pl.BlockSpec(memory_space=pl.ANY)] * len(loaded),
        out_specs=vmem,
        scratch_shapes=[
            pltpu.VMEM((2, members, slots * width), BF16),
            pltpu.VMEM((regions, members, members + points), F32),
            pltpu.VMEM((regions, PANEL, LANES), F32),
            pltpu.VMEM((regions, 8, points), F32),
            pltpu.SemaphoreType.DMA((regions // 2, len(loaded))),
        ]
        + [
            pltpu.VMEM(array.shape[:1] + (size,) + array.shape[2:], array.dtype)
            for (array, _), size in zip(loaded, sizes)
        ],
        cost_estimate=pl.CostEstimate(
            flops=16 * regions * members * members * (slots * width + points),
            bytes_accessed=2 * regions * members * (slots * width + 2 * points),
            transcendentals=0,
        ),
        compiler_params=pltpu.CompilerParams(vmem_limit_bytes=48 << 20),
    )(first, prior_rows, columns, weight_rows, *[array for array, _ in loaded])


def body(
    ensemble_state, obs_ens, innovation, obs_prec, block_list, block_count, loc_weight, prior_weight
):
    spaces = lax.axis_size("space")
    mem_count = lax.axis_size("mem")
    members_dev, regions_dev, points = ensemble_state.shape
    blocks_dev, width = obs_ens.shape[1:]
    group_size = regions_dev // mem_count
    slots = block_list.shape[1]
    part = group_size // SPLIT
    first_row = lax.axis_index("mem") * group_size

    inner = 2 ** ((spaces.bit_length() - 1) // 2)
    cycle = grid_cycle(spaces // inner, inner)
    forward = [(cycle[k], cycle[(k + 1) % spaces]) for k in range(spaces)]
    backward = [(to, start) for start, to in forward]
    position = [cycle.index(space) for space in range(spaces)]
    half_way = spaces // 2

    def place_of(space):
        return sum(
            jnp.where(space == index, position[index], 0) for index in range(spaces)
        )

    all_ids = block_list.reshape(regions_dev * slots)
    behind = place_of(lax.axis_index("space")) - place_of(all_ids // blocks_dev)
    places = (behind + spaces) % spaces * blocks_dev + all_ids % blocks_dev
    active = jnp.arange(slots, dtype=jnp.int32)[None, :] < block_count[:, None]
    local = jnp.where(active, loc_weight, 0.0).reshape(regions_dev * slots)
    waiting = []
    start = 0
    for share in CHUNKS:
        stop = start + members_dev // share
        waiting.append(jnp.transpose(obs_ens[start:stop], (1, 0, 2)))
        start = stop
    rows = jnp.concatenate([obs_prec, innovation], axis=1)
    rows_ahead, rows_back = [rows], [rows]
    by_region = jnp.transpose(ensemble_state, (1, 0, 2)).reshape(
        mem_count, group_size, members_dev, points
    )

    def ring_step(step, ahead, back):
        if step < half_way - 1:
            return lax.ppermute(ahead, "space", forward), lax.ppermute(
                back, "space", backward
            )
        middle = blocks_dev // 2
        return (
            lax.ppermute(ahead[:middle], "space", forward),
            lax.ppermute(back[middle:], "space", backward),
        )

    def exchange(picked):
        return lax.all_to_all(picked, "mem", split_axis=0, concat_axis=0, tiled=True)

    running = []
    obs_parts = [[] for _ in range(SPLIT)]
    stage = 0
    due = {}
    while waiting or running:
        if waiting and not running:
            own = waiting.pop(0)
            running.append({"step": 0, "ahead": [own], "back": [own]})
        moved = [
            ring_step(ring["step"], ring["ahead"][-1], ring["back"][-1])
            for ring in running
        ]
        tied = {"moved": moved, "waiting": waiting, "due": due.pop(stage, None)}
        if stage < half_way:
            tied["ahead"] = lax.ppermute(rows_ahead[-1], "space", forward)
        if stage < half_way - 1:
            tied["back"] = lax.ppermute(rows_back[-1], "space", backward)
        if stage == 0:
            tied["by_region"] = by_region
        if stage == half_way - 1:
            tied["states"] = states
        tied = lax.optimization_barrier(tied)
        waiting = tied["waiting"]
        for ring, (ahead, back) in zip(running, tied["moved"]):
            ring["ahead"].append(ahead)
            ring["back"].append(back)
            ring["step"] += 1
        if stage < half_way:
            rows_ahead.append(tied["ahead"])
        if stage < half_way - 1:
            rows_back.append(tied["back"])
        if stage == 0:
            states = exchange(tied["by_region"])
        if stage == half_way - 1:
            latest = states = tied["states"]
            weight_rows = weights(places, local, rows_ahead + rows_back[:0:-1])
        if tied["due"] is not None:
            picked, _ = lax.optimization_barrier((tied["due"], latest))
            latest = exchange(picked)
            for index in range(SPLIT):
                obs_parts[index].append((latest, index * part * slots))
        if running[0]["step"] == half_way:
            ring = running.pop(0)
            shards = ring["ahead"] + ring["back"][:0:-1]
            if waiting or running:
                picked = pick(
                    places, weight_rows, shards, mem_count, group_size, 0, group_size
                )
                due[stage + 1] = picked
            else:
                for index in range(SPLIT):
                    picked = pick(
                        places, weight_rows, shards, mem_count, group_size,
                        index * part, part,
                    )
                    picked, _ = lax.optimization_barrier((picked, latest))
                    latest = exchange(picked)
                    obs_parts[index].append((latest, 0))
        stage += 1

    results = []
    for index in range(SPLIT):
        start = first_row + index * part
        if results:
            start, results[-1] = lax.optimization_barrier((start, results[-1]))
            results[-1] = exchange(results[-1])
        result = analyse(
            (start * slots).reshape(1),
            lax.dynamic_slice_in_dim(prior_weight, start, part, 0),
            weight_rows,
            (states, index * part),
            obs_parts[index],
            slots,
        )
        results.append(result)
    results[-1] = exchange(results[-1])
    back = jnp.concatenate(results, axis=1)
    return jnp.transpose(back.reshape(regions_dev, members_dev, points), (1, 0, 2))


def solution(mesh):
    return jax.shard_map(
        body,
        mesh=mesh,
        in_specs=(
            P("mem", "space", None),
            P("mem", "space", None),
            P("space", None),
            P("space", None),
            P("space", None),
            P("space"),
            P("space", None),
            P("space", None),
        ),
        out_specs=P("mem", "space", None),
        check_vma=False,
    )
```
